512 devices in a mesh: req: 32 (over y, x), hist: 16 (over z, core).
Axes of the slice: x: 4, y: 8, z: 8, core: 2. Of those that a mesh axis runs over, the one named last changes fastest.
Arguments:
- codes: int32 [2, 1024], P(None, 'req'), may hold values from 0 to 255
- parents: int32 [1024], P('req'), may hold values from 0 to 63
- lengths: int32 [16], replicated, may hold values from 1 to 32768, as said below
- holders: int32 [16, 32], replicated, may hold values from 0 to 31, each once within a row
- history_keys: bfloat16 [32, 16384, 1024], P('req', 'hist')
- history_values: bfloat16 [32, 16384, 1024], P('req', 'hist')
- query_table: bfloat16 [2, 256, 4096], P(None, None, 'hist')
- kv_table: bfloat16 [2, 256, 2048], P(None, None, 'hist')
- embed_table: bfloat16 [2, 256, 4096], P(None, None, 'hist'), may hold values from -3 to 3
- out_weight: bfloat16 [4096, 4096], P(None, 'hist'), may hold values from -0.375 to 0.375
Outputs:
- layer_out: bfloat16 [2, 1024, 4096], P(None, 'req', 'hist')
The draws below stay inside these ranges and needn't reach their ends.
Inputs may be any that keep to these rules, and one draw needn't show every extreme that they name: `holders`: each row lists each of the 32 history devices of the request once. `lengths`: at least one request's history fills all 32768 positions.
All inputs are finite; a program needn't handle non-finite values.
Results may differ from the reference program's by a relative error of at most 0.0065.
Values may be sent and summed in bfloat16 or wider, within the bound.
No kernel may reach another device: no remote copies, remote signals or barrier semaphores. Data moves between devices by JAX's collectives and lax.ppermute only.
A program may use at most 128 MiB of HBM per device.

```python
import math
import jax
import jax.numpy as jnp
from jax import lax

D = 4096
QUERY_HEADS = 32
KEY_HEADS = 8
HEAD_SIZE = 128
CODE_COUNT = 256
LEVEL_COUNT = 2
HISTORY_PER_UNIT = 1024
BEAM_WIDTH = 64
HOLDER_COUNT = 32
REQUEST_COUNT = 16
ROWS = 1024
QW = 4096
KVW = 1024
N_REQ = 32
N_HIST = 16


query_share = 0.35


def shared_direction(key):
    return jax.random.normal(key, (LEVEL_COUNT, KEY_HEADS, HEAD_SIZE), jnp.float32)


def draw_query_table(key, part):
    directions = shared_direction(key)
    key = jax.random.fold_in(key, 11)
    random_jitter = jax.random.normal(key, (LEVEL_COUNT, CODE_COUNT, KEY_HEADS, QUERY_HEADS // KEY_HEADS, HEAD_SIZE), jnp.float32)
    table = random_jitter + query_share * directions[:, None, :, None, :]
    return table.reshape(LEVEL_COUNT, CODE_COUNT, QW).astype(jnp.bfloat16)


def draw_kv_table(key, part):
    directions = shared_direction(key)
    key = jax.random.fold_in(key, 12)
    initial_random_key, later_random_key, third_key = jax.random.split(key, 3)
    score_target = 3.0 * math.sqrt(1.0 + query_share ** 2) * math.sqrt(2.0 * math.log(HOLDER_COUNT * HISTORY_PER_UNIT))
    lift_unit = 1.0 / (query_share * math.sqrt(HEAD_SIZE))
    lift_magnitude = score_target * lift_unit * jax.random.uniform(initial_random_key, (LEVEL_COUNT, CODE_COUNT, KEY_HEADS, 1), jnp.float32, 0.8, 1.2)
    local_keys = jax.random.normal(later_random_key, (LEVEL_COUNT, CODE_COUNT, KEY_HEADS, HEAD_SIZE), jnp.float32) + lift_magnitude * directions[:, None, :, :]
    values_part = jax.random.normal(third_key, (LEVEL_COUNT, CODE_COUNT, KVW), jnp.float32)
    table = jnp.concatenate([local_keys.reshape(LEVEL_COUNT, CODE_COUNT, KVW), values_part], axis=2)
    return table.astype(jnp.bfloat16)


def draw_history_keys(key, part):
    key = jax.random.fold_in(key, 15)
    jitter_random_key = jax.random.fold_in(key, 0)
    random_jitter = jax.random.normal(jitter_random_key, (N_REQ, N_HIST * HISTORY_PER_UNIT, KEY_HEADS, HEAD_SIZE), jnp.float32)
    keys_full = jnp.clip(3.0 * random_jitter, -18.0, 18.0)
    return keys_full.reshape(N_REQ, N_HIST * HISTORY_PER_UNIT, KVW).astype(jnp.bfloat16)


def draw_history_values(key, part):
    key = jax.random.fold_in(key, 13)
    jitter_random_key, offset_key = jax.random.split(key)
    random_jitter = jax.random.normal(jitter_random_key, (N_REQ, N_HIST, HISTORY_PER_UNIT, KVW), jnp.float32)
    offsets = 1.5 * jax.random.normal(offset_key, (N_REQ, N_HIST, 1, KVW), jnp.float32)
    return (random_jitter + offsets).reshape(N_REQ, N_HIST * HISTORY_PER_UNIT, KVW).astype(jnp.bfloat16)


def draw_lengths(key, part):
    key = jax.random.fold_in(key, 14)
    level_random_key, chosen_key = jax.random.split(key)
    most = HOLDER_COUNT * HISTORY_PER_UNIT
    level = jax.random.randint(level_random_key, (REQUEST_COUNT,), 0, 1024)
    spread = 1 + (most - 1) * level // 1023 * level // 1023
    chosen = jax.random.randint(chosen_key, (), 0, REQUEST_COUNT)
    return jnp.where(jnp.arange(REQUEST_COUNT) == chosen, most, spread).astype(jnp.int32)


def plant(entries, own_key, least, top_value):
    dims = entries.shape
    index_at = [jax.random.randint(jax.random.fold_in(own_key, axis), (), 0, dims[axis]) for axis in range(len(dims))]
    entries = entries.at[tuple(index_at)].set(least)
    longest = dims.index(max(dims))
    index_at[longest] = (index_at[longest] + 1) % dims[longest]
    return entries.at[tuple(index_at)].set(top_value)


def level_of(rng, shape, cuts, least, high):
    def one(position, blocks):
        heights = jax.random.uniform(jax.random.fold_in(jax.random.fold_in(rng, 6), position), (blocks,), jnp.float32, least / len(cuts), high / len(cuts))
        return jnp.repeat(jnp.exp(heights), shape[position] // blocks).reshape((-1,) + (1,) * (len(shape) - position - 1))

    level = one(*cuts[0])
    for cut in cuts[1:]:
        level = level * one(*cut)
    return level


def noise(own_key, extent, scale, limit, pieces=(), kind=jnp.bfloat16):
    values = scale * jax.random.normal(own_key, extent, jnp.float32)
    if pieces:
        values = values * level_of(own_key, extent, pieces, -0.22, 0.18)
    return jnp.clip(values, -limit, limit).astype(kind)


def setup_inputs(seed: int = 0) -> dict:
    arg_keys = jax.random.split(jax.random.key(seed), 11)
    codes = plant(jax.random.randint(arg_keys[0], (LEVEL_COUNT, ROWS), 0, CODE_COUNT), jax.random.fold_in(arg_keys[0], 1), 0, CODE_COUNT - 1).astype(jnp.int32)
    parents = plant(jax.random.randint(arg_keys[1], (ROWS,), 0, BEAM_WIDTH), jax.random.fold_in(arg_keys[1], 1), 0, BEAM_WIDTH - 1).astype(jnp.int32)
    lengths = draw_lengths(jax.random.fold_in(arg_keys[10], 71), 0)
    holders = jax.vmap(lambda own: jax.random.permutation(own, HOLDER_COUNT))(jax.random.split(arg_keys[3], REQUEST_COUNT)).reshape((REQUEST_COUNT, HOLDER_COUNT)).astype(jnp.int32)
    history_keys = draw_history_keys(jax.random.fold_in(arg_keys[10], 71), 0)
    history_values = draw_history_values(jax.random.fold_in(arg_keys[10], 71), 0)
    query_table = draw_query_table(jax.random.fold_in(arg_keys[10], 71), 0)
    kv_table = draw_kv_table(jax.random.fold_in(arg_keys[10], 71), 0)
    embed_table = noise(arg_keys[8], (LEVEL_COUNT, CODE_COUNT, D), 0.5, 3.0, ((2, 16),))
    out_weight = noise(arg_keys[9], (QW, D), (QW // 16) ** -0.5, 0.375, ((1, 16),))
    return {"codes": codes, "parents": parents, "lengths": lengths, "holders": holders, "history_keys": history_keys, "history_values": history_values, "query_table": query_table, "kv_table": kv_table, "embed_table": embed_table, "out_weight": out_weight}


def look_rows(table, picks):
    return jnp.take(table, picks, axis=0)


def attend_request(packed):
    query_matrix, generated_keys, generated_values, block_key_rows, block_value_rows, live_slots = packed
    query_group_width = QUERY_HEADS // KEY_HEADS
    scale_factor = HEAD_SIZE ** -0.5
    query_vectors = query_matrix.astype(jnp.float32).reshape(BEAM_WIDTH, KEY_HEADS, query_group_width, HEAD_SIZE)
    keys_float = block_key_rows.astype(jnp.float32)
    values_float = block_value_rows.astype(jnp.float32)
    scores = jnp.einsum("bgrd,utgd->ugbrt", query_vectors, keys_float) * scale_factor
    live_mask = live_slots[:, None, None, None, :]
    block_top = jnp.max(jnp.where(live_mask, scores, -1e30), axis=-1)
    weights = jnp.where(live_mask, jnp.exp(scores - block_top[..., None]), 0.0).astype(jnp.bfloat16)
    weights_float = weights.astype(jnp.float32)
    block_total = jnp.sum(weights_float, axis=-1)
    block_out = jnp.einsum("ugbrt,utgd->ugbrd", weights_float, values_float)
    generated_key_wide = generated_keys.astype(jnp.float32).reshape(BEAM_WIDTH, -1, KEY_HEADS, HEAD_SIZE)
    generated_value_wide = generated_values.astype(jnp.float32).reshape(BEAM_WIDTH, -1, KEY_HEADS, HEAD_SIZE)
    gen_scores = jnp.einsum("bgrd,bngd->gbrn", query_vectors, generated_key_wide) * scale_factor
    overall = jnp.maximum(jnp.max(block_top, axis=0), jnp.max(gen_scores, axis=-1))
    block_factor = jnp.exp(block_top - overall[None])
    gen_weights = jnp.exp(gen_scores - overall[..., None])
    denominator = jnp.sum(block_total * block_factor, axis=0) + jnp.sum(gen_weights, axis=-1)
    numerator = jnp.sum(block_out * block_factor[..., None], axis=0)
    numerator = numerator + jnp.einsum("gbrn,bngd->gbrd", gen_weights, generated_value_wide)
    result = numerator / denominator[..., None]
    return jnp.transpose(result, (1, 0, 2, 3)).reshape(BEAM_WIDTH, QW).astype(jnp.bfloat16)


def reference(codes, parents, lengths, holders, history_keys, history_values, query_table, kv_table, embed_table, out_weight):
    block_ids = jnp.arange(HOLDER_COUNT, dtype=jnp.int32)
    positions = jnp.sum(jnp.where(holders[:, :, None] == block_ids[None, None, :], block_ids[None, :, None], 0), axis=1)
    slot_ids = jnp.arange(HISTORY_PER_UNIT, dtype=jnp.int32)
    live = positions[:, :, None] * HISTORY_PER_UNIT + slot_ids[None, None, :] < lengths[:, None, None]
    gathered_keys = history_keys.reshape(REQUEST_COUNT, HOLDER_COUNT, HISTORY_PER_UNIT, KEY_HEADS, HEAD_SIZE)
    gathered_values = history_values.reshape(REQUEST_COUNT, HOLDER_COUNT, HISTORY_PER_UNIT, KEY_HEADS, HEAD_SIZE)
    parent_rows = (jnp.arange(ROWS, dtype=jnp.int32) // BEAM_WIDTH) * BEAM_WIDTH + parents
    outputs = []
    earlier_rows = None
    for level_index in range(LEVEL_COUNT):
        query_matrix = look_rows(query_table[level_index], codes[level_index])
        kv_rows = look_rows(kv_table[level_index], codes[level_index])
        own_keys = kv_rows[:, None, :KVW]
        own_values = kv_rows[:, None, KVW:]
        if level_index == 0:
            generated_keys, generated_values = own_keys, own_values
        else:
            parent_kv = look_rows(earlier_rows, parent_rows)
            generated_keys = jnp.concatenate([parent_kv[:, None, :KVW], own_keys], axis=1)
            generated_values = jnp.concatenate([parent_kv[:, None, KVW:], own_values], axis=1)
        earlier_rows = kv_rows
        count = generated_keys.shape[1]
        attention = lax.map(attend_request, (query_matrix.reshape(REQUEST_COUNT, BEAM_WIDTH, QW), generated_keys.reshape(REQUEST_COUNT, BEAM_WIDTH, count, KVW), generated_values.reshape(REQUEST_COUNT, BEAM_WIDTH, count, KVW), gathered_keys, gathered_values, live))
        attention = attention.reshape(ROWS, QW)
        mixed = look_rows(embed_table[level_index], codes[level_index]).astype(jnp.float32) + jnp.dot(attention, out_weight, preferred_element_type=jnp.float32)
        outputs.append(mixed.astype(jnp.bfloat16))
    return jnp.stack(outputs)
```

```python
import functools
import math

import jax
import jax.numpy as jnp
from jax import lax
from jax.experimental import pallas as pl
from jax.experimental.pallas import tpu as pltpu
from jax.sharding import Mesh, PartitionSpec as P

KEY_HEADS = 8
HEAD = 128
STAT = 16
CHUNK = HEAD + STAT
DEAD = -1e30
EXP2_SCALE = HEAD ** (-0.5) * math.log2(math.e)
VMEM_LIMIT = 48 * 1024 * 1024


def params():
    return pltpu.CompilerParams(vmem_limit_bytes=VMEM_LIMIT)


def one_hot_rows(index_row, count):
    rows = index_row.shape[1]
    tall = jnp.transpose(jnp.broadcast_to(index_row, (128, rows)))
    parts = []
    for start in range(0, count, 128):
        lane = lax.broadcasted_iota(jnp.int32, (rows, 128), 1) + start
        parts.append((tall == lane).astype(jnp.float32).astype(jnp.bfloat16))
    return jnp.concatenate(parts, axis=1)


def look_kernel(index_ref, query_ref, kv_ref, query_out, kv_out):
    hot = one_hot_rows(index_ref[...], query_ref.shape[0])
    query_out[...] = jnp.dot(hot, query_ref[...], preferred_element_type=jnp.float32).astype(jnp.bfloat16)
    kv_out[...] = jnp.dot(hot, kv_ref[...], preferred_element_type=jnp.float32).astype(jnp.bfloat16)


def residual_kernel(index_ref, embed_ref, out_ref):
    hot = one_hot_rows(index_ref[...], embed_ref.shape[0])
    out_ref[...] = jnp.dot(hot, embed_ref[...], preferred_element_type=jnp.float32)[: out_ref.shape[0]]


def split3(value):
    high = value.astype(jnp.bfloat16).astype(jnp.float32)
    rest = value - high
    middle = rest.astype(jnp.bfloat16).astype(jnp.float32)
    return high, middle, rest - middle


def stat_rows(top, total):
    row = lax.broadcasted_iota(jnp.int32, (STAT, top.shape[1]), 0)
    out = jnp.zeros((STAT, top.shape[1]), jnp.float32)
    for at, piece in enumerate(split3(top) + split3(total)):
        out = jnp.where(row == at, piece, out)
    return out.astype(jnp.bfloat16)


def read_stats(rows):
    wide = rows.astype(jnp.float32)
    return wide[0:1] + wide[1:2] + wide[2:3], wide[3:4] + wide[4:5] + wide[5:6]


def attend_kernel(
    meta_ref, lengths_ref, holders_ref, query_ref, key_ref, value_ref, gen_key_ref, gen_value_ref, parent_ref,
    keep_ref, send_ref, live_ref, sums_ref, top_ref,
):
    group = pl.program_id(0)
    slots = key_ref.shape[0]
    request, place, core, gen_head = meta_ref[0], meta_ref[1], meta_ref[2], meta_ref[3]
    half = query_ref.shape[1] // 2

    @pl.when(group == 0)
    def _():
        position = jnp.int32(0)
        for block in range(holders_ref.shape[1]):
            position = jnp.where(holders_ref[request, block] == place, block, position)
        live_ref[0] = jnp.clip(lengths_ref[request] - position * slots, 0, slots)

    live = live_ref[0]

    def queries(local):
        pair = query_ref[2 * group + jnp.bitwise_xor(core, local)]
        return jnp.concatenate(
            [pair[x * half : (x + 1) * half, h * HEAD : (h + 1) * HEAD] for x in range(2) for h in range(2)], axis=0
        )

    def extended(values):
        return jnp.concatenate([jnp.transpose(values), jnp.ones((STAT, values.shape[0]), jnp.bfloat16)], axis=0)

    def scores_of(keys, rows):
        return lax.dot_general(keys, rows, (((1,), (1,)), ((), ())), preferred_element_type=jnp.float32)

    def attend(masked):
        keys = key_ref[...]
        values = extended(value_ref[...])
        width = 4 * half
        for local in range(2):
            lanes = slice(local * width, (local + 1) * width)
            scores = scores_of(keys, queries(local))
            if masked:
                slot = lax.broadcasted_iota(jnp.int32, (slots, 1), 0)
                scores = jnp.where(slot < live, scores, DEAD)
            top = jnp.max(scores, axis=0, keepdims=True)
            weights = jnp.exp2((scores - top) * EXP2_SCALE).astype(jnp.bfloat16)
            sums_ref[:, lanes] = jnp.dot(values, weights, preferred_element_type=jnp.float32)
            top_ref[:, lanes] = jnp.broadcast_to(top, (8, width))

    @pl.when(live == slots)
    def _():
        attend(False)

    @pl.when((live > 0) & (live < slots))
    def _():
        attend(True)

    @pl.when(live == 0)
    def _():
        sums_ref[...] = jnp.zeros(sums_ref.shape, jnp.float32)
        top_ref[...] = jnp.full(top_ref.shape, DEAD, jnp.float32)

    @pl.when(group == gen_head)
    def _():
        keys = gen_key_ref[...]
        values = extended(gen_value_ref[...])
        width = 4 * half
        row = lax.broadcasted_iota(jnp.int32, (2 * half, width), 0)
        lane = lax.broadcasted_iota(jnp.int32, (2 * half, width), 1)
        own = (lane // (2 * half)) * half + lane % half
        allowed = (row == own) | (row == parent_ref[...])
        for local in range(2):
            lanes = slice(local * width, (local + 1) * width)
            scores = jnp.where(allowed, scores_of(keys, queries(local)), DEAD)
            before = top_ref[0:1, lanes]
            top = jnp.maximum(before, jnp.max(scores, axis=0, keepdims=True))
            weights = jnp.where(allowed, jnp.exp2((scores - top) * EXP2_SCALE), 0.0)
            high = weights.astype(jnp.bfloat16)
            low = (weights - high.astype(jnp.float32)).astype(jnp.bfloat16)
            added = jnp.dot(values, high, preferred_element_type=jnp.float32)
            added = added + jnp.dot(values, low, preferred_element_type=jnp.float32)
            sums_ref[:, lanes] = sums_ref[:, lanes] * jnp.exp2((before - top) * EXP2_SCALE) + added
            top_ref[:, lanes] = jnp.broadcast_to(top, (8, width))

    for local, out_ref in enumerate((keep_ref, send_ref)):
        for x in range(2):
            lanes = slice(local * 4 * half + x * 2 * half, local * 4 * half + (x + 1) * 2 * half)
            out_ref[x, 0, 0:HEAD] = sums_ref[0:HEAD, lanes].astype(jnp.bfloat16)
            out_ref[x, 0, HEAD:CHUNK] = stat_rows(top_ref[0:1, lanes], sums_ref[HEAD : HEAD + 1, lanes])


def merge_kernel(mine_ref, other_ref, out_ref):
    for chunk in range(mine_ref.shape[0]):
        tops, totals = zip(*(read_stats(ref[chunk, HEAD:CHUNK]) for ref in (mine_ref, other_ref)))
        top = jnp.maximum(*tops)
        factors = [jnp.exp2((each - top) * EXP2_SCALE) for each in tops]
        total = totals[0] * factors[0] + totals[1] * factors[1]
        sums = (
            mine_ref[chunk, 0:HEAD].astype(jnp.float32) * factors[0]
            + other_ref[chunk, 0:HEAD].astype(jnp.float32) * factors[1]
        )
        out_ref[chunk, 0:HEAD] = sums.astype(jnp.bfloat16)
        out_ref[chunk, HEAD:CHUNK] = stat_rows(top, total)


def combine_kernel(parts_ref, out_ref):
    count = parts_ref.shape[0]
    stats = [read_stats(parts_ref[part, HEAD:CHUNK]) for part in range(count)]
    top = functools.reduce(jnp.maximum, [each for each, _ in stats])
    total = jnp.zeros_like(top)
    sums = jnp.zeros((HEAD, parts_ref.shape[2]), jnp.float32)
    for part in range(count):
        factor = jnp.exp2((stats[part][0] - top) * EXP2_SCALE)
        total = total + stats[part][1] * factor
        sums = sums + parts_ref[part, 0:HEAD].astype(jnp.float32) * factor
    tall = jnp.transpose(sums / total)
    rows = out_ref.shape[0]
    out_ref[...] = jnp.concatenate([tall[0:rows], tall[rows : 2 * rows]], axis=1).astype(jnp.bfloat16)


def project_kernel(rows_ref, weight_ref, residual_ref, out_ref):
    total = residual_ref[...]
    width = rows_ref.shape[2]
    for part in range(rows_ref.shape[0]):
        total = total + jnp.dot(
            rows_ref[part], weight_ref[part * width : (part + 1) * width], preferred_element_type=jnp.float32
        )
    out_ref[...] = total.astype(jnp.bfloat16)


def shards(
    codes, parents, lengths, holders, history_keys, history_values, query_table, kv_table, embed_table, out_weight
):
    beams = parents.shape[0]
    levels, code_count, width = query_table.shape
    half = levels * beams
    rows = 2 * half
    slots = history_keys.shape[1]
    z_count = lax.axis_size("z")
    pair, z, core = lax.axis_index("pair"), lax.axis_index("z"), lax.axis_index("core")
    hist = 2 * z + core
    first = pair == 0
    bf16, f32 = jnp.bfloat16, jnp.float32

    own_index = (codes + code_count * jnp.arange(levels, dtype=jnp.int32)[:, None]).reshape(half)
    mine = jnp.concatenate([own_index, parents])
    other = lax.ppermute(mine, "pair", [(0, 1), (1, 0)])
    residual = pl.pallas_call(
        residual_kernel,
        out_shape=jax.ShapeDtypeStruct((half, width), f32),
        compiler_params=params(),
        name="residual",
    )(jnp.concatenate([own_index, own_index]).reshape(1, rows), embed_table.reshape(levels * code_count, width))

    lower = jnp.where(first, mine, other)
    upper = jnp.where(first, other, mine)
    index = jnp.concatenate([lower[:half], upper[:half]]).reshape(1, rows)
    query_rows, kv_rows = pl.pallas_call(
        look_kernel,
        out_shape=(
            jax.ShapeDtypeStruct((rows, width), bf16),
            jax.ShapeDtypeStruct((rows, HEAD), bf16),
        ),
        compiler_params=params(),
        name="look",
    )(index, query_table.reshape(levels * code_count, width), kv_table.reshape(levels * code_count, HEAD))
    gen_values = lax.ppermute(kv_rows, "z", [(i + z_count // 2, i) for i in range(z_count // 2)])
    queries = lax.all_gather(query_rows, ("z", "core"), axis=0)

    both = jnp.stack([lower[half:], upper[half:]])
    parent_rows = (both // beams) * half + both % beams
    parent_lanes = jnp.concatenate([jnp.full((2, beams), -1, jnp.int32), parent_rows], axis=1)
    parent_lanes = jnp.broadcast_to(parent_lanes[:, None, :], (2, 2, half)).reshape(1, 2 * rows)

    gen_head = jnp.where(first & (z < z_count // 2), hist, -1)
    meta = jnp.stack([lax.axis_index("grp"), pair * 2 * z_count + hist, core, gen_head]).astype(jnp.int32)
    partial_shape = jax.ShapeDtypeStruct((2, z_count, CHUNK, 2 * half), bf16)
    whole = lambda *shape: pl.BlockSpec(shape, lambda g, *_: (0,) * len(shape))
    keep, send = pl.pallas_call(
        attend_kernel,
        out_shape=(partial_shape, partial_shape),
        grid_spec=pltpu.PrefetchScalarGridSpec(
            num_scalar_prefetch=3,
            grid=(KEY_HEADS,),
            in_specs=[
                whole(2 * z_count, rows, width),
                pl.BlockSpec((slots, HEAD), lambda g, *_: (0, g)),
                pl.BlockSpec((slots, HEAD), lambda g, *_: (0, g)),
                whole(rows, HEAD),
                whole(rows, HEAD),
                whole(1, 2 * rows),
            ],
            out_specs=[pl.BlockSpec((2, 1, CHUNK, 2 * half), lambda g, *_: (0, g, 0, 0))] * 2,
            scratch_shapes=[
                pltpu.SMEM((1,), jnp.int32),
                pltpu.VMEM((CHUNK, 4 * rows), f32),
                pltpu.VMEM((8, 4 * rows), f32),
            ],
        ),
        compiler_params=params(),
        cost_estimate=pl.CostEstimate(
            flops=4 * 4 * rows * KEY_HEADS * slots * HEAD,
            bytes_accessed=4 * slots * KEY_HEADS * HEAD,
            transcendentals=4 * rows * KEY_HEADS * slots,
        ),
        name="attend",
    )(meta, lengths, holders, queries, history_keys[0], history_values[0], kv_rows, gen_values, parent_lanes)

    shape = (2 * z_count, CHUNK, 2 * half)
    arrived = lax.ppermute(send, "core", [(0, 1), (1, 0)])
    merged = pl.pallas_call(
        merge_kernel, out_shape=jax.ShapeDtypeStruct(shape, bf16), compiler_params=params(), name="merge"
    )(keep.reshape(shape), arrived.reshape(shape))
    parts = lax.all_to_all(merged, ("pair", "z"), split_axis=0, concat_axis=0, tiled=True)
    attention = pl.pallas_call(
        combine_kernel,
        out_shape=jax.ShapeDtypeStruct((half, width), bf16),
        compiler_params=params(),
        name="combine",
    )(parts)
    gathered = lax.all_gather(attention, ("z", "core"), axis=0)
    out = pl.pallas_call(
        project_kernel,
        out_shape=jax.ShapeDtypeStruct((half, width), bf16),
        compiler_params=params(),
        name="project",
    )(gathered, out_weight, residual)
    return out.reshape(levels, beams, width)


def solution(mesh):
    split = Mesh(mesh.devices.reshape(16, 2, 8, 2), ("grp", "pair", "z", "core"))
    req, hist = ("grp", "pair"), ("z", "core")
    in_specs = (
        P(None, req),
        P(req),
        P(),
        P(),
        P(req, hist, None),
        P(req, hist, None),
        P(None, None, hist),
        P(None, None, hist),
        P(None, None, hist),
        P(None, hist),
    )
    return jax.shard_map(shards, mesh=split, in_specs=in_specs, out_specs=P(None, req, hist), check_vma=False)
```

```python
import functools
import math

import jax
import jax.numpy as jnp
from jax import lax
from jax.experimental import pallas as pl
from jax.experimental.pallas import tpu as pltpu
from jax.sharding import Mesh, PartitionSpec as P

KEY_HEADS = 8
HEAD = 128
STAT = 16
CHUNK = HEAD + STAT
DEAD = -1e30
EXP2_SCALE = HEAD ** (-0.5) * math.log2(math.e)
VMEM_LIMIT = 32 * 1024 * 1024


def params():
    return pltpu.CompilerParams(vmem_limit_bytes=VMEM_LIMIT)


def one_hot_rows(index_row, count):
    rows = index_row.shape[1]
    tall = jnp.transpose(jnp.broadcast_to(index_row, (128, rows)))
    parts = []
    for start in range(0, count, 128):
        lane = lax.broadcasted_iota(jnp.int32, (rows, 128), 1) + start
        parts.append((tall == lane).astype(jnp.float32).astype(jnp.bfloat16))
    return jnp.concatenate(parts, axis=1)


def look(hot, table_ref):
    return jnp.dot(hot, table_ref[...], preferred_element_type=jnp.float32)


def own_kernel(index_ref, query_ref, kv_ref, embed_ref, query_out, kv_out, residual_out):
    rows = query_out.shape[0]
    hot = one_hot_rows(index_ref[...], query_ref.shape[0])
    query_out[...] = look(hot, query_ref)[:rows].astype(jnp.bfloat16)
    kv_out[...] = look(hot, kv_ref)[:rows].astype(jnp.bfloat16)
    residual_out[...] = look(hot, embed_ref)[:rows]


def both_kernel(pair_ref, index_ref, query_ref, kv_ref, own_query_ref, own_kv_ref, query_out, kv_out):
    rows = own_query_ref.shape[0]
    hot = one_hot_rows(index_ref[...], query_ref.shape[0])
    mine = pl.ds(pl.multiple_of(pair_ref[0] * rows, rows), rows)
    theirs = pl.ds(pl.multiple_of((1 - pair_ref[0]) * rows, rows), rows)
    query_out[mine] = own_query_ref[...]
    query_out[theirs] = look(hot, query_ref)[:rows].astype(jnp.bfloat16)
    kv_out[mine] = own_kv_ref[...]
    kv_out[theirs] = look(hot, kv_ref)[:rows].astype(jnp.bfloat16)


def stage_kernel(key_ref, value_ref, key_out, value_out):
    slots = key_ref.shape[0]
    for head in range(key_out.shape[0]):
        lanes = slice(head * HEAD, (head + 1) * HEAD)
        key_out[head] = key_ref[:, lanes]
        value_out[head, 0:HEAD] = jnp.transpose(value_ref[:, lanes])
        value_out[head, HEAD:CHUNK] = jnp.ones((STAT, slots), jnp.bfloat16)


def split3(value):
    high = value.astype(jnp.bfloat16).astype(jnp.float32)
    rest = value - high
    middle = rest.astype(jnp.bfloat16).astype(jnp.float32)
    return high, middle, rest - middle


def stat_rows(top, total):
    row = lax.broadcasted_iota(jnp.int32, (STAT, top.shape[1]), 0)
    out = jnp.zeros((STAT, top.shape[1]), jnp.float32)
    for at, piece in enumerate(split3(top) + split3(total)):
        out = jnp.where(row == at, piece, out)
    return out.astype(jnp.bfloat16)


def read_stats(rows):
    wide = rows.astype(jnp.float32)
    return wide[0:1] + wide[1:2] + wide[2:3], wide[3:4] + wide[4:5] + wide[5:6]


def scores_of(keys, rows):
    return lax.dot_general(keys, rows, (((1,), (1,)), ((), ())), preferred_element_type=jnp.float32)


def attend_kernel(
    meta_ref, lengths_ref, holders_ref, query_ref, key_ref, value_ref, gen_key_ref, gen_value_ref, parent_ref,
    out_ref, score_ref,
):
    heads, slots = key_ref.shape[0], key_ref.shape[1]
    half = query_ref.shape[1] // 2
    width = 4 * half
    request, place, gen_head = meta_ref[0], meta_ref[1], meta_ref[2]

    position = jnp.int32(0)
    for block in range(holders_ref.shape[1]):
        position = jnp.where(holders_ref[request, block] == place, block, position)
    live = jnp.clip(lengths_ref[request] - position * slots, 0, slots)

    def queries(head):
        pair = query_ref[head]
        return jnp.concatenate(
            [pair[x * half : (x + 1) * half, h * HEAD : (h + 1) * HEAD] for x in range(2) for h in range(2)], axis=0
        )

    def write(head, sums, total, top):
        for x in range(2):
            lanes = slice(x * 2 * half, (x + 1) * 2 * half)
            out_ref[x, head, 0:HEAD] = sums[:, lanes].astype(jnp.bfloat16)
            out_ref[x, head, HEAD:CHUNK] = stat_rows(top[:, lanes], total[:, lanes])

    def attend(masked):
        def score(head, slot):
            scores = scores_of(key_ref[head], queries(head))
            if masked:
                scores = jnp.where(lax.broadcasted_iota(jnp.int32, (slots, 1), 0) < live, scores, DEAD)
            score_ref[slot] = scores
            return jnp.max(scores, axis=0, keepdims=True)

        def finish(head, slot, top):
            weights = jnp.exp2((score_ref[slot] - top) * EXP2_SCALE).astype(jnp.bfloat16)
            sums = jnp.dot(value_ref[head], weights, preferred_element_type=jnp.float32)
            write(head, sums[0:HEAD], sums[HEAD : HEAD + 1], top)

        def step(i, top):
            later = score(2 * i + 1, 1)
            finish(2 * i, 0, top)
            top = score(jnp.minimum(2 * i + 2, heads - 1), 0)
            finish(2 * i + 1, 1, later)
            return top

        top = lax.fori_loop(0, heads // 2 - 1, step, score(0, 0))
        later = score(heads - 1, 1)
        finish(heads - 2, 0, top)
        finish(heads - 1, 1, later)

    @pl.when(live == slots)
    def _():
        attend(False)

    @pl.when((live > 0) & (live < slots))
    def _():
        attend(True)

    @pl.when(live == 0)
    def _():
        row = lax.broadcasted_iota(jnp.int32, (CHUNK, 2 * half), 0)
        tops = split3(jnp.full((CHUNK, 2 * half), DEAD, jnp.float32))
        dead = jnp.zeros((CHUNK, 2 * half), jnp.float32)
        for at, piece in enumerate(tops):
            dead = jnp.where(row == HEAD + at, piece, dead)
        dead = dead.astype(jnp.bfloat16)
        for x in range(2):
            for head in range(heads):
                out_ref[x, head] = dead

    @pl.when(gen_head >= 0)
    def _():
        values = jnp.concatenate(
            [jnp.transpose(gen_value_ref[...]), jnp.ones((STAT, 2 * half), jnp.bfloat16)], axis=0
        )
        row = lax.broadcasted_iota(jnp.int32, (2 * half, width), 0)
        lane = lax.broadcasted_iota(jnp.int32, (2 * half, width), 1)
        own = (lane // (2 * half)) * half + lane % half
        allowed = (row == own) | (row == parent_ref[...])
        scores = jnp.where(allowed, scores_of(gen_key_ref[...], queries(gen_head)), DEAD)
        before = jnp.concatenate([out_ref[x, gen_head] for x in range(2)], axis=1)
        old_top, old_total = read_stats(before[HEAD:CHUNK])
        top = jnp.maximum(old_top, jnp.max(scores, axis=0, keepdims=True))
        weights = jnp.where(allowed, jnp.exp2((scores - top) * EXP2_SCALE), 0.0)
        high = weights.astype(jnp.bfloat16)
        low = (weights - high.astype(jnp.float32)).astype(jnp.bfloat16)
        added = jnp.dot(values, high, preferred_element_type=jnp.float32)
        added = added + jnp.dot(values, low, preferred_element_type=jnp.float32)
        factor = jnp.exp2((old_top - top) * EXP2_SCALE)
        sums = before[0:HEAD].astype(jnp.float32) * factor + added[0:HEAD]
        write(gen_head, sums, old_total * factor + added[HEAD : HEAD + 1], top)


def merge_kernel(mine_ref, other_ref, out_ref):
    for chunk in range(mine_ref.shape[0]):
        tops, totals = zip(*(read_stats(ref[chunk, HEAD:CHUNK]) for ref in (mine_ref, other_ref)))
        top = jnp.maximum(*tops)
        factors = [jnp.exp2((each - top) * EXP2_SCALE) for each in tops]
        total = totals[0] * factors[0] + totals[1] * factors[1]
        sums = (
            mine_ref[chunk, 0:HEAD].astype(jnp.float32) * factors[0]
            + other_ref[chunk, 0:HEAD].astype(jnp.float32) * factors[1]
        )
        out_ref[chunk, 0:HEAD] = sums.astype(jnp.bfloat16)
        out_ref[chunk, HEAD:CHUNK] = stat_rows(top, total)


def combine_kernel(parts_ref, out_ref):
    count = parts_ref.shape[0]
    stats = [read_stats(parts_ref[part, HEAD:CHUNK]) for part in range(count)]
    top = functools.reduce(jnp.maximum, [each for each, _ in stats])
    total = jnp.zeros_like(top)
    sums = jnp.zeros((HEAD, parts_ref.shape[2]), jnp.float32)
    for part in range(count):
        factor = jnp.exp2((stats[part][0] - top) * EXP2_SCALE)
        total = total + stats[part][1] * factor
        sums = sums + parts_ref[part, 0:HEAD].astype(jnp.float32) * factor
    tall = jnp.transpose(sums / total)
    rows = out_ref.shape[0]
    out_ref[...] = jnp.concatenate([tall[0:rows], tall[rows : 2 * rows]], axis=1).astype(jnp.bfloat16)


def project_kernel(parity, core_ref, rows_ref, weight_ref, before_ref, out_ref):
    total = before_ref[...]
    at = jnp.bitwise_xor(core_ref[0], parity)
    for part in range(rows_ref.shape[0]):
        total = total + jnp.dot(rows_ref[part], weight_ref[part, at], preferred_element_type=jnp.float32)
    out_ref[...] = total.astype(out_ref.dtype)


def call(kernel, out_shape, scalars, name, **rest):
    specs = lambda count, space: [pl.BlockSpec(memory_space=space)] * count

    def run(*args):
        return pl.pallas_call(
            kernel,
            out_shape=out_shape,
            in_specs=specs(scalars, pltpu.SMEM) + specs(len(args) - scalars, pltpu.VMEM),
            out_specs=jax.tree.map(lambda _: pl.BlockSpec(memory_space=pltpu.VMEM), out_shape),
            compiler_params=params(),
            name=name,
            **rest,
        )(*args)

    return run


def shards(
    codes, parents, lengths, holders, history_keys, history_values, query_table, kv_table, embed_table, out_weight
):
    beams = parents.shape[0]
    levels, code_count, width = query_table.shape
    half = levels * beams
    rows = 2 * half
    slots = history_keys.shape[1]
    z_count = lax.axis_size("z")
    pair, z, core = lax.axis_index("pair"), lax.axis_index("z"), lax.axis_index("core")
    hist = 2 * z + core
    first = pair == 0
    bf16, f32 = jnp.bfloat16, jnp.float32
    array = jax.ShapeDtypeStruct
    swap = [(0, 1), (1, 0)]

    other_codes = lax.ppermute(codes, "pair", swap)
    other_parents = lax.ppermute(parents, "pair", swap)

    def index_of(picks):
        flat = (picks + code_count * jnp.arange(levels, dtype=jnp.int32)[:, None]).reshape(half)
        return jnp.concatenate([flat, flat]).reshape(1, rows)

    query_flat = query_table.reshape(levels * code_count, width)
    kv_flat = kv_table.reshape(levels * code_count, HEAD)
    embed_flat = embed_table.reshape(levels * code_count, width)
    own_query, own_kv, residual = call(
        own_kernel, (array((half, width), bf16), array((half, HEAD), bf16), array((half, width), f32)), 0, "own"
    )(index_of(codes), query_flat, kv_flat, embed_flat)
    staged_keys, staged_values = call(
        stage_kernel,
        (array((KEY_HEADS, slots, HEAD), bf16), array((KEY_HEADS, CHUNK, slots), bf16)),
        0,
        "stage",
    )(history_keys[0], history_values[0])

    query_rows, kv_rows = call(both_kernel, (array((rows, width), bf16), array((rows, HEAD), bf16)), 1, "both")(
        pair.reshape(1), index_of(other_codes), query_flat, kv_flat, own_query, own_kv
    )
    gen_values = lax.ppermute(kv_rows, "z", [(i + z_count // 2, i) for i in range(z_count // 2)])
    near_queries = lax.all_gather(query_rows, "z", axis=0)
    far_queries = lax.ppermute(near_queries, "core", swap)

    lower = jnp.where(first, parents, other_parents)
    upper = jnp.where(first, other_parents, parents)
    both = jnp.stack([lower, upper])
    parent_rows = (both // beams) * half + both % beams
    parent_lanes = jnp.concatenate([jnp.full((2, beams), -1, jnp.int32), parent_rows], axis=1)
    parent_lanes = jnp.broadcast_to(parent_lanes[:, None, :], (2, 2, half)).reshape(1, 2 * rows)

    gen_head = jnp.where(first & (z < z_count // 2), hist, -1)
    meta = jnp.stack([lax.axis_index("grp"), pair * 2 * z_count + hist, gen_head]).astype(jnp.int32)
    attend = call(
        attend_kernel,
        array((2, z_count, CHUNK, 2 * half), bf16),
        3,
        "attend",
        scratch_shapes=[pltpu.VMEM((2, slots, 2 * rows), f32)],
        cost_estimate=pl.CostEstimate(
            flops=2 * 4 * rows * KEY_HEADS * slots * HEAD,
            bytes_accessed=4 * slots * KEY_HEADS * HEAD,
            transcendentals=2 * rows * KEY_HEADS * slots,
        ),
    )
    rest = (staged_keys, staged_values, kv_rows, gen_values, parent_lanes)
    send = attend(meta, lengths, holders, near_queries, *rest)
    arrived = lax.ppermute(send, "core", swap)
    keep = attend(meta, lengths, holders, far_queries, *rest)

    shape = (2 * z_count, CHUNK, 2 * half)
    merged = call(merge_kernel, array(shape, bf16), 0, "merge")(keep.reshape(shape), arrived.reshape(shape))
    parts = lax.all_to_all(merged, ("pair", "z"), split_axis=0, concat_axis=0, tiled=True)
    attention = call(combine_kernel, array((half, width), bf16), 0, "combine")(parts)
    near_rows = lax.all_gather(attention, "z", axis=0)
    far_rows = lax.ppermute(near_rows, "core", swap)
    weight = out_weight.reshape(z_count, 2, width, width)
    place = core.reshape(1)
    begun = call(functools.partial(project_kernel, 1), array((half, width), f32), 1, "project_near")(
        place, near_rows, weight, residual
    )
    out = call(functools.partial(project_kernel, 0), array((half, width), bf16), 1, "project_far")(
        place, far_rows, weight, begun
    )
    return out.reshape(levels, beams, width)


def solution(mesh):
    split = Mesh(mesh.devices.reshape(16, 2, 8, 2), ("grp", "pair", "z", "core"))
    req, hist = ("grp", "pair"), ("z", "core")
    in_specs = (
        P(None, req),
        P(req),
        P(),
        P(),
        P(req, hist, None),
        P(req, hist, None),
        P(None, None, hist),
        P(None, None, hist),
        P(None, None, hist),
        P(None, hist),
    )
    return jax.shard_map(shards, mesh=split, in_specs=in_specs, out_specs=P(None, req, hist), check_vma=False)
```

```python
import functools
import math

import jax
import jax.numpy as jnp
from jax import lax
from jax.experimental import pallas as pl
from jax.experimental.pallas import tpu as pltpu
from jax.sharding import Mesh, PartitionSpec as P

KEY_HEADS = 8
HEAD = 128
STAT = 16
CHUNK = HEAD + STAT
DEAD = -1e30
EXP2_SCALE = HEAD ** (-0.5) * math.log2(math.e)
VMEM_LIMIT = 32 * 1024 * 1024


def params():
    return pltpu.CompilerParams(vmem_limit_bytes=VMEM_LIMIT)


def one_hot_rows(index_row, count):
    rows = index_row.shape[1]
    tall = jnp.transpose(jnp.broadcast_to(index_row, (128, rows)))
    parts = []
    for start in range(0, count, 128):
        lane = lax.broadcasted_iota(jnp.int32, (rows, 128), 1) + start
        parts.append((tall == lane).astype(jnp.float32).astype(jnp.bfloat16))
    return jnp.concatenate(parts, axis=1)


def look(hot, table_ref):
    return jnp.dot(hot, table_ref[...], preferred_element_type=jnp.float32)


def own_kernel(index_ref, query_ref, kv_ref, embed_ref, query_out, kv_out, residual_out):
    rows = query_out.shape[0]
    hot = one_hot_rows(index_ref[...], query_ref.shape[0])
    query_out[...] = look(hot, query_ref)[:rows].astype(jnp.bfloat16)
    kv_out[...] = look(hot, kv_ref)[:rows].astype(jnp.bfloat16)
    residual_out[...] = look(hot, embed_ref)[:rows]


def both_kernel(pair_ref, index_ref, query_ref, kv_ref, own_query_ref, own_kv_ref, query_out, kv_out):
    rows = own_query_ref.shape[0]
    hot = one_hot_rows(index_ref[...], query_ref.shape[0])
    mine = pl.ds(pl.multiple_of(pair_ref[0] * rows, rows), rows)
    theirs = pl.ds(pl.multiple_of((1 - pair_ref[0]) * rows, rows), rows)
    found = look(hot, query_ref)[:rows].astype(jnp.bfloat16)
    for copy in range(query_out.shape[0]):
        query_out[copy, mine] = own_query_ref[...]
        query_out[copy, theirs] = found
    kv_out[mine] = own_kv_ref[...]
    kv_out[theirs] = look(hot, kv_ref)[:rows].astype(jnp.bfloat16)


def stage_kernel(*refs):
    *blocks, key_out, value_out = refs
    slots = blocks[0].shape[0]
    for block in range(len(blocks) // 2):
        key_ref, value_ref = blocks[2 * block : 2 * block + 2]
        span = slice(block * slots, (block + 1) * slots)
        for head in range(key_out.shape[0]):
            lanes = slice(head * HEAD, (head + 1) * HEAD)
            key_out[head, span] = key_ref[:, lanes]
            value_out[head, 0:HEAD, span] = jnp.transpose(value_ref[:, lanes])
            value_out[head, HEAD:CHUNK, span] = jnp.ones((STAT, slots), jnp.bfloat16)


def split3(value):
    high = value.astype(jnp.bfloat16).astype(jnp.float32)
    rest = value - high
    middle = rest.astype(jnp.bfloat16).astype(jnp.float32)
    return high, middle, rest - middle


def stat_rows(top, total):
    row = lax.broadcasted_iota(jnp.int32, (STAT, top.shape[1]), 0)
    out = jnp.zeros((STAT, top.shape[1]), jnp.float32)
    for at, piece in enumerate(split3(top) + split3(total)):
        out = jnp.where(row == at, piece, out)
    return out.astype(jnp.bfloat16)


def read_stats(rows):
    wide = rows.astype(jnp.float32)
    return wide[0:1] + wide[1:2] + wide[2:3], wide[3:4] + wide[4:5] + wide[5:6]


def scores_of(keys, rows):
    return lax.dot_general(keys, rows, (((1,), (1,)), ((), ())), preferred_element_type=jnp.float32)


def attend_kernel(
    meta_ref, lengths_ref, holders_ref, query_ref, key_ref, value_ref, gen_key_ref, gen_value_ref, parent_ref,
    out_ref, score_ref,
):
    heads, slots = key_ref.shape[0], key_ref.shape[1]
    half = query_ref.shape[1] // 2
    width = 4 * half
    request, place, gen_head = meta_ref[0], meta_ref[1], meta_ref[2]

    block_slots = slots // 2
    near, far = jnp.int32(0), jnp.int32(0)
    for block in range(holders_ref.shape[1]):
        holder = holders_ref[request, block]
        near = jnp.where(holder == place, block, near)
        far = jnp.where(holder == jnp.bitwise_xor(place, 1), block, far)
    near_live, far_live = (
        jnp.clip(lengths_ref[request] - each * block_slots, 0, block_slots) for each in (near, far)
    )
    live = near_live + far_live

    def queries(head):
        pair = query_ref[head]
        return jnp.concatenate(
            [pair[x * half : (x + 1) * half, h * HEAD : (h + 1) * HEAD] for x in range(2) for h in range(2)], axis=0
        )

    def write(head, sums, total, top):
        for x in range(2):
            lanes = slice(x * 2 * half, (x + 1) * 2 * half)
            out_ref[x, head, 0:HEAD] = sums[:, lanes].astype(jnp.bfloat16)
            out_ref[x, head, HEAD:CHUNK] = stat_rows(top[:, lanes], total[:, lanes])

    def attend(masked):
        def score(head, at):
            scores = scores_of(key_ref[head], queries(head))
            if masked:
                slot = lax.broadcasted_iota(jnp.int32, (slots, 1), 0)
                allowed = (slot < near_live) | ((slot >= block_slots) & (slot < block_slots + far_live))
                scores = jnp.where(allowed, scores, DEAD)
            score_ref[at] = scores
            return jnp.max(scores, axis=0, keepdims=True)

        def finish(head, at, top):
            weights = jnp.exp2((score_ref[at] - top) * EXP2_SCALE).astype(jnp.bfloat16)
            sums = jnp.dot(value_ref[head], weights, preferred_element_type=jnp.float32)
            write(head, sums[0:HEAD], sums[HEAD : HEAD + 1], top)

        def step(i, top):
            later = score(2 * i + 1, 1)
            finish(2 * i, 0, top)
            top = score(jnp.minimum(2 * i + 2, heads - 1), 0)
            finish(2 * i + 1, 1, later)
            return top

        top = lax.fori_loop(0, heads // 2 - 1, step, score(0, 0))
        later = score(heads - 1, 1)
        finish(heads - 2, 0, top)
        finish(heads - 1, 1, later)

    @pl.when(live == slots)
    def _():
        attend(False)

    @pl.when((live > 0) & (live < slots))
    def _():
        attend(True)

    @pl.when(live == 0)
    def _():
        row = lax.broadcasted_iota(jnp.int32, (CHUNK, 2 * half), 0)
        tops = split3(jnp.full((CHUNK, 2 * half), DEAD, jnp.float32))
        dead = jnp.zeros((CHUNK, 2 * half), jnp.float32)
        for at, piece in enumerate(tops):
            dead = jnp.where(row == HEAD + at, piece, dead)
        dead = dead.astype(jnp.bfloat16)
        for x in range(2):
            for head in range(heads):
                out_ref[x, head] = dead

    @pl.when(gen_head >= 0)
    def _():
        values = jnp.concatenate(
            [jnp.transpose(gen_value_ref[...]), jnp.ones((STAT, 2 * half), jnp.bfloat16)], axis=0
        )
        row = lax.broadcasted_iota(jnp.int32, (2 * half, width), 0)
        lane = lax.broadcasted_iota(jnp.int32, (2 * half, width), 1)
        own = (lane // (2 * half)) * half + lane % half
        allowed = (row == own) | (row == parent_ref[...])
        scores = jnp.where(allowed, scores_of(gen_key_ref[...], queries(gen_head)), DEAD)
        before = jnp.concatenate([out_ref[x, gen_head] for x in range(2)], axis=1)
        old_top, old_total = read_stats(before[HEAD:CHUNK])
        top = jnp.maximum(old_top, jnp.max(scores, axis=0, keepdims=True))
        weights = jnp.where(allowed, jnp.exp2((scores - top) * EXP2_SCALE), 0.0)
        high = weights.astype(jnp.bfloat16)
        low = (weights - high.astype(jnp.float32)).astype(jnp.bfloat16)
        added = jnp.dot(values, high, preferred_element_type=jnp.float32)
        added = added + jnp.dot(values, low, preferred_element_type=jnp.float32)
        factor = jnp.exp2((old_top - top) * EXP2_SCALE)
        sums = before[0:HEAD].astype(jnp.float32) * factor + added[0:HEAD]
        write(gen_head, sums, old_total * factor + added[HEAD : HEAD + 1], top)


def combine_kernel(parts_ref, out_ref):
    count = parts_ref.shape[0]
    stats = [read_stats(parts_ref[part, HEAD:CHUNK]) for part in range(count)]
    top = functools.reduce(jnp.maximum, [each for each, _ in stats])
    total = jnp.zeros_like(top)
    sums = jnp.zeros((HEAD, parts_ref.shape[2]), jnp.float32)
    for part in range(count):
        factor = jnp.exp2((stats[part][0] - top) * EXP2_SCALE)
        total = total + stats[part][1] * factor
        sums = sums + parts_ref[part, 0:HEAD].astype(jnp.float32) * factor
    tall = jnp.transpose(sums / total)
    rows = out_ref.shape[0]
    out_ref[...] = jnp.concatenate([tall[0:rows], tall[rows : 2 * rows]], axis=1).astype(jnp.bfloat16)


def project_kernel(rows_ref, weight_ref, residual_ref, out_ref):
    total = residual_ref[...]
    for part in range(rows_ref.shape[0]):
        total = total + jnp.dot(rows_ref[part], weight_ref[part], preferred_element_type=jnp.float32)
    out_ref[...] = total.astype(out_ref.dtype)


def call(kernel, out_shape, scalars, name, **rest):
    specs = lambda count, space: [pl.BlockSpec(memory_space=space)] * count

    def run(*args):
        return pl.pallas_call(
            kernel,
            out_shape=out_shape,
            in_specs=specs(scalars, pltpu.SMEM) + specs(len(args) - scalars, pltpu.VMEM),
            out_specs=jax.tree.map(lambda _: pl.BlockSpec(memory_space=pltpu.VMEM), out_shape),
            compiler_params=params(),
            name=name,
            **rest,
        )(*args)

    return run


def shards(
    codes, parents, lengths, holders, history_keys, history_values, query_table, kv_table, embed_table, out_weight
):
    beams = parents.shape[0]
    levels, code_count, width = query_table.shape
    half = levels * beams
    rows = 2 * half
    slots = history_keys.shape[1]
    z_count = lax.axis_size("z")
    pair, z, core = lax.axis_index("pair"), lax.axis_index("z"), lax.axis_index("core")
    hist = 2 * z + core
    first = pair == 0
    bf16, f32 = jnp.bfloat16, jnp.float32
    array = jax.ShapeDtypeStruct
    swap = [(0, 1), (1, 0)]

    mine = jnp.concatenate([codes, parents[None]])
    other = lax.ppermute(mine, "pair", swap)
    other_codes, other_parents = other[:levels], other[levels]
    near_keys, near_values = history_keys[0], history_values[0]
    far_keys = lax.ppermute(near_keys, "core", swap)
    far_values = lax.ppermute(near_values, "core", swap)

    def index_of(picks):
        flat = (picks + code_count * jnp.arange(levels, dtype=jnp.int32)[:, None]).reshape(half)
        return jnp.concatenate([flat, flat]).reshape(1, rows)

    query_flat = query_table.reshape(levels * code_count, width)
    kv_flat = kv_table.reshape(levels * code_count, HEAD)
    embed_flat = embed_table.reshape(levels * code_count, width)
    own_query, own_kv, residual = call(
        own_kernel, (array((half, width), bf16), array((half, HEAD), bf16), array((half, width), f32)), 0, "own"
    )(index_of(codes), query_flat, kv_flat, embed_flat)
    query_rows, kv_rows = call(
        both_kernel, (array((z_count, rows, width), bf16), array((rows, HEAD), bf16)), 1, "both"
    )(pair.reshape(1), index_of(other_codes), query_flat, kv_flat, own_query, own_kv)
    queries = lax.all_to_all(query_rows, "z", split_axis=0, concat_axis=0, tiled=True)
    far_kv = lax.ppermute(kv_rows, "core", swap)
    gen_keys = jnp.where(first, kv_rows, far_kv)
    gen_values = lax.ppermute(gen_keys, "z", [(i + z_count // 2, i) for i in range(z_count // 2)])
    staged_keys, staged_values = call(
        stage_kernel,
        (array((KEY_HEADS, 2 * slots, HEAD), bf16), array((KEY_HEADS, CHUNK, 2 * slots), bf16)),
        0,
        "stage",
    )(near_keys, near_values, far_keys, far_values)

    lower = jnp.where(first, parents, other_parents)
    upper = jnp.where(first, other_parents, parents)
    both = jnp.stack([lower, upper])
    parent_rows = (both // beams) * half + both % beams
    parent_lanes = jnp.concatenate([jnp.full((2, beams), -1, jnp.int32), parent_rows], axis=1)
    parent_lanes = jnp.broadcast_to(parent_lanes[:, None, :], (2, 2, half)).reshape(1, 2 * rows)

    gen_head = jnp.where(z < z_count // 2, 2 * z + jnp.bitwise_xor(core, pair), -1)
    meta = jnp.stack([lax.axis_index("grp"), pair * 2 * z_count + hist, gen_head]).astype(jnp.int32)
    partials = call(
        attend_kernel,
        array((2, z_count, CHUNK, 2 * half), bf16),
        3,
        "attend",
        scratch_shapes=[pltpu.VMEM((2, 2 * slots, 2 * rows), f32)],
        cost_estimate=pl.CostEstimate(
            flops=4 * 4 * rows * KEY_HEADS * slots * HEAD,
            bytes_accessed=4 * slots * KEY_HEADS * HEAD,
            transcendentals=4 * rows * KEY_HEADS * slots,
        ),
    )(meta, lengths, holders, queries, staged_keys, staged_values, gen_keys, gen_values, parent_lanes)

    shape = (2 * z_count, CHUNK, 2 * half)
    parts = lax.all_to_all(partials.reshape(shape), ("pair", "z"), split_axis=0, concat_axis=0, tiled=True)
    attention = call(combine_kernel, array((half, width), bf16), 0, "combine")(parts)
    gathered = lax.all_gather(attention, ("z", "core"), axis=0)
    out = call(project_kernel, array((half, width), bf16), 0, "project")(
        gathered, out_weight.reshape(2 * z_count, width, width), residual
    )
    return out.reshape(levels, beams, width)


def solution(mesh):
    split = Mesh(mesh.devices.reshape(16, 2, 8, 2), ("grp", "pair", "z", "core"))
    req, hist = ("grp", "pair"), ("z", "core")
    in_specs = (
        P(None, req),
        P(req),
        P(),
        P(),
        P(req, hist, None),
        P(req, hist, None),
        P(None, None, hist),
        P(None, None, hist),
        P(None, None, hist),
        P(None, hist),
    )
    return jax.shard_map(shards, mesh=split, in_specs=in_specs, out_specs=P(None, req, hist), check_vma=False)
```

```python
import functools
import math

import jax
import jax.numpy as jnp
from jax import lax
from jax.experimental import pallas as pl
from jax.experimental.pallas import tpu as pltpu
from jax.sharding import Mesh, PartitionSpec as P

KEY_HEADS = 8
HEAD = 128
STAT = 16
CHUNK = HEAD + STAT
DEAD = -1e30
EXP2_SCALE = HEAD ** (-0.5) * math.log2(math.e)
MIB = 1024 * 1024


def one_hot_rows(index_row, count):
    rows = index_row.shape[1]
    tall = jnp.transpose(jnp.broadcast_to(index_row, (128, rows)))
    parts = []
    for start in range(0, count, 128):
        lane = lax.broadcasted_iota(jnp.int32, (rows, 128), 1) + start
        parts.append((tall == lane).astype(jnp.float32).astype(jnp.bfloat16))
    return jnp.concatenate(parts, axis=1)


def residual_kernel(codes_ref, embed_hbm, out_ref, embed_ref, sem):
    copy = pltpu.make_async_copy(embed_hbm, embed_ref, sem.at[0])
    copy.start()
    beams = codes_ref.shape[1]
    hots = [one_hot_rows(codes_ref[level : level + 1], embed_ref.shape[1]) for level in range(codes_ref.shape[0])]
    copy.wait()
    for level, hot in enumerate(hots):
        out_ref[level * beams : (level + 1) * beams] = jnp.dot(
            hot, embed_ref[level], preferred_element_type=jnp.float32
        )


def look_kernel(pair_ref, mine_ref, other_ref, query_hbm, kv_hbm, query_out, kv_out, query_ref, kv_ref, sem):
    copies = [
        pltpu.make_async_copy(query_hbm, query_ref, sem.at[0]),
        pltpu.make_async_copy(kv_hbm, kv_ref, sem.at[1]),
    ]
    for copy in copies:
        copy.start()
    levels, beams = mine_ref.shape
    hots = [
        jnp.concatenate([one_hot_rows(ref[level : level + 1], query_ref.shape[1]) for ref in (mine_ref, other_ref)])
        for level in range(levels)
    ]
    for copy in copies:
        copy.wait()
    half = levels * beams
    for level, hot in enumerate(hots):
        queries = jnp.dot(hot, query_ref[level], preferred_element_type=jnp.float32).astype(jnp.bfloat16)
        kvs = jnp.dot(hot, kv_ref[level], preferred_element_type=jnp.float32).astype(jnp.bfloat16)
        for part, x in enumerate((pair_ref[0], 1 - pair_ref[0])):
            rows = slice(part * beams, (part + 1) * beams)
            place = pl.ds(pl.multiple_of(x * half + level * beams, beams), beams)
            for copy in range(query_out.shape[0]):
                query_out[copy, place] = queries[rows]
            kv_out[place] = kvs[rows]


def stage_kernel(*refs):
    *blocks, key_out, value_out, value_ref, key_sem, value_sem = refs
    heads = key_out.shape[0]
    count = len(blocks) // 2
    slots = value_ref.shape[1]
    key_copies, value_copies = [], []
    for block in range(count):
        span = pl.ds(block * slots, slots)
        value_copies.append(
            pltpu.make_async_copy(blocks[2 * block + 1], value_ref.at[block], value_sem.at[block])
        )
        for head in range(heads):
            lanes = pl.ds(head * HEAD, HEAD)
            key_copies.append(
                pltpu.make_async_copy(
                    blocks[2 * block].at[:, lanes], key_out.at[head, span], key_sem.at[block * heads + head]
                )
            )
    for copy in value_copies + key_copies:
        copy.start()
    value_out[:, HEAD:CHUNK] = jnp.ones((heads, STAT, count * slots), jnp.bfloat16)
    for block in range(count):
        value_copies[block].wait()
        for head in range(heads):
            lanes = slice(head * HEAD, (head + 1) * HEAD)
            value_out[head, 0:HEAD, block * slots : (block + 1) * slots] = jnp.transpose(value_ref[block, :, lanes])
    for copy in key_copies:
        copy.wait()


def split3(value):
    high = value.astype(jnp.bfloat16).astype(jnp.float32)
    rest = value - high
    middle = rest.astype(jnp.bfloat16).astype(jnp.float32)
    return high, middle, rest - middle


def stat_rows(top, total):
    row = lax.broadcasted_iota(jnp.int32, (STAT, top.shape[1]), 0)
    out = jnp.zeros((STAT, top.shape[1]), jnp.float32)
    for at, piece in enumerate(split3(top) + split3(total)):
        out = jnp.where(row == at, piece, out)
    return out.astype(jnp.bfloat16)


def read_stats(rows):
    wide = rows.astype(jnp.float32)
    return wide[0:1] + wide[1:2] + wide[2:3], wide[3:4] + wide[4:5] + wide[5:6]


def scores_of(keys, rows):
    return lax.dot_general(keys, rows, (((1,), (1,)), ((), ())), preferred_element_type=jnp.float32)


def attend_kernel(
    meta_ref, lengths_ref, holders_ref, query_ref, key_ref, value_ref, gen_key_ref, gen_value_ref, parent_ref,
    out_ref, score_ref,
):
    heads, slots = key_ref.shape[0], key_ref.shape[1]
    half = query_ref.shape[1] // 2
    width = 4 * half
    request, place, gen_head = meta_ref[0], meta_ref[1], meta_ref[2]

    block_slots = slots // 2
    near, far = jnp.int32(0), jnp.int32(0)
    for block in range(holders_ref.shape[1]):
        holder = holders_ref[request, block]
        near = jnp.where(holder == place, block, near)
        far = jnp.where(holder == jnp.bitwise_xor(place, 1), block, far)
    near_live, far_live = (
        jnp.clip(lengths_ref[request] - each * block_slots, 0, block_slots) for each in (near, far)
    )
    live = near_live + far_live

    def queries(head):
        pair = query_ref[head]
        return jnp.concatenate(
            [pair[x * half : (x + 1) * half, h * HEAD : (h + 1) * HEAD] for x in range(2) for h in range(2)], axis=0
        )

    def write(head, sums, total, top):
        for x in range(2):
            lanes = slice(x * 2 * half, (x + 1) * 2 * half)
            out_ref[x, head, 0:HEAD] = sums[:, lanes].astype(jnp.bfloat16)
            out_ref[x, head, HEAD:CHUNK] = stat_rows(top[:, lanes], total[:, lanes])

    def attend(masked):
        def score(head, at):
            scores = scores_of(key_ref[head], queries(head))
            if masked:
                slot = lax.broadcasted_iota(jnp.int32, (slots, 1), 0)
                allowed = (slot < near_live) | ((slot >= block_slots) & (slot < block_slots + far_live))
                scores = jnp.where(allowed, scores, DEAD)
            score_ref[at] = scores
            return jnp.max(scores, axis=0, keepdims=True)

        def finish(head, at, top):
            weights = jnp.exp2((score_ref[at] - top) * EXP2_SCALE).astype(jnp.bfloat16)
            sums = jnp.dot(value_ref[head], weights, preferred_element_type=jnp.float32)
            write(head, sums[0:HEAD], sums[HEAD : HEAD + 1], top)

        def step(i, top):
            later = score(2 * i + 1, 1)
            finish(2 * i, 0, top)
            top = score(jnp.minimum(2 * i + 2, heads - 1), 0)
            finish(2 * i + 1, 1, later)
            return top

        top = lax.fori_loop(0, heads // 2 - 1, step, score(0, 0))
        later = score(heads - 1, 1)
        finish(heads - 2, 0, top)
        finish(heads - 1, 1, later)

    @pl.when(live == slots)
    def _():
        attend(False)

    @pl.when((live > 0) & (live < slots))
    def _():
        attend(True)

    @pl.when(live == 0)
    def _():
        row = lax.broadcasted_iota(jnp.int32, (CHUNK, 2 * half), 0)
        tops = split3(jnp.full((CHUNK, 2 * half), DEAD, jnp.float32))
        dead = jnp.zeros((CHUNK, 2 * half), jnp.float32)
        for at, piece in enumerate(tops):
            dead = jnp.where(row == HEAD + at, piece, dead)
        dead = dead.astype(jnp.bfloat16)
        for x in range(2):
            for head in range(heads):
                out_ref[x, head] = dead

    @pl.when(gen_head >= 0)
    def _():
        values = jnp.concatenate(
            [jnp.transpose(gen_value_ref[...]), jnp.ones((STAT, 2 * half), jnp.bfloat16)], axis=0
        )
        row = lax.broadcasted_iota(jnp.int32, (2 * half, width), 0)
        lane = lax.broadcasted_iota(jnp.int32, (2 * half, width), 1)
        own = (lane // (2 * half)) * half + lane % half
        allowed = (row == own) | (row == parent_ref[...])
        scores = jnp.where(allowed, scores_of(gen_key_ref[...], queries(gen_head)), DEAD)
        before = jnp.concatenate([out_ref[x, gen_head] for x in range(2)], axis=1)
        old_top, old_total = read_stats(before[HEAD:CHUNK])
        top = jnp.maximum(old_top, jnp.max(scores, axis=0, keepdims=True))
        weights = jnp.where(allowed, jnp.exp2((scores - top) * EXP2_SCALE), 0.0)
        high = weights.astype(jnp.bfloat16)
        low = (weights - high.astype(jnp.float32)).astype(jnp.bfloat16)
        added = jnp.dot(values, high, preferred_element_type=jnp.float32)
        added = added + jnp.dot(values, low, preferred_element_type=jnp.float32)
        factor = jnp.exp2((old_top - top) * EXP2_SCALE)
        sums = before[0:HEAD].astype(jnp.float32) * factor + added[0:HEAD]
        write(gen_head, sums, old_total * factor + added[HEAD : HEAD + 1], top)


def combine_kernel(parts_ref, out_ref):
    count = parts_ref.shape[0]
    stats = [read_stats(parts_ref[part, HEAD:CHUNK]) for part in range(count)]
    top = functools.reduce(jnp.maximum, [each for each, _ in stats])
    total = jnp.zeros_like(top)
    sums = jnp.zeros((HEAD, parts_ref.shape[2]), jnp.float32)
    for part in range(count):
        factor = jnp.exp2((stats[part][0] - top) * EXP2_SCALE)
        total = total + stats[part][1] * factor
        sums = sums + parts_ref[part, 0:HEAD].astype(jnp.float32) * factor
    tall = jnp.transpose(sums / total)
    rows = out_ref.shape[0]
    out_ref[...] = jnp.concatenate([tall[0:rows], tall[rows : 2 * rows]], axis=1).astype(jnp.bfloat16)


def project_kernel(rows_ref, weight_ref, residual_ref, out_ref):
    total = residual_ref[...]
    for part in range(rows_ref.shape[0]):
        total = total + jnp.dot(rows_ref[part], weight_ref[part], preferred_element_type=jnp.float32)
    out_ref[...] = total.astype(out_ref.dtype)


def call(kernel, out_shape, name, spaces, vmem, **rest):
    kinds = {"s": pltpu.SMEM, "v": pltpu.VMEM, "h": pltpu.HBM, "a": pl.ANY}
    return pl.pallas_call(
        kernel,
        out_shape=out_shape,
        in_specs=[pl.BlockSpec(memory_space=kinds[space]) for space in spaces],
        out_specs=jax.tree.map(lambda _: pl.BlockSpec(memory_space=pltpu.VMEM), out_shape),
        compiler_params=pltpu.CompilerParams(vmem_limit_bytes=vmem * MIB),
        name=name,
        **rest,
    )


def shards(
    codes, parents, lengths, holders, history_keys, history_values, query_table, kv_table, embed_table, out_weight
):
    beams = parents.shape[0]
    levels, code_count, width = query_table.shape
    half = levels * beams
    rows = 2 * half
    slots = history_keys.shape[1]
    z_count = lax.axis_size("z")
    pair, z, core = lax.axis_index("pair"), lax.axis_index("z"), lax.axis_index("core")
    hist = 2 * z + core
    first = pair == 0
    bf16, f32 = jnp.bfloat16, jnp.float32
    array = jax.ShapeDtypeStruct
    dma = pltpu.SemaphoreType.DMA
    swap = [(0, 1), (1, 0)]

    other_codes = lax.ppermute(codes, "pair", swap)
    residual = call(
        residual_kernel,
        array((half, width), f32),
        "residual",
        "vh",
        4,
        scratch_shapes=[pltpu.VMEM(embed_table.shape, bf16), dma((1,))],
    )(codes, embed_table)

    query_rows, kv_rows = call(
        look_kernel,
        (array((z_count, rows, width), bf16), array((rows, HEAD), bf16)),
        "look",
        "svvhh",
        4,
        scratch_shapes=[pltpu.VMEM(query_table.shape, bf16), pltpu.VMEM(kv_table.shape, bf16), dma((2,))],
    )(pair.reshape(1), codes, other_codes, query_table, kv_table)
    queries = lax.all_to_all(query_rows, "z", split_axis=0, concat_axis=0, tiled=True)

    kv_rows, near_keys, near_values, parents = lax.optimization_barrier(
        (kv_rows, history_keys[0], history_values[0], parents)
    )
    far_keys = lax.ppermute(near_keys, "core", swap)
    far_values = lax.ppermute(near_values, "core", swap)
    far_kv = lax.ppermute(kv_rows, "core", swap)
    other_parents = lax.ppermute(parents, "pair", swap)
    gen_keys = jnp.where(first, kv_rows, far_kv)
    gen_values = lax.ppermute(gen_keys, "z", [(i + z_count // 2, i) for i in range(z_count // 2)])
    staged_keys, staged_values = call(
        stage_kernel,
        (array((KEY_HEADS, 2 * slots, HEAD), bf16), array((KEY_HEADS, CHUNK, 2 * slots), bf16)),
        "stage",
        "hhaa",
        8,
        scratch_shapes=[pltpu.VMEM((2, slots, KEY_HEADS * HEAD), bf16), dma((2 * KEY_HEADS,)), dma((2,))],
        cost_estimate=pl.CostEstimate(flops=0, bytes_accessed=16 * MIB, transcendentals=0),
    )(near_keys, near_values, far_keys, far_values)

    lower = jnp.where(first, parents, other_parents)
    upper = jnp.where(first, other_parents, parents)
    both = jnp.stack([lower, upper])
    parent_rows = (both // beams) * half + both % beams
    parent_lanes = jnp.concatenate([jnp.full((2, beams), -1, jnp.int32), parent_rows], axis=1)
    parent_lanes = jnp.broadcast_to(parent_lanes[:, None, :], (2, 2, half)).reshape(1, 2 * rows)

    gen_head = jnp.where(z < z_count // 2, 2 * z + jnp.bitwise_xor(core, pair), -1)
    meta = jnp.stack([lax.axis_index("grp"), pair * 2 * z_count + hist, gen_head]).astype(jnp.int32)
    partials = call(
        attend_kernel,
        array((2, z_count, CHUNK, 2 * half), bf16),
        "attend",
        "sssvvvvvv",
        16,
        scratch_shapes=[pltpu.VMEM((2, 2 * slots, 2 * rows), f32)],
        cost_estimate=pl.CostEstimate(
            flops=4 * 4 * rows * KEY_HEADS * slots * HEAD,
            bytes_accessed=4 * slots * KEY_HEADS * HEAD,
            transcendentals=4 * rows * KEY_HEADS * slots,
        ),
    )(meta, lengths, holders, queries, staged_keys, staged_values, gen_keys, gen_values, parent_lanes)

    shape = (2 * z_count, CHUNK, 2 * half)
    parts = lax.all_to_all(partials.reshape(shape), ("pair", "z"), split_axis=0, concat_axis=0, tiled=True)
    attention = call(combine_kernel, array((half, width), bf16), "combine", "v", 4)(parts)
    gathered = lax.all_gather(attention, ("z", "core"), axis=0)
    out = call(project_kernel, array((half, width), bf16), "project", "vvv", 4)(
        gathered, out_weight.reshape(2 * z_count, width, width), residual
    )
    return out.reshape(levels, beams, width)


def solution(mesh):
    split = Mesh(mesh.devices.reshape(16, 2, 8, 2), ("grp", "pair", "z", "core"))
    req, hist = ("grp", "pair"), ("z", "core")
    in_specs = (
        P(None, req),
        P(req),
        P(),
        P(),
        P(req, hist, None),
        P(req, hist, None),
        P(None, None, hist),
        P(None, None, hist),
        P(None, None, hist),
        P(None, hist),
    )
    return jax.shard_map(shards, mesh=split, in_specs=in_specs, out_specs=P(None, req, hist), check_vma=False)
```

```python
import functools
import math

import jax
import jax.numpy as jnp
from jax import lax
from jax.experimental import pallas as pl
from jax.experimental.pallas import tpu as pltpu
from jax.sharding import Mesh, PartitionSpec as P

KEY_HEADS = 8
HEAD = 128
STAT = 16
CHUNK = HEAD + STAT
DEAD = -1e30
EXP2_SCALE = HEAD ** (-0.5) * math.log2(math.e)
MIB = 1024 * 1024


def one_hot_rows(index_row, count):
    rows = index_row.shape[1]
    tall = jnp.transpose(jnp.broadcast_to(index_row, (128, rows)))
    parts = []
    for start in range(0, count, 128):
        lane = lax.broadcasted_iota(jnp.int32, (rows, 128), 1) + start
        parts.append((tall == lane).astype(jnp.float32).astype(jnp.bfloat16))
    return jnp.concatenate(parts, axis=1)


def residual_kernel(codes_ref, embed_hbm, out_ref, embed_ref, sem):
    copy = pltpu.make_async_copy(embed_hbm, embed_ref, sem.at[0])
    copy.start()
    beams = codes_ref.shape[1]
    hots = [one_hot_rows(codes_ref[level : level + 1], embed_ref.shape[1]) for level in range(codes_ref.shape[0])]
    copy.wait()
    for level, hot in enumerate(hots):
        out_ref[level * beams : (level + 1) * beams] = jnp.dot(
            hot, embed_ref[level], preferred_element_type=jnp.float32
        )


def look_kernel(codes_ref, query_hbm, out_ref, query_ref, sem):
    copy = pltpu.make_async_copy(query_hbm, query_ref, sem.at[0])
    copy.start()
    levels, beams = codes_ref.shape
    hots = [one_hot_rows(codes_ref[level : level + 1], query_ref.shape[1]) for level in range(levels)]
    copy.wait()
    for level, hot in enumerate(hots):
        found = jnp.dot(hot, query_ref[level], preferred_element_type=jnp.float32).astype(jnp.bfloat16)
        for target in range(out_ref.shape[0]):
            out_ref[target, level * beams : (level + 1) * beams] = found


def generated_kernel(pair_ref, mine_ref, other_ref, kv_hbm, out_ref, kv_ref, sem):
    copy = pltpu.make_async_copy(kv_hbm, kv_ref, sem.at[0])
    copy.start()
    levels, beams = kv_ref.shape[0], mine_ref.shape[1]
    hots = [
        jnp.concatenate([one_hot_rows(ref[level : level + 1], kv_ref.shape[1]) for ref in (mine_ref, other_ref)])
        for level in range(levels)
    ]
    copy.wait()
    for level, hot in enumerate(hots):
        found = jnp.dot(hot, kv_ref[level], preferred_element_type=jnp.float32).astype(jnp.bfloat16)
        for part, x in enumerate((pair_ref[0], 1 - pair_ref[0])):
            place = pl.ds(pl.multiple_of((x * levels + level) * beams, beams), beams)
            out_ref[place] = found[part * beams : (part + 1) * beams]


def stage_kernel(*refs):
    *blocks, key_out, value_out, value_ref, key_sem, value_sem = refs
    heads = key_out.shape[0]
    count = len(blocks) // 2
    slots = value_ref.shape[1]
    key_copies, value_copies = [], []
    for block in range(count):
        span = pl.ds(block * slots, slots)
        value_copies.append(
            pltpu.make_async_copy(blocks[2 * block + 1], value_ref.at[block], value_sem.at[block])
        )
        for head in range(heads):
            lanes = pl.ds(head * HEAD, HEAD)
            key_copies.append(
                pltpu.make_async_copy(
                    blocks[2 * block].at[:, lanes], key_out.at[head, span], key_sem.at[block * heads + head]
                )
            )
    for copy in value_copies + key_copies:
        copy.start()
    value_out[:, HEAD:CHUNK] = jnp.ones((heads, STAT, count * slots), jnp.bfloat16)
    for block in range(count):
        value_copies[block].wait()
        for head in range(heads):
            lanes = slice(head * HEAD, (head + 1) * HEAD)
            value_out[head, 0:HEAD, block * slots : (block + 1) * slots] = jnp.transpose(value_ref[block, :, lanes])
    for copy in key_copies:
        copy.wait()


def split3(value):
    high = value.astype(jnp.bfloat16).astype(jnp.float32)
    rest = value - high
    middle = rest.astype(jnp.bfloat16).astype(jnp.float32)
    return high, middle, rest - middle


def stat_rows(top, total):
    row = lax.broadcasted_iota(jnp.int32, (STAT, top.shape[1]), 0)
    out = jnp.zeros((STAT, top.shape[1]), jnp.float32)
    for at, piece in enumerate(split3(top) + split3(total)):
        out = jnp.where(row == at, piece, out)
    return out.astype(jnp.bfloat16)


def read_stats(rows):
    wide = rows.astype(jnp.float32)
    return wide[0:1] + wide[1:2] + wide[2:3], wide[3:4] + wide[4:5] + wide[5:6]


def scores_of(keys, rows):
    return lax.dot_general(keys, rows, (((1,), (1,)), ((), ())), preferred_element_type=jnp.float32)


def attend_kernel(
    meta_ref, lengths_ref, holders_ref, query_ref, key_ref, value_ref, gen_key_ref, gen_value_ref, parent_ref,
    out_ref, score_ref,
):
    heads, slots = key_ref.shape[0], key_ref.shape[1]
    half = query_ref.shape[1]
    width = 4 * half
    request, place, gen_head = meta_ref[0], meta_ref[1], meta_ref[2]

    block_slots = slots // 2
    near, far = jnp.int32(0), jnp.int32(0)
    for block in range(holders_ref.shape[1]):
        holder = holders_ref[request, block]
        near = jnp.where(holder == place, block, near)
        far = jnp.where(holder == jnp.bitwise_xor(place, 1), block, far)
    near_live, far_live = (
        jnp.clip(lengths_ref[request] - each * block_slots, 0, block_slots) for each in (near, far)
    )
    live = near_live + far_live

    def queries(head):
        pieces = []
        for x in range(2):
            pair = query_ref[x * heads + head]
            pieces += [pair[:, h * HEAD : (h + 1) * HEAD] for h in range(2)]
        return jnp.concatenate(pieces, axis=0)

    def write(head, sums, total, top):
        for x in range(2):
            lanes = slice(x * 2 * half, (x + 1) * 2 * half)
            out_ref[x, head, 0:HEAD] = sums[:, lanes].astype(jnp.bfloat16)
            out_ref[x, head, HEAD:CHUNK] = stat_rows(top[:, lanes], total[:, lanes])

    def attend(masked):
        def score(head, at):
            scores = scores_of(key_ref[head], queries(head))
            if masked:
                slot = lax.broadcasted_iota(jnp.int32, (slots, 1), 0)
                allowed = (slot < near_live) | ((slot >= block_slots) & (slot < block_slots + far_live))
                scores = jnp.where(allowed, scores, DEAD)
            score_ref[at] = scores
            return jnp.max(scores, axis=0, keepdims=True)

        def finish(head, at, top):
            weights = jnp.exp2((score_ref[at] - top) * EXP2_SCALE).astype(jnp.bfloat16)
            sums = jnp.dot(value_ref[head], weights, preferred_element_type=jnp.float32)
            write(head, sums[0:HEAD], sums[HEAD : HEAD + 1], top)

        def step(i, top):
            later = score(2 * i + 1, 1)
            finish(2 * i, 0, top)
            top = score(jnp.minimum(2 * i + 2, heads - 1), 0)
            finish(2 * i + 1, 1, later)
            return top

        top = lax.fori_loop(0, heads // 2 - 1, step, score(0, 0))
        later = score(heads - 1, 1)
        finish(heads - 2, 0, top)
        finish(heads - 1, 1, later)

    @pl.when(live == slots)
    def _():
        attend(False)

    @pl.when((live > 0) & (live < slots))
    def _():
        attend(True)

    @pl.when(live == 0)
    def _():
        row = lax.broadcasted_iota(jnp.int32, (CHUNK, 2 * half), 0)
        tops = split3(jnp.full((CHUNK, 2 * half), DEAD, jnp.float32))
        dead = jnp.zeros((CHUNK, 2 * half), jnp.float32)
        for at, piece in enumerate(tops):
            dead = jnp.where(row == HEAD + at, piece, dead)
        dead = dead.astype(jnp.bfloat16)
        for x in range(2):
            for head in range(heads):
                out_ref[x, head] = dead

    @pl.when(gen_head >= 0)
    def _():
        values = jnp.concatenate(
            [jnp.transpose(gen_value_ref[...]), jnp.ones((STAT, 2 * half), jnp.bfloat16)], axis=0
        )
        row = lax.broadcasted_iota(jnp.int32, (2 * half, width), 0)
        lane = lax.broadcasted_iota(jnp.int32, (2 * half, width), 1)
        own = (lane // (2 * half)) * half + lane % half
        allowed = (row == own) | (row == parent_ref[...])
        scores = jnp.where(allowed, scores_of(gen_key_ref[...], queries(gen_head)), DEAD)
        before = jnp.concatenate([out_ref[x, gen_head] for x in range(2)], axis=1)
        old_top, old_total = read_stats(before[HEAD:CHUNK])
        top = jnp.maximum(old_top, jnp.max(scores, axis=0, keepdims=True))
        weights = jnp.where(allowed, jnp.exp2((scores - top) * EXP2_SCALE), 0.0)
        high = weights.astype(jnp.bfloat16)
        low = (weights - high.astype(jnp.float32)).astype(jnp.bfloat16)
        added = jnp.dot(values, high, preferred_element_type=jnp.float32)
        added = added + jnp.dot(values, low, preferred_element_type=jnp.float32)
        factor = jnp.exp2((old_top - top) * EXP2_SCALE)
        sums = before[0:HEAD].astype(jnp.float32) * factor + added[0:HEAD]
        write(gen_head, sums, old_total * factor + added[HEAD : HEAD + 1], top)


def combine_kernel(parts_ref, out_ref):
    count = parts_ref.shape[0]
    stats = [read_stats(parts_ref[part, HEAD:CHUNK]) for part in range(count)]
    top = functools.reduce(jnp.maximum, [each for each, _ in stats])
    total = jnp.zeros_like(top)
    sums = jnp.zeros((HEAD, parts_ref.shape[2]), jnp.float32)
    for part in range(count):
        factor = jnp.exp2((stats[part][0] - top) * EXP2_SCALE)
        total = total + stats[part][1] * factor
        sums = sums + parts_ref[part, 0:HEAD].astype(jnp.float32) * factor
    tall = jnp.transpose(sums / total)
    rows = out_ref.shape[0]
    out_ref[...] = jnp.concatenate([tall[0:rows], tall[rows : 2 * rows]], axis=1).astype(jnp.bfloat16)


def project_kernel(rows_ref, weight_ref, residual_ref, out_ref):
    total = residual_ref[...]
    for part in range(rows_ref.shape[0]):
        total = total + jnp.dot(rows_ref[part], weight_ref[part], preferred_element_type=jnp.float32)
    out_ref[...] = total.astype(out_ref.dtype)


def call(kernel, out_shape, name, spaces, vmem, **rest):
    kinds = {"s": pltpu.SMEM, "v": pltpu.VMEM, "h": pltpu.HBM, "a": pl.ANY}
    return pl.pallas_call(
        kernel,
        out_shape=out_shape,
        in_specs=[pl.BlockSpec(memory_space=kinds[space]) for space in spaces],
        out_specs=jax.tree.map(lambda _: pl.BlockSpec(memory_space=pltpu.VMEM), out_shape),
        compiler_params=pltpu.CompilerParams(vmem_limit_bytes=vmem * MIB),
        name=name,
        **rest,
    )


def shards(
    codes, parents, lengths, holders, history_keys, history_values, query_table, kv_table, embed_table, out_weight
):
    beams = parents.shape[0]
    levels, code_count, width = query_table.shape
    half = levels * beams
    rows = 2 * half
    slots = history_keys.shape[1]
    z_count = lax.axis_size("z")
    pair, z, core = lax.axis_index("pair"), lax.axis_index("z"), lax.axis_index("core")
    hist = 2 * z + core
    first = pair == 0
    bf16, f32 = jnp.bfloat16, jnp.float32
    array = jax.ShapeDtypeStruct
    dma = pltpu.SemaphoreType.DMA
    swap = [(0, 1), (1, 0)]

    hbm = lambda x: pltpu.with_memory_space_constraint(x, pltpu.HBM)
    vmem = lambda x: pltpu.with_memory_space_constraint(x, pltpu.VMEM)

    query_rows = call(
        look_kernel,
        array((2 * z_count, half, width), bf16),
        "look",
        "vh",
        4,
        scratch_shapes=[pltpu.VMEM(query_table.shape, bf16), dma((1,))],
    )(codes, hbm(query_table))
    queries = lax.all_to_all(query_rows, ("pair", "z"), split_axis=0, concat_axis=0, tiled=True)
    residual = call(
        residual_kernel,
        array((half, width), f32),
        "residual",
        "vh",
        4,
        scratch_shapes=[pltpu.VMEM(embed_table.shape, bf16), dma((1,))],
    )(codes, hbm(embed_table))

    query_rows, mine, near_keys, near_values = lax.optimization_barrier(
        (query_rows, jnp.concatenate([codes, parents[None]]), history_keys[0], history_values[0])
    )
    other = lax.ppermute(mine, "pair", swap)
    other_parents = other[levels]
    far_keys = lax.ppermute(near_keys, "core", swap)
    far_values = lax.ppermute(near_values, "core", swap)
    kv_rows = call(
        generated_kernel,
        array((rows, HEAD), bf16),
        "generated",
        "svvh",
        4,
        scratch_shapes=[pltpu.VMEM(kv_table.shape, bf16), dma((1,))],
    )(pair.reshape(1), mine, other, hbm(kv_table))
    far_kv = lax.ppermute(kv_rows, "core", swap)
    gen_keys = jnp.where(first, kv_rows, far_kv)
    gen_values = lax.ppermute(gen_keys, "z", [(i + z_count // 2, i) for i in range(z_count // 2)])
    staged_keys, staged_values = call(
        stage_kernel,
        (pltpu.VMEM((KEY_HEADS, 2 * slots, HEAD), bf16), pltpu.VMEM((KEY_HEADS, CHUNK, 2 * slots), bf16)),
        "stage",
        "hhaa",
        8,
        scratch_shapes=[pltpu.VMEM((2, slots, KEY_HEADS * HEAD), bf16), dma((2 * KEY_HEADS,)), dma((2,))],
        cost_estimate=pl.CostEstimate(flops=0, bytes_accessed=16 * MIB, transcendentals=0),
    )(hbm(near_keys), hbm(near_values), far_keys, far_values)
    staged_keys, staged_values = vmem(staged_keys), vmem(staged_values)

    lower = jnp.where(first, parents, other_parents)
    upper = jnp.where(first, other_parents, parents)
    both = jnp.stack([lower, upper])
    parent_rows = (both // beams) * half + both % beams
    parent_lanes = jnp.concatenate([jnp.full((2, beams), -1, jnp.int32), parent_rows], axis=1)
    parent_lanes = jnp.broadcast_to(parent_lanes[:, None, :], (2, 2, half)).reshape(1, 2 * rows)

    gen_head = jnp.where(z < z_count // 2, 2 * z + jnp.bitwise_xor(core, pair), -1)
    meta = jnp.stack([lax.axis_index("grp"), pair * 2 * z_count + hist, gen_head]).astype(jnp.int32)
    partials = call(
        attend_kernel,
        array((2, z_count, CHUNK, 2 * half), bf16),
        "attend",
        "sssvvvvvv",
        16,
        scratch_shapes=[pltpu.VMEM((2, 2 * slots, 2 * rows), f32)],
        cost_estimate=pl.CostEstimate(
            flops=4 * 4 * rows * KEY_HEADS * slots * HEAD,
            bytes_accessed=4 * slots * KEY_HEADS * HEAD,
            transcendentals=4 * rows * KEY_HEADS * slots,
        ),
    )(meta, lengths, holders, queries, staged_keys, staged_values, gen_keys, gen_values, parent_lanes)

    shape = (2 * z_count, CHUNK, 2 * half)
    parts = lax.all_to_all(partials.reshape(shape), ("pair", "z"), split_axis=0, concat_axis=0, tiled=True)
    attention = call(combine_kernel, array((half, width), bf16), "combine", "v", 4)(parts)
    gathered = lax.all_gather(attention, ("z", "core"), axis=0)
    out = call(project_kernel, array((half, width), bf16), "project", "vvv", 4)(
        gathered, out_weight.reshape(2 * z_count, width, width), residual
    )
    return out.reshape(levels, beams, width)


def solution(mesh):
    split = Mesh(mesh.devices.reshape(16, 2, 8, 2), ("grp", "pair", "z", "core"))
    req, hist = ("grp", "pair"), ("z", "core")
    in_specs = (
        P(None, req),
        P(req),
        P(),
        P(),
        P(req, hist, None),
        P(req, hist, None),
        P(None, None, hist),
        P(None, None, hist),
        P(None, None, hist),
        P(None, hist),
    )
    return jax.shard_map(shards, mesh=split, in_specs=in_specs, out_specs=P(None, req, hist), check_vma=False)
```

```python
import functools
import math

import jax
import jax.numpy as jnp
from jax import lax
from jax.experimental import pallas as pl
from jax.experimental.pallas import tpu as pltpu
from jax.sharding import Mesh, PartitionSpec as P

KEY_HEADS = 8
HEAD = 128
STAT = 16
CHUNK = HEAD + STAT
DEAD = -1e30
EXP2_SCALE = HEAD ** (-0.5) * math.log2(math.e)
MIB = 1024 * 1024


def one_hot_rows(index_row, count):
    rows = index_row.shape[1]
    tall = jnp.transpose(jnp.broadcast_to(index_row, (128, rows)))
    parts = []
    for start in range(0, count, 128):
        lane = lax.broadcasted_iota(jnp.int32, (rows, 128), 1) + start
        parts.append((tall == lane).astype(jnp.float32).astype(jnp.bfloat16))
    return jnp.concatenate(parts, axis=1)


def residual_kernel(codes_ref, embed_hbm, out_ref, embed_ref, sem):
    copy = pltpu.make_async_copy(embed_hbm, embed_ref, sem.at[0])
    copy.start()
    beams = codes_ref.shape[1]
    hots = [one_hot_rows(codes_ref[level : level + 1], embed_ref.shape[1]) for level in range(codes_ref.shape[0])]
    copy.wait()
    for level, hot in enumerate(hots):
        out_ref[level * beams : (level + 1) * beams] = jnp.dot(
            hot, embed_ref[level], preferred_element_type=jnp.float32
        )


def look_kernel(codes_hbm, parents_hbm, query_hbm, out_ref, mine_ref, query_ref, sem):
    levels, beams = codes_hbm.shape
    copies = [
        pltpu.make_async_copy(codes_hbm, mine_ref.at[pl.ds(0, levels)], sem.at[0]),
        pltpu.make_async_copy(parents_hbm, mine_ref.at[pl.ds(levels, 1)], sem.at[1]),
        pltpu.make_async_copy(query_hbm, query_ref, sem.at[2]),
    ]
    for copy in copies:
        copy.start()
    copies[0].wait()
    copies[1].wait()
    hots = [one_hot_rows(mine_ref[level : level + 1], query_ref.shape[1]) for level in range(levels)]
    copies[2].wait()
    for level, hot in enumerate(hots):
        found = jnp.dot(hot, query_ref[level], preferred_element_type=jnp.float32).astype(jnp.bfloat16)
        for target in range(out_ref.shape[0]):
            out_ref[target, level * beams : (level + 1) * beams] = found


def generated_kernel(pair_ref, mine_ref, other_ref, kv_hbm, out_ref, kv_ref, sem):
    copy = pltpu.make_async_copy(kv_hbm, kv_ref, sem.at[0])
    copy.start()
    levels, beams = kv_ref.shape[0], mine_ref.shape[1]
    hots = [
        jnp.concatenate([one_hot_rows(ref[level : level + 1], kv_ref.shape[1]) for ref in (mine_ref, other_ref)])
        for level in range(levels)
    ]
    copy.wait()
    for level, hot in enumerate(hots):
        found = jnp.dot(hot, kv_ref[level], preferred_element_type=jnp.float32).astype(jnp.bfloat16)
        for part, x in enumerate((pair_ref[0], 1 - pair_ref[0])):
            place = pl.ds(pl.multiple_of((x * levels + level) * beams, beams), beams)
            out_ref[place] = found[part * beams : (part + 1) * beams]


def split3(value):
    high = value.astype(jnp.bfloat16).astype(jnp.float32)
    rest = value - high
    middle = rest.astype(jnp.bfloat16).astype(jnp.float32)
    return high, middle, rest - middle


def stat_rows(top, total):
    row = lax.broadcasted_iota(jnp.int32, (STAT, top.shape[1]), 0)
    out = jnp.zeros((STAT, top.shape[1]), jnp.float32)
    for at, piece in enumerate(split3(top) + split3(total)):
        out = jnp.where(row == at, piece, out)
    return out.astype(jnp.bfloat16)


def read_stats(rows):
    wide = rows.astype(jnp.float32)
    return wide[0:1] + wide[1:2] + wide[2:3], wide[3:4] + wide[4:5] + wide[5:6]


def scores_of(keys, rows):
    return lax.dot_general(keys, rows, (((1,), (1,)), ((), ())), preferred_element_type=jnp.float32)


def extended(values):
    return jnp.concatenate([jnp.transpose(values), jnp.ones((STAT, values.shape[0]), jnp.bfloat16)], axis=0)


def attend_kernel(
    meta_ref, lengths_ref, holders_ref, query_ref, near_key, near_value, far_key, far_value, kv_ref, far_kv_ref,
    gen_value_ref, mine_ref, other_ref, out_ref, score_ref, key_ref, value_ref, key_sem, value_sem,
):
    heads, slots = key_ref.shape[0], key_ref.shape[1]
    half = query_ref.shape[1]
    width = 4 * half
    request, place, gen_head = meta_ref[0], meta_ref[1], meta_ref[2]

    block_slots = slots // 2
    near, far = jnp.int32(0), jnp.int32(0)
    for block in range(holders_ref.shape[1]):
        holder = holders_ref[request, block]
        near = jnp.where(holder == place, block, near)
        far = jnp.where(holder == jnp.bitwise_xor(place, 1), block, far)
    near_live, far_live = (
        jnp.clip(lengths_ref[request] - each * block_slots, 0, block_slots) for each in (near, far)
    )
    live = near_live + far_live

    def queries(head):
        pieces = []
        for x in range(2):
            pair = query_ref[x * heads + head]
            pieces += [pair[:, h * HEAD : (h + 1) * HEAD] for h in range(2)]
        return jnp.concatenate(pieces, axis=0)

    def write(head, sums, total, top):
        for x in range(2):
            lanes = slice(x * 2 * half, (x + 1) * 2 * half)
            out_ref[x, head, 0:HEAD] = sums[:, lanes].astype(jnp.bfloat16)
            out_ref[x, head, HEAD:CHUNK] = stat_rows(top[:, lanes], total[:, lanes])

    def copies(head, keys):
        sources, target, sem = ((near_key, far_key), key_ref, key_sem) if keys else ((near_value, far_value), value_ref, value_sem)
        lanes = pl.ds(pl.multiple_of(head * HEAD, HEAD), HEAD)
        return [
            pltpu.make_async_copy(
                source.at[:, lanes], target.at[head, pl.ds(block * block_slots, block_slots)], sem.at[block * heads + head]
            )
            for block, source in enumerate(sources)
        ]

    def wait(head, keys):
        for copy in copies(head, keys):
            copy.wait()

    def attend(masked):
        def begin(head, _):
            for keys in (True, False):
                for copy in copies(head, keys):
                    copy.start()
            return 0

        lax.fori_loop(0, heads, begin, 0)

        def score(head, at):
            scores = scores_of(key_ref[head], queries(head))
            if masked:
                slot = lax.broadcasted_iota(jnp.int32, (slots, 1), 0)
                allowed = (slot < near_live) | ((slot >= block_slots) & (slot < block_slots + far_live))
                scores = jnp.where(allowed, scores, DEAD)
            score_ref[at] = scores
            return jnp.max(scores, axis=0, keepdims=True)

        def finish(head, at, top):
            weights = jnp.exp2((score_ref[at] - top) * EXP2_SCALE).astype(jnp.bfloat16)
            sums = jnp.dot(extended(value_ref[head]), weights, preferred_element_type=jnp.float32)
            write(head, sums[0:HEAD], sums[HEAD : HEAD + 1], top)

        def step(i, top):
            wait(2 * i + 1, True)
            wait(2 * i + 2, True)
            wait(2 * i, False)
            wait(2 * i + 1, False)
            later = score(2 * i + 1, 1)
            finish(2 * i, 0, top)
            top = score(2 * i + 2, 0)
            finish(2 * i + 1, 1, later)
            return top

        wait(0, True)
        top = lax.fori_loop(0, heads // 2 - 1, step, score(0, 0))
        wait(heads - 1, True)
        wait(heads - 2, False)
        wait(heads - 1, False)
        later = score(heads - 1, 1)
        finish(heads - 2, 0, top)
        finish(heads - 1, 1, later)

    @pl.when(live == slots)
    def _():
        attend(False)

    @pl.when((live > 0) & (live < slots))
    def _():
        attend(True)

    @pl.when(live == 0)
    def _():
        row = lax.broadcasted_iota(jnp.int32, (CHUNK, 2 * half), 0)
        tops = split3(jnp.full((CHUNK, 2 * half), DEAD, jnp.float32))
        dead = jnp.zeros((CHUNK, 2 * half), jnp.float32)
        for at, piece in enumerate(tops):
            dead = jnp.where(row == HEAD + at, piece, dead)
        dead = dead.astype(jnp.bfloat16)
        for x in range(2):
            for head in range(heads):
                out_ref[x, head] = dead

    @pl.when(gen_head >= 0)
    def _():
        values = extended(gen_value_ref[...])
        row = lax.broadcasted_iota(jnp.int32, (2 * half, width), 0)
        lane = lax.broadcasted_iota(jnp.int32, (2 * half, width), 1)
        own = (lane // (2 * half)) * half + lane % half
        beams = mine_ref.shape[1]
        swapped = meta_ref[3] != 0
        mine, other = (ref[mine_ref.shape[0] - 1 :] for ref in (mine_ref, other_ref))
        pieces = []
        for parents in (jnp.where(swapped, other, mine), jnp.where(swapped, mine, other)):
            parents = (parents // beams) * half + parents % beams
            pieces += [jnp.full_like(parents, -1), parents] * 2
        allowed = (row == own) | (row == jnp.concatenate(pieces, axis=1))
        keys = jnp.where(swapped, far_kv_ref[...], kv_ref[...])
        scores = jnp.where(allowed, scores_of(keys, queries(gen_head)), DEAD)
        before = jnp.concatenate([out_ref[x, gen_head] for x in range(2)], axis=1)
        old_top, old_total = read_stats(before[HEAD:CHUNK])
        top = jnp.maximum(old_top, jnp.max(scores, axis=0, keepdims=True))
        weights = jnp.where(allowed, jnp.exp2((scores - top) * EXP2_SCALE), 0.0)
        high = weights.astype(jnp.bfloat16)
        low = (weights - high.astype(jnp.float32)).astype(jnp.bfloat16)
        added = jnp.dot(values, high, preferred_element_type=jnp.float32)
        added = added + jnp.dot(values, low, preferred_element_type=jnp.float32)
        factor = jnp.exp2((old_top - top) * EXP2_SCALE)
        sums = before[0:HEAD].astype(jnp.float32) * factor + added[0:HEAD]
        write(gen_head, sums, old_total * factor + added[HEAD : HEAD + 1], top)


def combine_kernel(parts_ref, out_ref):
    count = parts_ref.shape[0]
    stats = [read_stats(parts_ref[part, HEAD:CHUNK]) for part in range(count)]
    top = functools.reduce(jnp.maximum, [each for each, _ in stats])
    total = jnp.zeros_like(top)
    sums = jnp.zeros((HEAD, parts_ref.shape[2]), jnp.float32)
    for part in range(count):
        factor = jnp.exp2((stats[part][0] - top) * EXP2_SCALE)
        total = total + stats[part][1] * factor
        sums = sums + parts_ref[part, 0:HEAD].astype(jnp.float32) * factor
    tall = jnp.transpose(sums / total)
    rows = out_ref.shape[0]
    out_ref[...] = jnp.concatenate([tall[0:rows], tall[rows : 2 * rows]], axis=1).astype(jnp.bfloat16)


def project_kernel(rows_ref, weight_ref, residual_ref, out_ref):
    total = residual_ref[...]
    for part in range(rows_ref.shape[0]):
        total = total + jnp.dot(rows_ref[part], weight_ref[part], preferred_element_type=jnp.float32)
    out_ref[...] = total.astype(out_ref.dtype)


def call(kernel, out_shape, name, spaces, vmem, **rest):
    kinds = {"s": pltpu.SMEM, "v": pltpu.VMEM, "h": pltpu.HBM, "a": pl.ANY}
    return pl.pallas_call(
        kernel,
        out_shape=out_shape,
        in_specs=[pl.BlockSpec(memory_space=kinds[space]) for space in spaces],
        out_specs=jax.tree.map(lambda _: pl.BlockSpec(memory_space=pltpu.VMEM), out_shape),
        compiler_params=pltpu.CompilerParams(vmem_limit_bytes=vmem * MIB),
        name=name,
        **rest,
    )


def shards(
    codes, parents, lengths, holders, history_keys, history_values, query_table, kv_table, embed_table, out_weight
):
    beams = parents.shape[0]
    levels, code_count, width = query_table.shape
    half = levels * beams
    rows = 2 * half
    slots = history_keys.shape[1]
    z_count = lax.axis_size("z")
    pair, z, core = lax.axis_index("pair"), lax.axis_index("z"), lax.axis_index("core")
    hist = 2 * z + core
    bf16, f32 = jnp.bfloat16, jnp.float32
    array = jax.ShapeDtypeStruct
    dma = pltpu.SemaphoreType.DMA
    swap = [(0, 1), (1, 0)]

    hbm = lambda x: pltpu.with_memory_space_constraint(x, pltpu.HBM)

    query_rows, mine = call(
        look_kernel,
        (array((2 * z_count, half, width), bf16), array((levels + 1, beams), jnp.int32)),
        "look",
        "hhh",
        4,
        scratch_shapes=[pltpu.VMEM(query_table.shape, bf16), dma((3,))],
    )(hbm(codes), hbm(parents[None]), hbm(query_table))
    queries = lax.all_to_all(query_rows, ("pair", "z"), split_axis=0, concat_axis=0, tiled=True)
    residual = call(
        residual_kernel,
        array((half, width), f32),
        "residual",
        "vh",
        4,
        scratch_shapes=[pltpu.VMEM(embed_table.shape, bf16), dma((1,))],
    )(codes, hbm(embed_table))

    mine, near_keys, near_values = lax.optimization_barrier((mine, history_keys[0], history_values[0]))
    other = lax.ppermute(mine, "pair", swap)
    far_keys = lax.ppermute(near_keys, "core", swap)
    far_values = lax.ppermute(near_values, "core", swap)
    kv_rows = call(
        generated_kernel,
        array((rows, HEAD), bf16),
        "generated",
        "svvh",
        4,
        scratch_shapes=[pltpu.VMEM(kv_table.shape, bf16), dma((1,))],
    )(pair.reshape(1), mine, other, hbm(kv_table))
    at = lambda p, k, c: (p * z_count + k) * 2 + c
    taken = [(p, k, c) for p in range(2) for k in range(z_count // 2) for c in range(2)]
    gen_values = lax.ppermute(
        kv_rows, ("pair", "z", "core"), [(at(p, k + z_count // 2, c ^ p), at(p, k, c)) for p, k, c in taken]
    )
    far_kv = lax.ppermute(kv_rows, ("pair", "z", "core"), [(at(1, k, 1 - c), at(1, k, c)) for p, k, c in taken if p])

    gen_head = jnp.where(z < z_count // 2, 2 * z + jnp.bitwise_xor(core, pair), -1)
    meta = jnp.stack([lax.axis_index("grp"), pair * 2 * z_count + hist, gen_head, pair]).astype(jnp.int32)
    partials = call(
        attend_kernel,
        array((2, z_count, CHUNK, 2 * half), bf16),
        "attend",
        "sssvhhaavvvvv",
        24,
        scratch_shapes=[
            pltpu.VMEM((2, 2 * slots, 2 * rows), f32),
            pltpu.VMEM((KEY_HEADS, 2 * slots, HEAD), bf16),
            pltpu.VMEM((KEY_HEADS, 2 * slots, HEAD), bf16),
            dma((2 * KEY_HEADS,)),
            dma((2 * KEY_HEADS,)),
        ],
        cost_estimate=pl.CostEstimate(
            flops=4 * 4 * rows * KEY_HEADS * slots * HEAD,
            bytes_accessed=4 * slots * KEY_HEADS * HEAD,
            transcendentals=4 * rows * KEY_HEADS * slots,
        ),
    )(
        *(meta, lengths, holders, queries),
        *(hbm(near_keys), hbm(near_values), far_keys, far_values),
        *(kv_rows, far_kv, gen_values, mine, other),
    )

    shape = (2 * z_count, CHUNK, 2 * half)
    parts = lax.all_to_all(partials.reshape(shape), ("pair", "z"), split_axis=0, concat_axis=0, tiled=True)
    attention = call(combine_kernel, array((half, width), bf16), "combine", "v", 4)(parts)
    gathered = lax.all_gather(attention, ("z", "core"), axis=0)
    out = call(project_kernel, array((half, width), bf16), "project", "vvv", 4)(
        gathered, out_weight.reshape(2 * z_count, width, width), residual
    )
    return out.reshape(levels, beams, width)


def solution(mesh):
    split = Mesh(mesh.devices.reshape(16, 2, 8, 2), ("grp", "pair", "z", "core"))
    req, hist = ("grp", "pair"), ("z", "core")
    in_specs = (
        P(None, req),
        P(req),
        P(),
        P(),
        P(req, hist, None),
        P(req, hist, None),
        P(None, None, hist),
        P(None, None, hist),
        P(None, None, hist),
        P(None, hist),
    )
    return jax.shard_map(shards, mesh=split, in_specs=in_specs, out_specs=P(None, req, hist), check_vma=False)
```

```python
import functools
import math

import jax
import jax.numpy as jnp
from jax import lax
from jax.experimental import pallas as pl
from jax.experimental.pallas import tpu as pltpu
from jax.sharding import Mesh, PartitionSpec as P

KEY_HEADS = 8
HEAD = 128
STAT = 16
CHUNK = HEAD + STAT
DEAD = -1e30
EXP2_SCALE = HEAD ** (-0.5) * math.log2(math.e)
MIB = 1024 * 1024


def one_hot_rows(index_row, count):
    rows = index_row.shape[1]
    tall = jnp.transpose(jnp.broadcast_to(index_row, (128, rows)))
    parts = []
    for start in range(0, count, 128):
        lane = lax.broadcasted_iota(jnp.int32, (rows, 128), 1) + start
        parts.append((tall == lane).astype(jnp.float32).astype(jnp.bfloat16))
    return jnp.concatenate(parts, axis=1)


def residual_kernel(codes_ref, embed_hbm, out_ref, embed_ref, sem):
    copy = pltpu.make_async_copy(embed_hbm, embed_ref, sem.at[0])
    copy.start()
    beams = codes_ref.shape[1]
    hots = [one_hot_rows(codes_ref[level : level + 1], embed_ref.shape[1]) for level in range(codes_ref.shape[0])]
    copy.wait()
    for level, hot in enumerate(hots):
        out_ref[level * beams : (level + 1) * beams] = jnp.dot(
            hot, embed_ref[level], preferred_element_type=jnp.float32
        )


def look_kernel(codes_hbm, parents_hbm, query_hbm, out_ref, mine_ref, query_ref, sem):
    levels, beams = codes_hbm.shape
    copies = [
        pltpu.make_async_copy(codes_hbm, mine_ref.at[pl.ds(0, levels)], sem.at[0]),
        pltpu.make_async_copy(parents_hbm, mine_ref.at[pl.ds(levels, 1)], sem.at[1]),
        pltpu.make_async_copy(query_hbm, query_ref, sem.at[2]),
    ]
    for copy in copies:
        copy.start()
    copies[0].wait()
    copies[1].wait()
    hots = [one_hot_rows(mine_ref[level : level + 1], query_ref.shape[1]) for level in range(levels)]
    copies[2].wait()
    for level, hot in enumerate(hots):
        found = jnp.dot(hot, query_ref[level], preferred_element_type=jnp.float32).astype(jnp.bfloat16)
        for target in range(out_ref.shape[0]):
            out_ref[target, level * beams : (level + 1) * beams] = found


def generated_kernel(
    meta_ref, mine_ref, other_ref, kv_hbm, lengths_hbm, holders_hbm, out_ref, live_ref, kv_ref, lengths_ref, holders_ref, sem
):
    copies = [
        pltpu.make_async_copy(lengths_hbm, lengths_ref, sem.at[0]),
        pltpu.make_async_copy(holders_hbm, holders_ref, sem.at[1]),
        pltpu.make_async_copy(kv_hbm, kv_ref, sem.at[2]),
    ]
    for copy in copies:
        copy.start()
    levels, beams = kv_ref.shape[0], mine_ref.shape[1]
    hots = [
        jnp.concatenate([one_hot_rows(ref[level : level + 1], kv_ref.shape[1]) for ref in (mine_ref, other_ref)])
        for level in range(levels)
    ]
    for copy in copies:
        copy.wait()
    for level, hot in enumerate(hots):
        found = jnp.dot(hot, kv_ref[level], preferred_element_type=jnp.float32).astype(jnp.bfloat16)
        for part, x in enumerate((meta_ref[3], 1 - meta_ref[3])):
            place = pl.ds(pl.multiple_of((x * levels + level) * beams, beams), beams)
            out_ref[place] = found[part * beams : (part + 1) * beams]
    request, place, block_slots = meta_ref[0], meta_ref[1], meta_ref[4]
    near, far = jnp.int32(0), jnp.int32(0)
    for block in range(holders_ref.shape[1]):
        holder = holders_ref[request, block]
        near = jnp.where(holder == place, block, near)
        far = jnp.where(holder == jnp.bitwise_xor(place, 1), block, far)
    for at, position in enumerate((near, far)):
        live_ref[at] = jnp.clip(lengths_ref[request] - position * block_slots, 0, block_slots)


def split3(value):
    high = value.astype(jnp.bfloat16).astype(jnp.float32)
    rest = value - high
    middle = rest.astype(jnp.bfloat16).astype(jnp.float32)
    return high, middle, rest - middle


def stat_rows(top, total):
    row = lax.broadcasted_iota(jnp.int32, (STAT, top.shape[1]), 0)
    out = jnp.zeros((STAT, top.shape[1]), jnp.float32)
    for at, piece in enumerate(split3(top) + split3(total)):
        out = jnp.where(row == at, piece, out)
    return out.astype(jnp.bfloat16)


def read_stats(rows):
    wide = rows.astype(jnp.float32)
    return wide[0:1] + wide[1:2] + wide[2:3], wide[3:4] + wide[4:5] + wide[5:6]


def scores_of(keys, rows):
    return lax.dot_general(keys, rows, (((1,), (1,)), ((), ())), preferred_element_type=jnp.float32)


def extended(values):
    return jnp.concatenate([jnp.transpose(values), jnp.ones((STAT, values.shape[0]), jnp.bfloat16)], axis=0)


def queries_of(query_ref, head):
    pieces = []
    for x in range(2):
        pair = query_ref[x * KEY_HEADS + head]
        pieces += [pair[:, h * HEAD : (h + 1) * HEAD] for h in range(2)]
    return jnp.concatenate(pieces, axis=0)


def write(out_ref, head, sums, total, top):
    width = sums.shape[1] // 2
    for x in range(2):
        lanes = slice(x * width, (x + 1) * width)
        out_ref[x, head, 0:HEAD] = sums[:, lanes].astype(jnp.bfloat16)
        out_ref[x, head, HEAD:CHUNK] = stat_rows(top[:, lanes], total[:, lanes])


def attend_kernel(
    live_ref, query_ref, near_key, near_value, far_key, far_value, out_ref, score_ref, key_ref, value_ref, key_sem, value_sem
):
    heads, slots = key_ref.shape[0], key_ref.shape[1]
    half = query_ref.shape[1]
    block_slots = slots // 2
    near_live, far_live = live_ref[0], live_ref[1]
    live = near_live + far_live

    def copies(head, keys):
        sources, target, sem = ((near_key, far_key), key_ref, key_sem) if keys else ((near_value, far_value), value_ref, value_sem)
        lanes = pl.ds(pl.multiple_of(head * HEAD, HEAD), HEAD)
        return [
            pltpu.make_async_copy(
                source.at[:, lanes], target.at[head, pl.ds(block * block_slots, block_slots)], sem.at[block * heads + head]
            )
            for block, source in enumerate(sources)
        ]

    def wait(head, keys):
        for copy in copies(head, keys):
            copy.wait()

    def attend(masked):
        def begin(head, _):
            for keys in (True, False):
                for copy in copies(head, keys):
                    copy.start()
            return 0

        lax.fori_loop(0, heads, begin, 0)

        def score(head, at):
            scores = scores_of(key_ref[head], queries_of(query_ref, head))
            if masked:
                slot = lax.broadcasted_iota(jnp.int32, (slots, 1), 0)
                allowed = (slot < near_live) | ((slot >= block_slots) & (slot < block_slots + far_live))
                scores = jnp.where(allowed, scores, DEAD)
            score_ref[at] = scores
            return jnp.max(scores, axis=0, keepdims=True)

        def finish(head, at, top):
            weights = jnp.exp2((score_ref[at] - top) * EXP2_SCALE).astype(jnp.bfloat16)
            sums = jnp.dot(extended(value_ref[head]), weights, preferred_element_type=jnp.float32)
            write(out_ref, head, sums[0:HEAD], sums[HEAD : HEAD + 1], top)

        def step(i, top):
            wait(2 * i + 1, True)
            wait(2 * i + 2, True)
            wait(2 * i, False)
            wait(2 * i + 1, False)
            later = score(2 * i + 1, 1)
            finish(2 * i, 0, top)
            top = score(2 * i + 2, 0)
            finish(2 * i + 1, 1, later)
            return top

        wait(0, True)
        top = lax.fori_loop(0, heads // 2 - 1, step, score(0, 0))
        wait(heads - 1, True)
        wait(heads - 2, False)
        wait(heads - 1, False)
        later = score(heads - 1, 1)
        finish(heads - 2, 0, top)
        finish(heads - 1, 1, later)

    @pl.when(live == slots)
    def _():
        attend(False)

    @pl.when((live > 0) & (live < slots))
    def _():
        attend(True)

    @pl.when(live == 0)
    def _():
        row = lax.broadcasted_iota(jnp.int32, (CHUNK, 2 * half), 0)
        tops = split3(jnp.full((CHUNK, 2 * half), DEAD, jnp.float32))
        dead = jnp.zeros((CHUNK, 2 * half), jnp.float32)
        for at, piece in enumerate(tops):
            dead = jnp.where(row == HEAD + at, piece, dead)
        dead = dead.astype(jnp.bfloat16)
        for x in range(2):
            for head in range(heads):
                out_ref[x, head] = dead


def add_generated_kernel(
    meta_ref, query_ref, kv_ref, far_kv_ref, gen_value_ref, mine_ref, other_ref, before_ref, out_ref
):
    half = query_ref.shape[1]
    width = 4 * half
    head = meta_ref[2]

    @pl.when(head >= 0)
    def _():
        values = extended(gen_value_ref[...])
        row = lax.broadcasted_iota(jnp.int32, (2 * half, width), 0)
        lane = lax.broadcasted_iota(jnp.int32, (2 * half, width), 1)
        own = (lane // (2 * half)) * half + lane % half
        beams = mine_ref.shape[1]
        swapped = meta_ref[3] != 0
        mine, other = (ref[mine_ref.shape[0] - 1 :] for ref in (mine_ref, other_ref))
        pieces = []
        for parents in (jnp.where(swapped, other, mine), jnp.where(swapped, mine, other)):
            parents = (parents // beams) * half + parents % beams
            pieces += [jnp.full_like(parents, -1), parents] * 2
        allowed = (row == own) | (row == jnp.concatenate(pieces, axis=1))
        keys = jnp.where(swapped, far_kv_ref[...], kv_ref[...])
        scores = jnp.where(allowed, scores_of(keys, queries_of(query_ref, head)), DEAD)
        before = jnp.concatenate([before_ref[x, head] for x in range(2)], axis=1)
        old_top, old_total = read_stats(before[HEAD:CHUNK])
        top = jnp.maximum(old_top, jnp.max(scores, axis=0, keepdims=True))
        weights = jnp.where(allowed, jnp.exp2((scores - top) * EXP2_SCALE), 0.0)
        high = weights.astype(jnp.bfloat16)
        low = (weights - high.astype(jnp.float32)).astype(jnp.bfloat16)
        added = jnp.dot(values, high, preferred_element_type=jnp.float32)
        added = added + jnp.dot(values, low, preferred_element_type=jnp.float32)
        factor = jnp.exp2((old_top - top) * EXP2_SCALE)
        sums = before[0:HEAD].astype(jnp.float32) * factor + added[0:HEAD]
        write(out_ref, head, sums, old_total * factor + added[HEAD : HEAD + 1], top)


def combine_kernel(parts_ref, out_ref):
    count = parts_ref.shape[0]
    stats = [read_stats(parts_ref[part, HEAD:CHUNK]) for part in range(count)]
    top = functools.reduce(jnp.maximum, [each for each, _ in stats])
    total = jnp.zeros_like(top)
    sums = jnp.zeros((HEAD, parts_ref.shape[2]), jnp.float32)
    for part in range(count):
        factor = jnp.exp2((stats[part][0] - top) * EXP2_SCALE)
        total = total + stats[part][1] * factor
        sums = sums + parts_ref[part, 0:HEAD].astype(jnp.float32) * factor
    tall = jnp.transpose(sums / total)
    rows = out_ref.shape[1]
    found = jnp.concatenate([tall[0:rows], tall[rows : 2 * rows]], axis=1).astype(jnp.bfloat16)
    for target in range(out_ref.shape[0]):
        out_ref[target] = found


def project_kernel(flip, meta_ref, rows_ref, weight_ref, before_ref, out_ref):
    total = before_ref[...]
    parity = jnp.bitwise_xor(jnp.bitwise_and(meta_ref[1], 1), flip)
    for part in range(rows_ref.shape[0]):
        total = total + jnp.dot(rows_ref[part], weight_ref[part, parity], preferred_element_type=jnp.float32)
    out_ref[...] = total.astype(out_ref.dtype)


def call(kernel, out_shape, name, spaces, vmem, out_spaces="v", **rest):
    kinds = {"s": pltpu.SMEM, "v": pltpu.VMEM, "h": pltpu.HBM, "a": pl.ANY}
    specs = lambda letters: [pl.BlockSpec(memory_space=kinds[letter]) for letter in letters]
    return pl.pallas_call(
        kernel,
        out_shape=out_shape,
        in_specs=specs(spaces),
        out_specs=specs(out_spaces) if len(out_spaces) > 1 else specs(out_spaces)[0],
        compiler_params=pltpu.CompilerParams(vmem_limit_bytes=vmem * MIB),
        name=name,
        **rest,
    )


def shards(
    codes, parents, lengths, holders, history_keys, history_values, query_table, kv_table, embed_table, out_weight
):
    beams = parents.shape[0]
    levels, code_count, width = query_table.shape
    half = levels * beams
    rows = 2 * half
    slots = history_keys.shape[1]
    z_count = lax.axis_size("z")
    pair, z, core = lax.axis_index("pair"), lax.axis_index("z"), lax.axis_index("core")
    hist = 2 * z + core
    bf16, f32 = jnp.bfloat16, jnp.float32
    array = jax.ShapeDtypeStruct
    dma = pltpu.SemaphoreType.DMA
    swap = [(0, 1), (1, 0)]

    hbm = lambda x: pltpu.with_memory_space_constraint(x, pltpu.HBM)

    query_rows, mine = call(
        look_kernel,
        (array((2 * z_count, half, width), bf16), array((levels + 1, beams), jnp.int32)),
        "look",
        "hhh",
        4,
        "vv",
        scratch_shapes=[pltpu.VMEM(query_table.shape, bf16), dma((3,))],
    )(hbm(codes), hbm(parents[None]), hbm(query_table))
    queries = lax.all_to_all(query_rows, ("pair", "z"), split_axis=0, concat_axis=0, tiled=True)
    residual = call(
        residual_kernel,
        array((half, width), f32),
        "residual",
        "vh",
        4,
        scratch_shapes=[pltpu.VMEM(embed_table.shape, bf16), dma((1,))],
    )(codes, hbm(embed_table))

    mine, near_keys, near_values = lax.optimization_barrier((mine, history_keys[0], history_values[0]))
    other = lax.ppermute(mine, "pair", swap)
    far_keys = lax.ppermute(near_keys, "core", swap)
    far_values = lax.ppermute(near_values, "core", swap)
    gen_head = jnp.where(z < z_count // 2, 2 * z + jnp.bitwise_xor(core, pair), -1)
    meta = jnp.stack([lax.axis_index("grp"), pair * 2 * z_count + hist, gen_head, pair, jnp.int32(slots)]).astype(jnp.int32)
    kv_rows, live = call(
        generated_kernel,
        (array((rows, HEAD), bf16), array((2,), jnp.int32)),
        "generated",
        "svvhhh",
        4,
        "vs",
        scratch_shapes=[
            pltpu.VMEM(kv_table.shape, bf16),
            pltpu.SMEM(lengths.shape, jnp.int32),
            pltpu.SMEM(holders.shape, jnp.int32),
            dma((3,)),
        ],
    )(meta, mine, other, hbm(kv_table), hbm(lengths), hbm(holders))
    at = lambda p, k, c: (p * z_count + k) * 2 + c
    taken = [(p, k, c) for p in range(2) for k in range(z_count // 2) for c in range(2)]
    gen_values = lax.ppermute(
        kv_rows, ("pair", "z", "core"), [(at(p, k + z_count // 2, c ^ p), at(p, k, c)) for p, k, c in taken]
    )
    far_kv = lax.ppermute(kv_rows, ("pair", "z", "core"), [(at(1, k, 1 - c), at(1, k, c)) for p, k, c in taken if p])

    partial_shape = (2, z_count, CHUNK, 2 * half)
    partials = call(
        attend_kernel,
        array(partial_shape, bf16),
        "attend",
        "svhhaa",
        24,
        scratch_shapes=[
            pltpu.VMEM((2, 2 * slots, 2 * rows), f32),
            pltpu.VMEM((KEY_HEADS, 2 * slots, HEAD), bf16),
            pltpu.VMEM((KEY_HEADS, 2 * slots, HEAD), bf16),
            dma((2 * KEY_HEADS,)),
            dma((2 * KEY_HEADS,)),
        ],
        cost_estimate=pl.CostEstimate(
            flops=4 * 4 * rows * KEY_HEADS * slots * HEAD,
            bytes_accessed=4 * slots * KEY_HEADS * HEAD,
            transcendentals=4 * rows * KEY_HEADS * slots,
        ),
    )(live, queries, hbm(near_keys), hbm(near_values), far_keys, far_values)
    partials = call(
        add_generated_kernel, array(partial_shape, bf16), "add_generated", "svvvvvvv", 4, input_output_aliases={7: 0}
    )(meta, queries, kv_rows, far_kv, gen_values, mine, other, partials)

    shape = (2 * z_count, CHUNK, 2 * half)
    parts = lax.all_to_all(partials.reshape(shape), ("pair", "z"), split_axis=0, concat_axis=0, tiled=True)
    attention = call(combine_kernel, array((z_count, half, width), bf16), "combine", "v", 4)(parts)
    near_rows = lax.all_to_all(attention, "z", split_axis=0, concat_axis=0, tiled=True)
    far_rows = lax.ppermute(near_rows, "core", swap)
    weight = out_weight.reshape(z_count, 2, width, width)
    begun = call(functools.partial(project_kernel, 0), array((half, width), f32), "project_near", "svvv", 4)(
        meta, near_rows, weight, residual
    )
    out = call(functools.partial(project_kernel, 1), array((half, width), bf16), "project_far", "svvv", 4)(
        meta, far_rows, weight, begun
    )
    return out.reshape(levels, beams, width)


def solution(mesh):
    split = Mesh(mesh.devices.reshape(16, 2, 8, 2), ("grp", "pair", "z", "core"))
    req, hist = ("grp", "pair"), ("z", "core")
    in_specs = (
        P(None, req),
        P(req),
        P(),
        P(),
        P(req, hist, None),
        P(req, hist, None),
        P(None, None, hist),
        P(None, None, hist),
        P(None, None, hist),
        P(None, hist),
    )
    return jax.shard_map(shards, mesh=split, in_specs=in_specs, out_specs=P(None, req, hist), check_vma=False)
```

```python
import functools
import math

import jax
import jax.numpy as jnp
from jax import lax
from jax.experimental import pallas as pl
from jax.experimental.pallas import tpu as pltpu
from jax.sharding import Mesh, PartitionSpec as P

KEY_HEADS = 8
HEAD = 128
STAT = 16
CHUNK = HEAD + STAT
DEAD = -1e30
EXP2_SCALE = HEAD ** (-0.5) * math.log2(math.e)
MIB = 1024 * 1024


def one_hot_rows(index_row, count):
    rows = index_row.shape[1]
    tall = jnp.transpose(jnp.broadcast_to(index_row, (128, rows)))
    parts = []
    for start in range(0, count, 128):
        lane = lax.broadcasted_iota(jnp.int32, (rows, 128), 1) + start
        parts.append((tall == lane).astype(jnp.float32).astype(jnp.bfloat16))
    return jnp.concatenate(parts, axis=1)


def look_kernel(codes_hbm, parents_hbm, query_hbm, out_ref, own_ref, mine_ref, query_ref, sem):
    levels, beams = codes_hbm.shape
    copies = [
        pltpu.make_async_copy(codes_hbm, mine_ref.at[pl.ds(0, levels)], sem.at[0]),
        pltpu.make_async_copy(parents_hbm, mine_ref.at[pl.ds(levels, 1)], sem.at[1]),
        pltpu.make_async_copy(query_hbm, query_ref, sem.at[2]),
    ]
    for copy in copies:
        copy.start()
    copies[0].wait()
    copies[1].wait()
    hots = [one_hot_rows(mine_ref[level : level + 1], query_ref.shape[1]) for level in range(levels)]
    copies[2].wait()
    for level, hot in enumerate(hots):
        found = jnp.dot(hot, query_ref[level], preferred_element_type=jnp.float32).astype(jnp.bfloat16)
        own_ref[level * beams : (level + 1) * beams] = found
        for target in range(out_ref.shape[0]):
            out_ref[target, level * beams : (level + 1) * beams] = found


def generated_kernel(
    meta_ref, mine_ref, other_ref, kv_hbm, embed_hbm, lengths_hbm, holders_hbm, out_ref, residual_ref, live_ref,
    kv_ref, embed_ref, lengths_ref, holders_ref, sem
):
    copies = [
        pltpu.make_async_copy(lengths_hbm, lengths_ref, sem.at[0]),
        pltpu.make_async_copy(holders_hbm, holders_ref, sem.at[1]),
        pltpu.make_async_copy(kv_hbm, kv_ref, sem.at[2]),
        pltpu.make_async_copy(embed_hbm, embed_ref, sem.at[3]),
    ]
    for copy in copies:
        copy.start()
    levels, beams = kv_ref.shape[0], mine_ref.shape[1]
    hots = [
        jnp.concatenate([one_hot_rows(ref[level : level + 1], kv_ref.shape[1]) for ref in (mine_ref, other_ref)])
        for level in range(levels)
    ]
    for copy in copies:
        copy.wait()
    for level, hot in enumerate(hots):
        found = jnp.dot(hot, kv_ref[level], preferred_element_type=jnp.float32).astype(jnp.bfloat16)
        residual_ref[level * beams : (level + 1) * beams] = jnp.dot(
            hot[:beams], embed_ref[level], preferred_element_type=jnp.float32
        )
        for part, x in enumerate((meta_ref[2], 1 - meta_ref[2])):
            place = pl.ds(pl.multiple_of((x * levels + level) * beams, beams), beams)
            out_ref[place] = found[part * beams : (part + 1) * beams]
    request, place, block_slots = meta_ref[0], meta_ref[1], meta_ref[3]
    near, far = jnp.int32(0), jnp.int32(0)
    for block in range(holders_ref.shape[1]):
        holder = holders_ref[request, block]
        near = jnp.where(holder == place, block, near)
        far = jnp.where(holder == jnp.bitwise_xor(place, 1), block, far)
    for at, position in enumerate((near, far)):
        live_ref[at] = jnp.clip(lengths_ref[request] - position * block_slots, 0, block_slots)


def split3(value):
    high = value.astype(jnp.bfloat16).astype(jnp.float32)
    rest = value - high
    middle = rest.astype(jnp.bfloat16).astype(jnp.float32)
    return high, middle, rest - middle


def stat_rows(top, total):
    row = lax.broadcasted_iota(jnp.int32, (STAT, top.shape[1]), 0)
    out = jnp.zeros((STAT, top.shape[1]), jnp.float32)
    for at, piece in enumerate(split3(top) + split3(total)):
        out = jnp.where(row == at, piece, out)
    return out.astype(jnp.bfloat16)


def read_stats(rows):
    wide = rows.astype(jnp.float32)
    return wide[0:1] + wide[1:2] + wide[2:3], wide[3:4] + wide[4:5] + wide[5:6]


def scores_of(keys, rows):
    return lax.dot_general(keys, rows, (((1,), (1,)), ((), ())), preferred_element_type=jnp.float32)


def extended(values):
    return jnp.concatenate([jnp.transpose(values), jnp.ones((STAT, values.shape[0]), jnp.bfloat16)], axis=0)


def query_rows_of(pair):
    return jnp.concatenate([pair[:, h * HEAD : (h + 1) * HEAD] for h in range(2)], axis=0)


def attend_kernel(
    flip, meta_ref, live_ref, query_ref, near_key, near_value, far_key, far_value,
    out_ref, score_ref, key_ref, value_ref, key_sem, value_sem
):
    heads, slots, pair_lanes = key_ref.shape
    block_slots = slots // 2
    near_live, far_live = live_ref[0], live_ref[1]
    live = near_live + far_live
    first = jnp.bitwise_xor(meta_ref[2], flip) * 2 * heads

    def queries(head):
        pieces = []
        for part in range(2):
            rows = query_rows_of(query_ref[first + 2 * head + part])
            blank = jnp.zeros_like(rows)
            pieces.append(jnp.concatenate([blank, rows] if part else [rows, blank], axis=1))
        return jnp.concatenate(pieces, axis=0)

    def write(head, sums, top):
        width = sums.shape[1] // 2
        for part in range(2):
            lanes = slice(part * width, (part + 1) * width)
            out_ref[2 * head + part, 0:HEAD] = sums[part * HEAD : (part + 1) * HEAD, lanes].astype(jnp.bfloat16)
            out_ref[2 * head + part, HEAD:CHUNK] = stat_rows(top[:, lanes], sums[2 * HEAD : 2 * HEAD + 1, lanes])

    def copies(head, keys):
        sources, target, sem = ((near_key, far_key), key_ref, key_sem) if keys else ((near_value, far_value), value_ref, value_sem)
        lanes = pl.ds(pl.multiple_of(head * pair_lanes, pair_lanes), pair_lanes)
        return [
            pltpu.make_async_copy(
                source.at[:, lanes], target.at[head, pl.ds(block * block_slots, block_slots)], sem.at[block * heads + head]
            )
            for block, source in enumerate(sources)
        ]

    def wait(head, keys):
        for copy in copies(head, keys):
            copy.wait()

    def attend(masked):
        def begin(head, _):
            for keys in (True, False):
                for copy in copies(head, keys):
                    copy.start()
            return 0

        lax.fori_loop(0, heads, begin, 0)

        def score(head, at):
            scores = scores_of(key_ref[head], queries(head))
            if masked:
                slot = lax.broadcasted_iota(jnp.int32, (slots, 1), 0)
                allowed = (slot < near_live) | ((slot >= block_slots) & (slot < block_slots + far_live))
                scores = jnp.where(allowed, scores, DEAD)
            score_ref[at] = scores
            return jnp.max(scores, axis=0, keepdims=True)

        def finish(head, at, top):
            weights = jnp.exp2((score_ref[at] - top) * EXP2_SCALE).astype(jnp.bfloat16)
            sums = jnp.dot(extended(value_ref[head]), weights, preferred_element_type=jnp.float32)
            write(head, sums, top)

        def step(i, top):
            wait(2 * i + 1, True)
            wait(2 * i + 2, True)
            wait(2 * i, False)
            wait(2 * i + 1, False)
            later = score(2 * i + 1, 1)
            finish(2 * i, 0, top)
            top = score(2 * i + 2, 0)
            finish(2 * i + 1, 1, later)
            return top

        wait(0, True)
        top = lax.fori_loop(0, heads // 2 - 1, step, score(0, 0))
        wait(heads - 1, True)
        wait(heads - 2, False)
        wait(heads - 1, False)
        later = score(heads - 1, 1)
        finish(heads - 2, 0, top)
        finish(heads - 1, 1, later)

    @pl.when(live == slots)
    def _():
        attend(False)

    @pl.when((live > 0) & (live < slots))
    def _():
        attend(True)

    @pl.when(live == 0)
    def _():
        row = lax.broadcasted_iota(jnp.int32, out_ref.shape[1:], 0)
        dead = jnp.zeros(out_ref.shape[1:], jnp.float32)
        for at, piece in enumerate(split3(jnp.full(out_ref.shape[1:], DEAD, jnp.float32))):
            dead = jnp.where(row == HEAD + at, piece, dead)
        for head in range(out_ref.shape[0]):
            out_ref[head] = dead.astype(jnp.bfloat16)


def merge_kernel(mine_ref, other_ref, out_ref):
    for chunk in range(mine_ref.shape[0]):
        tops, totals = zip(*(read_stats(ref[chunk, HEAD:CHUNK]) for ref in (mine_ref, other_ref)))
        top = jnp.maximum(*tops)
        factors = [jnp.exp2((each - top) * EXP2_SCALE) for each in tops]
        total = totals[0] * factors[0] + totals[1] * factors[1]
        sums = (
            mine_ref[chunk, 0:HEAD].astype(jnp.float32) * factors[0]
            + other_ref[chunk, 0:HEAD].astype(jnp.float32) * factors[1]
        )
        out_ref[chunk, 0:HEAD] = sums.astype(jnp.bfloat16)
        out_ref[chunk, HEAD:CHUNK] = stat_rows(top, total)


def combine_kernel(meta_ref, parts_ref, query_ref, even_ref, odd_ref, mine_ref, out_ref):
    count, _, lanes = parts_ref.shape
    half = query_ref.shape[0]
    beams = mine_ref.shape[1]
    second = jnp.bitwise_and(meta_ref[1], 1) == 1
    keys = jnp.where(second, odd_ref[...], even_ref[...])
    values = jnp.where(second, even_ref[...], odd_ref[...])
    row = lax.broadcasted_iota(jnp.int32, (2 * half, lanes), 0)
    lane = lax.broadcasted_iota(jnp.int32, (2 * half, lanes), 1)
    parents = mine_ref[mine_ref.shape[0] - 1 :]
    parents = (parents // beams) * half + parents % beams
    parents = jnp.concatenate([jnp.full_like(parents, -1), parents] * 2, axis=1)
    allowed = (row == meta_ref[2] * half + lane % half) | (row == parents)
    scores = jnp.where(allowed, scores_of(keys, query_rows_of(query_ref[...])), DEAD)

    stats = [read_stats(parts_ref[part, HEAD:CHUNK]) for part in range(count)]
    top = functools.reduce(jnp.maximum, [each for each, _ in stats], jnp.max(scores, axis=0, keepdims=True))
    weights = jnp.where(allowed, jnp.exp2((scores - top) * EXP2_SCALE), 0.0)
    high = weights.astype(jnp.bfloat16)
    low = (weights - high.astype(jnp.float32)).astype(jnp.bfloat16)
    tall_values = jnp.transpose(values)
    sums = jnp.dot(tall_values, high, preferred_element_type=jnp.float32)
    sums = sums + jnp.dot(tall_values, low, preferred_element_type=jnp.float32)
    total = jnp.sum(weights, axis=0, keepdims=True)
    for part in range(count):
        factor = jnp.exp2((stats[part][0] - top) * EXP2_SCALE)
        total = total + stats[part][1] * factor
        sums = sums + parts_ref[part, 0:HEAD].astype(jnp.float32) * factor
    tall = jnp.transpose(sums / total)
    found = jnp.concatenate([tall[0:half], tall[half : 2 * half]], axis=1).astype(jnp.bfloat16)
    for target in range(out_ref.shape[0]):
        out_ref[target] = found


def project_kernel(flip, meta_ref, rows_ref, weight_ref, before_ref, out_ref):
    total = before_ref[...]
    parity = jnp.bitwise_xor(jnp.bitwise_and(meta_ref[1], 1), flip)
    for part in range(rows_ref.shape[0]):
        total = total + jnp.dot(rows_ref[part], weight_ref[part, parity], preferred_element_type=jnp.float32)
    out_ref[...] = total.astype(out_ref.dtype)


def call(kernel, out_shape, name, spaces, vmem, out_spaces="v", **rest):
    kinds = {"s": pltpu.SMEM, "v": pltpu.VMEM, "h": pltpu.HBM, "a": pl.ANY}
    specs = lambda letters: [pl.BlockSpec(memory_space=kinds[letter]) for letter in letters]
    return pl.pallas_call(
        kernel,
        out_shape=out_shape,
        in_specs=specs(spaces),
        out_specs=specs(out_spaces) if len(out_spaces) > 1 else specs(out_spaces)[0],
        compiler_params=pltpu.CompilerParams(vmem_limit_bytes=vmem * MIB),
        name=name,
        **rest,
    )


def shards(
    codes, parents, lengths, holders, history_keys, history_values, query_table, kv_table, embed_table, out_weight
):
    beams = parents.shape[0]
    levels, code_count, width = query_table.shape
    half = levels * beams
    rows = 2 * half
    slots = history_keys.shape[1]
    z_count = lax.axis_size("z")
    pair, z, core = lax.axis_index("pair"), lax.axis_index("z"), lax.axis_index("core")
    hist = 2 * z + core
    bf16, f32 = jnp.bfloat16, jnp.float32
    array = jax.ShapeDtypeStruct
    dma = pltpu.SemaphoreType.DMA
    swap = [(0, 1), (1, 0)]

    hbm = lambda x: pltpu.with_memory_space_constraint(x, pltpu.HBM)

    query_rows, own_query, mine = call(
        look_kernel,
        (array((2 * z_count, half, width), bf16), array((half, width), bf16), array((levels + 1, beams), jnp.int32)),
        "look",
        "hhh",
        4,
        "vvv",
        scratch_shapes=[pltpu.VMEM(query_table.shape, bf16), dma((3,))],
    )(hbm(codes), hbm(parents[None]), hbm(query_table))
    queries = lax.all_to_all(query_rows, ("pair", "z"), split_axis=0, concat_axis=0, tiled=True)

    mine, near_keys, near_values = lax.optimization_barrier((mine, history_keys[0], history_values[0]))
    other = lax.ppermute(mine, "pair", swap)
    far_keys = lax.ppermute(near_keys, "core", swap)
    far_values = lax.ppermute(near_values, "core", swap)
    meta = jnp.stack([lax.axis_index("grp"), pair * 2 * z_count + hist, pair, jnp.int32(slots)]).astype(jnp.int32)
    kv_rows, residual, live = call(
        generated_kernel,
        (array((rows, HEAD), bf16), array((half, width), f32), array((2,), jnp.int32)),
        "generated",
        "svvhhhh",
        4,
        "vvs",
        scratch_shapes=[
            pltpu.VMEM(kv_table.shape, bf16),
            pltpu.VMEM(embed_table.shape, bf16),
            pltpu.SMEM(lengths.shape, jnp.int32),
            pltpu.SMEM(holders.shape, jnp.int32),
            dma((4,)),
        ],
    )(meta, mine, other, hbm(kv_table), hbm(embed_table), hbm(lengths), hbm(holders))
    even = [(k + KEY_HEADS * v, 2 * k + v) for k in range(KEY_HEADS) for v in range(2)]
    odd = [(k + KEY_HEADS * v, 2 * k + 1 - v) for k in range(KEY_HEADS) for v in range(2)]
    even_rows = lax.ppermute(kv_rows, ("z", "core"), even)
    odd_rows = lax.ppermute(kv_rows, ("z", "core"), odd)

    shape = (z_count, CHUNK, 2 * half)

    def attend(flip, name, queries):
        return call(
            functools.partial(attend_kernel, flip),
            array(shape, bf16),
            name,
            "ssvhhaa",
            24,
            scratch_shapes=[
                pltpu.VMEM((2, 2 * slots, 2 * rows), f32),
                pltpu.VMEM((KEY_HEADS // 2, 2 * slots, 2 * HEAD), bf16),
                pltpu.VMEM((KEY_HEADS // 2, 2 * slots, 2 * HEAD), bf16),
                dma((KEY_HEADS,)),
                dma((KEY_HEADS,)),
            ],
            cost_estimate=pl.CostEstimate(
                flops=2 * 4 * rows * KEY_HEADS * slots * HEAD,
                bytes_accessed=4 * slots * KEY_HEADS * HEAD,
                transcendentals=2 * rows * KEY_HEADS * slots,
            ),
        )(meta, live, queries, hbm(near_keys), hbm(near_values), far_keys, far_values)

    send = attend(1, "attend_other", queries)
    arrived = lax.ppermute(send, "pair", swap)
    queries, even_rows, odd_rows = lax.optimization_barrier((queries, even_rows, odd_rows))
    keep = attend(0, "attend_own", queries)
    merged = call(merge_kernel, array(shape, bf16), "merge", "vv", 4)(keep, arrived)
    parts = lax.all_to_all(merged, "z", split_axis=0, concat_axis=0, tiled=True)
    attention = call(combine_kernel, array((z_count, half, width), bf16), "combine", "svvvvv", 4)(
        meta, parts, own_query, even_rows, odd_rows, mine
    )
    near_rows = lax.all_to_all(attention, "z", split_axis=0, concat_axis=0, tiled=True)
    far_rows = lax.ppermute(near_rows, "core", swap)
    weight = out_weight.reshape(z_count, 2, width, width)
    begun = call(functools.partial(project_kernel, 0), array((half, width), f32), "project_near", "svvv", 4)(
        meta, near_rows, weight, residual
    )
    out = call(functools.partial(project_kernel, 1), array((half, width), bf16), "project_far", "svvv", 4)(
        meta, far_rows, weight, begun
    )
    return out.reshape(levels, beams, width)


def solution(mesh):
    split = Mesh(mesh.devices.reshape(16, 2, 8, 2), ("grp", "pair", "z", "core"))
    req, hist = ("grp", "pair"), ("z", "core")
    in_specs = (
        P(None, req),
        P(req),
        P(),
        P(),
        P(req, hist, None),
        P(req, hist, None),
        P(None, None, hist),
        P(None, None, hist),
        P(None, None, hist),
        P(None, hist),
    )
    return jax.shard_map(shards, mesh=split, in_specs=in_specs, out_specs=P(None, req, hist), check_vma=False)
```

```python
import functools
import math

import jax
import jax.numpy as jnp
from jax import lax
from jax.experimental import pallas as pl
from jax.experimental.pallas import tpu as pltpu
from jax.sharding import Mesh, PartitionSpec as P

KEY_HEADS = 8
HEAD = 128
STAT = 16
CHUNK = HEAD + STAT
DEAD = -1e30
EXP2_SCALE = HEAD ** (-0.5) * math.log2(math.e)
MIB = 1024 * 1024


def one_hot_rows(index_row, count):
    rows = index_row.shape[1]
    tall = jnp.transpose(jnp.broadcast_to(index_row, (128, rows)))
    parts = []
    for start in range(0, count, 128):
        lane = lax.broadcasted_iota(jnp.int32, (rows, 128), 1) + start
        parts.append((tall == lane).astype(jnp.float32).astype(jnp.bfloat16))
    return jnp.concatenate(parts, axis=1)


def look_kernel(codes_hbm, parents_hbm, query_hbm, out_ref, mine_ref, query_ref, sem):
    levels, beams = codes_hbm.shape
    copies = [
        pltpu.make_async_copy(codes_hbm, mine_ref.at[pl.ds(0, levels)], sem.at[0]),
        pltpu.make_async_copy(parents_hbm, mine_ref.at[pl.ds(levels, 1)], sem.at[1]),
        pltpu.make_async_copy(query_hbm, query_ref, sem.at[2]),
    ]
    for copy in copies:
        copy.start()
    copies[0].wait()
    copies[1].wait()
    hots = [one_hot_rows(mine_ref[level : level + 1], query_ref.shape[1]) for level in range(levels)]
    copies[2].wait()
    for level, hot in enumerate(hots):
        found = jnp.dot(hot, query_ref[level], preferred_element_type=jnp.float32).astype(jnp.bfloat16)
        for target in range(out_ref.shape[0]):
            out_ref[target, level * beams : (level + 1) * beams] = found


def generated_kernel(
    meta_ref, mine_ref, other_ref, kv_hbm, embed_hbm, lengths_hbm, holders_hbm, out_ref, residual_ref, live_ref,
    kv_ref, embed_ref, lengths_ref, holders_ref, sem
):
    copies = [
        pltpu.make_async_copy(lengths_hbm, lengths_ref, sem.at[0]),
        pltpu.make_async_copy(holders_hbm, holders_ref, sem.at[1]),
        pltpu.make_async_copy(kv_hbm, kv_ref, sem.at[2]),
        pltpu.make_async_copy(embed_hbm, embed_ref, sem.at[3]),
    ]
    for copy in copies:
        copy.start()
    levels, beams = kv_ref.shape[0], mine_ref.shape[1]
    hots = [
        jnp.concatenate([one_hot_rows(ref[level : level + 1], kv_ref.shape[1]) for ref in (mine_ref, other_ref)])
        for level in range(levels)
    ]
    for copy in copies:
        copy.wait()
    for level, hot in enumerate(hots):
        found = jnp.dot(hot, kv_ref[level], preferred_element_type=jnp.float32).astype(jnp.bfloat16)
        residual_ref[level * beams : (level + 1) * beams] = jnp.dot(
            hot[:beams], embed_ref[level], preferred_element_type=jnp.float32
        )
        for part, x in enumerate((meta_ref[3], 1 - meta_ref[3])):
            place = pl.ds(pl.multiple_of((x * levels + level) * beams, beams), beams)
            out_ref[place] = found[part * beams : (part + 1) * beams]
    request, place, block_slots = meta_ref[0], meta_ref[1], meta_ref[4]
    near, far = jnp.int32(0), jnp.int32(0)
    for block in range(holders_ref.shape[1]):
        holder = holders_ref[request, block]
        near = jnp.where(holder == place, block, near)
        far = jnp.where(holder == jnp.bitwise_xor(place, 1), block, far)
    for at, position in enumerate((near, far)):
        live_ref[at] = jnp.clip(lengths_ref[request] - position * block_slots, 0, block_slots)


def split3(value):
    high = value.astype(jnp.bfloat16).astype(jnp.float32)
    rest = value - high
    middle = rest.astype(jnp.bfloat16).astype(jnp.float32)
    return high, middle, rest - middle


def stat_rows(top, total):
    row = lax.broadcasted_iota(jnp.int32, (STAT, top.shape[1]), 0)
    out = jnp.zeros((STAT, top.shape[1]), jnp.float32)
    for at, piece in enumerate(split3(top) + split3(total)):
        out = jnp.where(row == at, piece, out)
    return out.astype(jnp.bfloat16)


def read_stats(rows):
    wide = rows.astype(jnp.float32)
    return wide[0:1] + wide[1:2] + wide[2:3], wide[3:4] + wide[4:5] + wide[5:6]


def scores_of(keys, rows):
    return lax.dot_general(keys, rows, (((1,), (1,)), ((), ())), preferred_element_type=jnp.float32)


def extended(values):
    return jnp.concatenate([jnp.transpose(values), jnp.ones((STAT, values.shape[0]), jnp.bfloat16)], axis=0)


def regroup_kernel(query_ref, out_ref):
    heads, half = out_ref.shape[0], query_ref.shape[1]
    for head in range(heads):
        for x in range(2):
            for h in range(2):
                rows = slice((2 * x + h) * half, (2 * x + h + 1) * half)
                out_ref[head, rows] = query_ref[x * heads + head, :, h * HEAD : (h + 1) * HEAD]


def write(out_ref, head, sums, total, top):
    width = sums.shape[1] // 2
    for x in range(2):
        lanes = slice(x * width, (x + 1) * width)
        out_ref[x, head, 0:HEAD] = sums[:, lanes].astype(jnp.bfloat16)
        out_ref[x, head, HEAD:CHUNK] = stat_rows(top[:, lanes], total[:, lanes])


def attend_kernel(
    live_ref, query_ref, near_key, near_value, far_key, far_value, out_ref, score_ref, key_ref, value_ref, key_sem, value_sem
):
    heads, slots = key_ref.shape[0], key_ref.shape[1]
    half = query_ref.shape[1] // 4
    block_slots = slots // 2
    near_live, far_live = live_ref[0], live_ref[1]
    live = near_live + far_live

    def copies(head, keys):
        sources, target, sem = ((near_key, far_key), key_ref, key_sem) if keys else ((near_value, far_value), value_ref, value_sem)
        lanes = pl.ds(pl.multiple_of(head * HEAD, HEAD), HEAD)
        return [
            pltpu.make_async_copy(
                source.at[:, lanes], target.at[head, pl.ds(block * block_slots, block_slots)], sem.at[block * heads + head]
            )
            for block, source in enumerate(sources)
        ]

    def wait(head, keys):
        for copy in copies(head, keys):
            copy.wait()

    def attend(masked):
        def begin(head, _):
            for keys in (True, False):
                for copy in copies(head, keys):
                    copy.start()
            return 0

        lax.fori_loop(0, heads, begin, 0)

        def score(head, at):
            scores = scores_of(key_ref[head], query_ref[head])
            if masked:
                slot = lax.broadcasted_iota(jnp.int32, (slots, 1), 0)
                allowed = (slot < near_live) | ((slot >= block_slots) & (slot < block_slots + far_live))
                scores = jnp.where(allowed, scores, DEAD)
            score_ref[at] = scores
            return jnp.max(scores, axis=0, keepdims=True)

        def finish(head, at, top):
            weights = jnp.exp2((score_ref[at] - top) * EXP2_SCALE).astype(jnp.bfloat16)
            sums = jnp.dot(extended(value_ref[head]), weights, preferred_element_type=jnp.float32)
            write(out_ref, head, sums[0:HEAD], sums[HEAD : HEAD + 1], top)

        def step(i, top):
            wait(2 * i + 1, True)
            wait(2 * i + 2, True)
            wait(2 * i, False)
            wait(2 * i + 1, False)
            later = score(2 * i + 1, 1)
            finish(2 * i, 0, top)
            top = score(2 * i + 2, 0)
            finish(2 * i + 1, 1, later)
            return top

        wait(0, True)
        top = lax.fori_loop(0, heads // 2 - 1, step, score(0, 0))
        wait(heads - 1, True)
        wait(heads - 2, False)
        wait(heads - 1, False)
        later = score(heads - 1, 1)
        finish(heads - 2, 0, top)
        finish(heads - 1, 1, later)

    @pl.when(live == slots)
    def _():
        attend(False)

    @pl.when((live > 0) & (live < slots))
    def _():
        attend(True)

    @pl.when(live == 0)
    def _():
        row = lax.broadcasted_iota(jnp.int32, (CHUNK, 2 * half), 0)
        tops = split3(jnp.full((CHUNK, 2 * half), DEAD, jnp.float32))
        dead = jnp.zeros((CHUNK, 2 * half), jnp.float32)
        for at, piece in enumerate(tops):
            dead = jnp.where(row == HEAD + at, piece, dead)
        dead = dead.astype(jnp.bfloat16)
        for x in range(2):
            for head in range(heads):
                out_ref[x, head] = dead


def add_generated_kernel(
    meta_ref, query_ref, kv_ref, far_kv_ref, gen_value_ref, mine_ref, other_ref, before_ref, out_ref
):
    width = query_ref.shape[1]
    half = width // 4
    head = meta_ref[2]

    @pl.when(head >= 0)
    def _():
        values = extended(gen_value_ref[...])
        row = lax.broadcasted_iota(jnp.int32, (2 * half, width), 0)
        lane = lax.broadcasted_iota(jnp.int32, (2 * half, width), 1)
        own = (lane // (2 * half)) * half + lane % half
        beams = mine_ref.shape[1]
        swapped = meta_ref[3] != 0
        mine, other = (ref[mine_ref.shape[0] - 1 :] for ref in (mine_ref, other_ref))
        pieces = []
        for parents in (jnp.where(swapped, other, mine), jnp.where(swapped, mine, other)):
            parents = (parents // beams) * half + parents % beams
            pieces += [jnp.full_like(parents, -1), parents] * 2
        allowed = (row == own) | (row == jnp.concatenate(pieces, axis=1))
        keys = jnp.where(swapped, far_kv_ref[...], kv_ref[...])
        scores = jnp.where(allowed, scores_of(keys, query_ref[head]), DEAD)
        before = jnp.concatenate([before_ref[x, head] for x in range(2)], axis=1)
        old_top, old_total = read_stats(before[HEAD:CHUNK])
        top = jnp.maximum(old_top, jnp.max(scores, axis=0, keepdims=True))
        weights = jnp.where(allowed, jnp.exp2((scores - top) * EXP2_SCALE), 0.0)
        high = weights.astype(jnp.bfloat16)
        low = (weights - high.astype(jnp.float32)).astype(jnp.bfloat16)
        added = jnp.dot(values, high, preferred_element_type=jnp.float32)
        added = added + jnp.dot(values, low, preferred_element_type=jnp.float32)
        factor = jnp.exp2((old_top - top) * EXP2_SCALE)
        sums = before[0:HEAD].astype(jnp.float32) * factor + added[0:HEAD]
        write(out_ref, head, sums, old_total * factor + added[HEAD : HEAD + 1], top)


def combine_kernel(parts_ref, out_ref):
    count = parts_ref.shape[0]
    stats = [read_stats(parts_ref[part, HEAD:CHUNK]) for part in range(count)]
    top = functools.reduce(jnp.maximum, [each for each, _ in stats])
    total = jnp.zeros_like(top)
    sums = jnp.zeros((HEAD, parts_ref.shape[2]), jnp.float32)
    for part in range(count):
        factor = jnp.exp2((stats[part][0] - top) * EXP2_SCALE)
        total = total + stats[part][1] * factor
        sums = sums + parts_ref[part, 0:HEAD].astype(jnp.float32) * factor
    tall = jnp.transpose(sums / total)
    rows = out_ref.shape[1]
    found = jnp.concatenate([tall[0:rows], tall[rows : 2 * rows]], axis=1).astype(jnp.bfloat16)
    for target in range(out_ref.shape[0]):
        out_ref[target] = found


def project_kernel(flip, meta_ref, rows_ref, weight_ref, before_ref, out_ref):
    total = before_ref[...]
    parity = jnp.bitwise_xor(jnp.bitwise_and(meta_ref[1], 1), flip)
    for part in range(rows_ref.shape[0]):
        total = total + jnp.dot(rows_ref[part], weight_ref[part, parity], preferred_element_type=jnp.float32)
    out_ref[...] = total.astype(out_ref.dtype)


def call(kernel, out_shape, name, spaces, vmem, out_spaces="v", **rest):
    kinds = {"s": pltpu.SMEM, "v": pltpu.VMEM, "h": pltpu.HBM, "a": pl.ANY}
    specs = lambda letters: [pl.BlockSpec(memory_space=kinds[letter]) for letter in letters]
    return pl.pallas_call(
        kernel,
        out_shape=out_shape,
        in_specs=specs(spaces),
        out_specs=specs(out_spaces) if len(out_spaces) > 1 else specs(out_spaces)[0],
        compiler_params=pltpu.CompilerParams(vmem_limit_bytes=vmem * MIB),
        name=name,
        **rest,
    )


def shards(
    codes, parents, lengths, holders, history_keys, history_values, query_table, kv_table, embed_table, out_weight
):
    beams = parents.shape[0]
    levels, code_count, width = query_table.shape
    half = levels * beams
    rows = 2 * half
    slots = history_keys.shape[1]
    z_count = lax.axis_size("z")
    pair, z, core = lax.axis_index("pair"), lax.axis_index("z"), lax.axis_index("core")
    hist = 2 * z + core
    bf16, f32 = jnp.bfloat16, jnp.float32
    array = jax.ShapeDtypeStruct
    dma = pltpu.SemaphoreType.DMA
    swap = [(0, 1), (1, 0)]

    hbm = lambda x: pltpu.with_memory_space_constraint(x, pltpu.HBM)

    query_rows, mine = call(
        look_kernel,
        (array((2 * z_count, half, width), bf16), array((levels + 1, beams), jnp.int32)),
        "look",
        "hhh",
        4,
        "vv",
        scratch_shapes=[pltpu.VMEM(query_table.shape, bf16), dma((3,))],
    )(hbm(codes), hbm(parents[None]), hbm(query_table))
    queries = lax.all_to_all(query_rows, ("pair", "z"), split_axis=0, concat_axis=0, tiled=True)
    mine, near_keys, near_values = lax.optimization_barrier((mine, history_keys[0], history_values[0]))
    other = lax.ppermute(mine, "pair", swap)
    far_keys = lax.ppermute(near_keys, "core", swap)
    far_values = lax.ppermute(near_values, "core", swap)
    gen_head = jnp.where(z < z_count // 2, 2 * z + jnp.bitwise_xor(core, pair), -1)
    meta = jnp.stack([lax.axis_index("grp"), pair * 2 * z_count + hist, gen_head, pair, jnp.int32(slots)]).astype(jnp.int32)
    kv_rows, residual, live = call(
        generated_kernel,
        (array((rows, HEAD), bf16), array((half, width), f32), array((2,), jnp.int32)),
        "generated",
        "svvhhhh",
        4,
        "vvs",
        scratch_shapes=[
            pltpu.VMEM(kv_table.shape, bf16),
            pltpu.VMEM(embed_table.shape, bf16),
            pltpu.SMEM(lengths.shape, jnp.int32),
            pltpu.SMEM(holders.shape, jnp.int32),
            dma((4,)),
        ],
    )(meta, mine, other, hbm(kv_table), hbm(embed_table), hbm(lengths), hbm(holders))
    at = lambda p, k, c: (p * z_count + k) * 2 + c
    taken = [(p, k, c) for p in range(2) for k in range(z_count // 2) for c in range(2)]
    gen_values = lax.ppermute(
        kv_rows, ("pair", "z", "core"), [(at(p, k + z_count // 2, c ^ p), at(p, k, c)) for p, k, c in taken]
    )
    far_kv = lax.ppermute(kv_rows, ("pair", "z", "core"), [(at(1, k, 1 - c), at(1, k, c)) for p, k, c in taken if p])

    queries, live = lax.optimization_barrier((queries, live))
    queries = call(
        regroup_kernel,
        array((KEY_HEADS, 2 * rows, HEAD), bf16),
        "regroup",
        "v",
        4,
        cost_estimate=pl.CostEstimate(flops=0, bytes_accessed=44 * 10**6, transcendentals=0),
    )(queries)
    partial_shape = (2, z_count, CHUNK, 2 * half)
    partials = call(
        attend_kernel,
        array(partial_shape, bf16),
        "attend",
        "svhhaa",
        24,
        scratch_shapes=[
            pltpu.VMEM((2, 2 * slots, 2 * rows), f32),
            pltpu.VMEM((KEY_HEADS, 2 * slots, HEAD), bf16),
            pltpu.VMEM((KEY_HEADS, 2 * slots, HEAD), bf16),
            dma((2 * KEY_HEADS,)),
            dma((2 * KEY_HEADS,)),
        ],
        cost_estimate=pl.CostEstimate(
            flops=4 * 4 * rows * KEY_HEADS * slots * HEAD,
            bytes_accessed=4 * slots * KEY_HEADS * HEAD,
            transcendentals=4 * rows * KEY_HEADS * slots,
        ),
    )(live, queries, hbm(near_keys), hbm(near_values), far_keys, far_values)
    partials = call(
        add_generated_kernel, array(partial_shape, bf16), "add_generated", "svvvvvvv", 4, input_output_aliases={7: 0}
    )(meta, queries, kv_rows, far_kv, gen_values, mine, other, partials)

    shape = (2 * z_count, CHUNK, 2 * half)
    parts = lax.all_to_all(partials.reshape(shape), ("pair", "z"), split_axis=0, concat_axis=0, tiled=True)
    attention = call(combine_kernel, array((z_count, half, width), bf16), "combine", "v", 4)(parts)
    near_rows = lax.all_to_all(attention, "z", split_axis=0, concat_axis=0, tiled=True)
    far_rows = lax.ppermute(near_rows, "core", swap)
    weight = out_weight.reshape(z_count, 2, width, width)
    begun = call(functools.partial(project_kernel, 0), array((half, width), f32), "project_near", "svvv", 4)(
        meta, near_rows, weight, residual
    )
    out = call(functools.partial(project_kernel, 1), array((half, width), bf16), "project_far", "svvv", 4)(
        meta, far_rows, weight, begun
    )
    return out.reshape(levels, beams, width)


def solution(mesh):
    split = Mesh(mesh.devices.reshape(16, 2, 8, 2), ("grp", "pair", "z", "core"))
    req, hist = ("grp", "pair"), ("z", "core")
    in_specs = (
        P(None, req),
        P(req),
        P(),
        P(),
        P(req, hist, None),
        P(req, hist, None),
        P(None, None, hist),
        P(None, None, hist),
        P(None, None, hist),
        P(None, hist),
    )
    return jax.shard_map(shards, mesh=split, in_specs=in_specs, out_specs=P(None, req, hist), check_vma=False)
```

```python
import functools
import math

import jax
import jax.numpy as jnp
from jax import lax
from jax.experimental import pallas as pl
from jax.experimental.pallas import tpu as pltpu
from jax.sharding import Mesh, PartitionSpec as P

KEY_HEADS = 8
HEAD = 128
STAT = 16
CHUNK = HEAD + STAT
DEAD = -1e30
EXP2_SCALE = HEAD ** (-0.5) * math.log2(math.e)
MIB = 1024 * 1024


def one_hot_rows(index_row, count):
    rows = index_row.shape[1]
    tall = jnp.transpose(jnp.broadcast_to(index_row, (128, rows)))
    parts = []
    for start in range(0, count, 128):
        lane = lax.broadcasted_iota(jnp.int32, (rows, 128), 1) + start
        parts.append((tall == lane).astype(jnp.float32).astype(jnp.bfloat16))
    return jnp.concatenate(parts, axis=1)


def look_kernel(codes_hbm, parents_hbm, query_hbm, out_ref, mine_ref, query_ref, sem):
    levels, beams = codes_hbm.shape
    copies = [
        pltpu.make_async_copy(codes_hbm, mine_ref.at[pl.ds(0, levels)], sem.at[0]),
        pltpu.make_async_copy(parents_hbm, mine_ref.at[pl.ds(levels, 1)], sem.at[1]),
        pltpu.make_async_copy(query_hbm, query_ref, sem.at[2]),
    ]
    for copy in copies:
        copy.start()
    copies[0].wait()
    copies[1].wait()
    hots = [one_hot_rows(mine_ref[level : level + 1], query_ref.shape[1]) for level in range(levels)]
    copies[2].wait()
    for level, hot in enumerate(hots):
        found = jnp.dot(hot, query_ref[level], preferred_element_type=jnp.float32).astype(jnp.bfloat16)
        for target in range(out_ref.shape[0]):
            out_ref[target, level * beams : (level + 1) * beams] = found


def generated_kernel(
    meta_ref, mine_ref, other_ref, kv_hbm, embed_hbm, lengths_hbm, holders_hbm, out_ref, residual_ref, live_ref,
    kv_ref, embed_ref, lengths_ref, holders_ref, sem
):
    copies = [
        pltpu.make_async_copy(lengths_hbm, lengths_ref, sem.at[0]),
        pltpu.make_async_copy(holders_hbm, holders_ref, sem.at[1]),
        pltpu.make_async_copy(kv_hbm, kv_ref, sem.at[2]),
        pltpu.make_async_copy(embed_hbm, embed_ref, sem.at[3]),
    ]
    for copy in copies:
        copy.start()
    levels, beams = kv_ref.shape[0], mine_ref.shape[1]
    hots = [
        jnp.concatenate([one_hot_rows(ref[level : level + 1], kv_ref.shape[1]) for ref in (mine_ref, other_ref)])
        for level in range(levels)
    ]
    for copy in copies:
        copy.wait()
    for level, hot in enumerate(hots):
        found = jnp.dot(hot, kv_ref[level], preferred_element_type=jnp.float32).astype(jnp.bfloat16)
        residual_ref[level * beams : (level + 1) * beams] = jnp.dot(
            hot[:beams], embed_ref[level], preferred_element_type=jnp.float32
        )
        for part, x in enumerate((meta_ref[3], 1 - meta_ref[3])):
            place = pl.ds(pl.multiple_of((x * levels + level) * beams, beams), beams)
            out_ref[place] = found[part * beams : (part + 1) * beams]
    request, place, block_slots = meta_ref[0], meta_ref[1], meta_ref[4]
    near, far = jnp.int32(0), jnp.int32(0)
    for block in range(holders_ref.shape[1]):
        holder = holders_ref[request, block]
        near = jnp.where(holder == place, block, near)
        far = jnp.where(holder == jnp.bitwise_xor(place, 1), block, far)
    for at, position in enumerate((near, far)):
        live_ref[at] = jnp.clip(lengths_ref[request] - position * block_slots, 0, block_slots)


def split3(value):
    high = value.astype(jnp.bfloat16).astype(jnp.float32)
    rest = value - high
    middle = rest.astype(jnp.bfloat16).astype(jnp.float32)
    return high, middle, rest - middle


def stat_rows(top, total):
    row = lax.broadcasted_iota(jnp.int32, (STAT, top.shape[1]), 0)
    out = jnp.zeros((STAT, top.shape[1]), jnp.float32)
    for at, piece in enumerate(split3(top) + split3(total)):
        out = jnp.where(row == at, piece, out)
    return out.astype(jnp.bfloat16)


def read_stats(rows):
    wide = rows.astype(jnp.float32)
    return wide[0:1] + wide[1:2] + wide[2:3], wide[3:4] + wide[4:5] + wide[5:6]


def scores_of(keys, rows):
    return lax.dot_general(keys, rows, (((1,), (1,)), ((), ())), preferred_element_type=jnp.float32)


def extended(values):
    return jnp.concatenate([jnp.transpose(values), jnp.ones((STAT, values.shape[0]), jnp.bfloat16)], axis=0)


def regroup_kernel(query_ref, out_ref):
    heads, half = out_ref.shape[0], query_ref.shape[1]
    for head in range(heads):
        for x in range(2):
            for h in range(2):
                rows = slice((2 * x + h) * half, (2 * x + h + 1) * half)
                out_ref[head, rows] = query_ref[x * heads + head, :, h * HEAD : (h + 1) * HEAD]


def write(out_ref, head, sums, total, top):
    width = sums.shape[1] // 2
    for x in range(2):
        lanes = slice(x * width, (x + 1) * width)
        out_ref[x, head, 0:HEAD] = sums[:, lanes].astype(jnp.bfloat16)
        out_ref[x, head, HEAD:CHUNK] = stat_rows(top[:, lanes], total[:, lanes])


def attend_kernel(
    live_ref, query_ref, near_key, near_value, far_key, far_value, out_ref, score_ref, key_ref, value_ref, key_sem, value_sem
):
    heads, slots = key_ref.shape[0], key_ref.shape[1]
    half = query_ref.shape[1] // 4
    block_slots = slots // 2
    near_live, far_live = live_ref[0], live_ref[1]
    live = near_live + far_live

    def copies(head, keys):
        sources, target, sem = ((near_key, far_key), key_ref, key_sem) if keys else ((near_value, far_value), value_ref, value_sem)
        lanes = pl.ds(pl.multiple_of(head * HEAD, HEAD), HEAD)
        return [
            pltpu.make_async_copy(
                source.at[:, lanes], target.at[head, pl.ds(block * block_slots, block_slots)], sem.at[block * heads + head]
            )
            for block, source in enumerate(sources)
        ]

    def wait(head, keys):
        for copy in copies(head, keys):
            copy.wait()

    def attend(masked):
        def begin(head, _):
            for keys in (True, False):
                for copy in copies(head, keys):
                    copy.start()
            return 0

        lax.fori_loop(0, heads, begin, 0)

        def score(head, at):
            scores = scores_of(key_ref[head], query_ref[head])
            if masked:
                slot = lax.broadcasted_iota(jnp.int32, (slots, 1), 0)
                allowed = (slot < near_live) | ((slot >= block_slots) & (slot < block_slots + far_live))
                scores = jnp.where(allowed, scores, DEAD)
            score_ref[at] = scores
            return jnp.max(scores, axis=0, keepdims=True)

        def finish(head, at, top):
            weights = jnp.exp2((score_ref[at] - top) * EXP2_SCALE).astype(jnp.bfloat16)
            sums = jnp.dot(extended(value_ref[head]), weights, preferred_element_type=jnp.float32)
            write(out_ref, head, sums[0:HEAD], sums[HEAD : HEAD + 1], top)

        def step(i, top):
            wait(2 * i + 1, True)
            wait(2 * i + 2, True)
            wait(2 * i, False)
            wait(2 * i + 1, False)
            later = score(2 * i + 1, 1)
            finish(2 * i, 0, top)
            top = score(2 * i + 2, 0)
            finish(2 * i + 1, 1, later)
            return top

        wait(0, True)
        top = lax.fori_loop(0, heads // 2 - 1, step, score(0, 0))
        wait(heads - 1, True)
        wait(heads - 2, False)
        wait(heads - 1, False)
        later = score(heads - 1, 1)
        finish(heads - 2, 0, top)
        finish(heads - 1, 1, later)

    @pl.when(live == slots)
    def _():
        attend(False)

    @pl.when((live > 0) & (live < slots))
    def _():
        attend(True)

    @pl.when(live == 0)
    def _():
        row = lax.broadcasted_iota(jnp.int32, (CHUNK, 2 * half), 0)
        tops = split3(jnp.full((CHUNK, 2 * half), DEAD, jnp.float32))
        dead = jnp.zeros((CHUNK, 2 * half), jnp.float32)
        for at, piece in enumerate(tops):
            dead = jnp.where(row == HEAD + at, piece, dead)
        dead = dead.astype(jnp.bfloat16)
        for x in range(2):
            for head in range(heads):
                out_ref[x, head] = dead


def add_generated_kernel(
    meta_ref, query_ref, kv_ref, far_kv_ref, gen_value_ref, mine_ref, other_ref, before_ref, out_ref
):
    width = query_ref.shape[1]
    half = width // 4
    head = meta_ref[2]

    @pl.when(head >= 0)
    def _():
        values = extended(gen_value_ref[...])
        row = lax.broadcasted_iota(jnp.int32, (2 * half, width), 0)
        lane = lax.broadcasted_iota(jnp.int32, (2 * half, width), 1)
        own = (lane // (2 * half)) * half + lane % half
        beams = mine_ref.shape[1]
        swapped = meta_ref[3] != 0
        mine, other = (ref[mine_ref.shape[0] - 1 :] for ref in (mine_ref, other_ref))
        pieces = []
        for parents in (jnp.where(swapped, other, mine), jnp.where(swapped, mine, other)):
            parents = (parents // beams) * half + parents % beams
            pieces += [jnp.full_like(parents, -1), parents] * 2
        allowed = (row == own) | (row == jnp.concatenate(pieces, axis=1))
        keys = jnp.where(swapped, far_kv_ref[...], kv_ref[...])
        scores = jnp.where(allowed, scores_of(keys, query_ref[head]), DEAD)
        before = jnp.concatenate([before_ref[x, head] for x in range(2)], axis=1)
        old_top, old_total = read_stats(before[HEAD:CHUNK])
        top = jnp.maximum(old_top, jnp.max(scores, axis=0, keepdims=True))
        weights = jnp.where(allowed, jnp.exp2((scores - top) * EXP2_SCALE), 0.0)
        high = weights.astype(jnp.bfloat16)
        low = (weights - high.astype(jnp.float32)).astype(jnp.bfloat16)
        added = jnp.dot(values, high, preferred_element_type=jnp.float32)
        added = added + jnp.dot(values, low, preferred_element_type=jnp.float32)
        factor = jnp.exp2((old_top - top) * EXP2_SCALE)
        sums = before[0:HEAD].astype(jnp.float32) * factor + added[0:HEAD]
        write(out_ref, head, sums, old_total * factor + added[HEAD : HEAD + 1], top)


def combine_kernel(parts_ref, out_ref):
    count = parts_ref.shape[0]
    stats = [read_stats(parts_ref[part, HEAD:CHUNK]) for part in range(count)]
    top = functools.reduce(jnp.maximum, [each for each, _ in stats])
    total = jnp.zeros_like(top)
    sums = jnp.zeros((HEAD, parts_ref.shape[2]), jnp.float32)
    for part in range(count):
        factor = jnp.exp2((stats[part][0] - top) * EXP2_SCALE)
        total = total + stats[part][1] * factor
        sums = sums + parts_ref[part, 0:HEAD].astype(jnp.float32) * factor
    tall = jnp.transpose(sums / total)
    rows = out_ref.shape[1]
    found = jnp.concatenate([tall[0:rows], tall[rows : 2 * rows]], axis=1).astype(jnp.bfloat16)
    for target in range(out_ref.shape[0]):
        out_ref[target] = found


def project_kernel(flip, meta_ref, rows_ref, weight_ref, before_ref, out_ref):
    total = before_ref[...]
    parity = jnp.bitwise_xor(jnp.bitwise_and(meta_ref[1], 1), flip)
    for part in range(rows_ref.shape[0]):
        total = total + jnp.dot(rows_ref[part], weight_ref[part, parity], preferred_element_type=jnp.float32)
    out_ref[...] = total.astype(out_ref.dtype)


def call(kernel, out_shape, name, spaces, vmem, out_spaces="v", **rest):
    kinds = {"s": pltpu.SMEM, "v": pltpu.VMEM, "h": pltpu.HBM, "a": pl.ANY}
    specs = lambda letters: [pl.BlockSpec(memory_space=kinds[letter]) for letter in letters]
    return pl.pallas_call(
        kernel,
        out_shape=out_shape,
        in_specs=specs(spaces),
        out_specs=specs(out_spaces) if len(out_spaces) > 1 else specs(out_spaces)[0],
        compiler_params=pltpu.CompilerParams(vmem_limit_bytes=vmem * MIB),
        name=name,
        **rest,
    )


def shards(
    codes, parents, lengths, holders, history_keys, history_values, query_table, kv_table, embed_table, out_weight
):
    beams = parents.shape[0]
    levels, code_count, width = query_table.shape
    half = levels * beams
    rows = 2 * half
    slots = history_keys.shape[1]
    z_count = lax.axis_size("z")
    pair, z, core = lax.axis_index("pair"), lax.axis_index("z"), lax.axis_index("core")
    hist = 2 * z + core
    bf16, f32 = jnp.bfloat16, jnp.float32
    array = jax.ShapeDtypeStruct
    dma = pltpu.SemaphoreType.DMA
    swap = [(0, 1), (1, 0)]

    hbm = lambda x: pltpu.with_memory_space_constraint(x, pltpu.HBM)

    query_rows, mine = call(
        look_kernel,
        (array((2 * z_count, half, width), bf16), array((levels + 1, beams), jnp.int32)),
        "look",
        "hhh",
        4,
        "vv",
        scratch_shapes=[pltpu.VMEM(query_table.shape, bf16), dma((3,))],
    )(hbm(codes), hbm(parents[None]), hbm(query_table))
    queries = lax.all_to_all(query_rows, ("pair", "z"), split_axis=0, concat_axis=0, tiled=True)
    mine, near_keys, near_values = lax.optimization_barrier((mine, history_keys[0], history_values[0]))
    other = lax.ppermute(mine, "pair", swap)
    far_keys = lax.ppermute(near_keys, "core", swap)
    far_values = lax.ppermute(near_values, "core", swap)
    gen_head = jnp.where(z < z_count // 2, 2 * z + jnp.bitwise_xor(core, pair), -1)
    meta = jnp.stack([lax.axis_index("grp"), pair * 2 * z_count + hist, gen_head, pair, jnp.int32(slots)]).astype(jnp.int32)
    kv_rows, residual, live = call(
        generated_kernel,
        (array((rows, HEAD), bf16), array((half, width), f32), array((2,), jnp.int32)),
        "generated",
        "svvhhhh",
        4,
        "vvs",
        scratch_shapes=[
            pltpu.VMEM(kv_table.shape, bf16),
            pltpu.VMEM(embed_table.shape, bf16),
            pltpu.SMEM(lengths.shape, jnp.int32),
            pltpu.SMEM(holders.shape, jnp.int32),
            dma((4,)),
        ],
    )(meta, mine, other, hbm(kv_table), hbm(embed_table), hbm(lengths), hbm(holders))
    at = lambda p, k, c: (p * z_count + k) * 2 + c
    taken = [(p, k, c) for p in range(2) for k in range(z_count // 2) for c in range(2)]
    gen_values = lax.ppermute(
        kv_rows, ("pair", "z", "core"), [(at(p, k + z_count // 2, c ^ p), at(p, k, c)) for p, k, c in taken]
    )
    far_kv = lax.ppermute(kv_rows, ("pair", "z", "core"), [(at(1, k, 1 - c), at(1, k, c)) for p, k, c in taken if p])

    queries, live = lax.optimization_barrier((queries, live))
    queries = call(
        regroup_kernel,
        array((KEY_HEADS, 2 * rows, HEAD), bf16),
        "regroup",
        "v",
        4,
        cost_estimate=pl.CostEstimate(flops=10**12, bytes_accessed=0, transcendentals=0),
    )(queries)
    partial_shape = (2, z_count, CHUNK, 2 * half)
    partials = call(
        attend_kernel,
        array(partial_shape, bf16),
        "attend",
        "svhhaa",
        24,
        scratch_shapes=[
            pltpu.VMEM((2, 2 * slots, 2 * rows), f32),
            pltpu.VMEM((KEY_HEADS, 2 * slots, HEAD), bf16),
            pltpu.VMEM((KEY_HEADS, 2 * slots, HEAD), bf16),
            dma((2 * KEY_HEADS,)),
            dma((2 * KEY_HEADS,)),
        ],
        cost_estimate=pl.CostEstimate(
            flops=4 * 4 * rows * KEY_HEADS * slots * HEAD,
            bytes_accessed=4 * slots * KEY_HEADS * HEAD,
            transcendentals=4 * rows * KEY_HEADS * slots,
        ),
    )(live, queries, hbm(near_keys), hbm(near_values), far_keys, far_values)
    partials = call(
        add_generated_kernel, array(partial_shape, bf16), "add_generated", "svvvvvvv", 4, input_output_aliases={7: 0}
    )(meta, queries, kv_rows, far_kv, gen_values, mine, other, partials)

    shape = (2 * z_count, CHUNK, 2 * half)
    parts = lax.all_to_all(partials.reshape(shape), ("pair", "z"), split_axis=0, concat_axis=0, tiled=True)
    attention = call(combine_kernel, array((z_count, half, width), bf16), "combine", "v", 4)(parts)
    near_rows = lax.all_to_all(attention, "z", split_axis=0, concat_axis=0, tiled=True)
    far_rows = lax.ppermute(near_rows, "core", swap)
    weight = out_weight.reshape(z_count, 2, width, width)
    begun = call(functools.partial(project_kernel, 0), array((half, width), f32), "project_near", "svvv", 4)(
        meta, near_rows, weight, residual
    )
    out = call(functools.partial(project_kernel, 1), array((half, width), bf16), "project_far", "svvv", 4)(
        meta, far_rows, weight, begun
    )
    return out.reshape(levels, beams, width)


def solution(mesh):
    split = Mesh(mesh.devices.reshape(16, 2, 8, 2), ("grp", "pair", "z", "core"))
    req, hist = ("grp", "pair"), ("z", "core")
    in_specs = (
        P(None, req),
        P(req),
        P(),
        P(),
        P(req, hist, None),
        P(req, hist, None),
        P(None, None, hist),
        P(None, None, hist),
        P(None, None, hist),
        P(None, hist),
    )
    return jax.shard_map(shards, mesh=split, in_specs=in_specs, out_specs=P(None, req, hist), check_vma=False)
```

```python
import functools
import math

import jax
import jax.numpy as jnp
from jax import lax
from jax.experimental import pallas as pl
from jax.experimental.pallas import tpu as pltpu
from jax.sharding import Mesh, PartitionSpec as P

KEY_HEADS = 8
HEAD = 128
STAT = 16
CHUNK = HEAD + STAT
DEAD = -1e30
EXP2_SCALE = HEAD ** (-0.5) * math.log2(math.e)
MIB = 1024 * 1024


def one_hot_rows(index_row, count):
    rows = index_row.shape[1]
    tall = jnp.transpose(jnp.broadcast_to(index_row, (128, rows)))
    parts = []
    for start in range(0, count, 128):
        lane = lax.broadcasted_iota(jnp.int32, (rows, 128), 1) + start
        parts.append((tall == lane).astype(jnp.float32).astype(jnp.bfloat16))
    return jnp.concatenate(parts, axis=1)


def look_kernel(codes_hbm, parents_hbm, query_hbm, out_ref, mine_ref, query_ref, sem):
    levels, beams = codes_hbm.shape
    copies = [
        pltpu.make_async_copy(codes_hbm, mine_ref.at[pl.ds(0, levels)], sem.at[0]),
        pltpu.make_async_copy(parents_hbm, mine_ref.at[pl.ds(levels, 1)], sem.at[1]),
        pltpu.make_async_copy(query_hbm, query_ref, sem.at[2]),
    ]
    for copy in copies:
        copy.start()
    copies[0].wait()
    copies[1].wait()
    hots = [one_hot_rows(mine_ref[level : level + 1], query_ref.shape[1]) for level in range(levels)]
    copies[2].wait()
    for level, hot in enumerate(hots):
        found = jnp.dot(hot, query_ref[level], preferred_element_type=jnp.float32).astype(jnp.bfloat16)
        for target in range(out_ref.shape[0]):
            out_ref[target, level * beams : (level + 1) * beams] = found


def generated_kernel(
    meta_ref, mine_ref, other_ref, kv_hbm, embed_hbm, lengths_hbm, holders_hbm, out_ref, residual_ref, live_ref,
    kv_ref, embed_ref, lengths_ref, holders_ref, sem
):
    copies = [
        pltpu.make_async_copy(lengths_hbm, lengths_ref, sem.at[0]),
        pltpu.make_async_copy(holders_hbm, holders_ref, sem.at[1]),
        pltpu.make_async_copy(kv_hbm, kv_ref, sem.at[2]),
        pltpu.make_async_copy(embed_hbm, embed_ref, sem.at[3]),
    ]
    for copy in copies:
        copy.start()
    levels, beams = kv_ref.shape[0], mine_ref.shape[1]
    hots = [
        jnp.concatenate([one_hot_rows(ref[level : level + 1], kv_ref.shape[1]) for ref in (mine_ref, other_ref)])
        for level in range(levels)
    ]
    for copy in copies:
        copy.wait()
    for level, hot in enumerate(hots):
        found = jnp.dot(hot, kv_ref[level], preferred_element_type=jnp.float32).astype(jnp.bfloat16)
        residual_ref[level * beams : (level + 1) * beams] = jnp.dot(
            hot[:beams], embed_ref[level], preferred_element_type=jnp.float32
        )
        for part, x in enumerate((meta_ref[3], 1 - meta_ref[3])):
            place = pl.ds(pl.multiple_of((x * levels + level) * beams, beams), beams)
            out_ref[place] = found[part * beams : (part + 1) * beams]
    request, place, block_slots = meta_ref[0], meta_ref[1], meta_ref[4]
    near, far = jnp.int32(0), jnp.int32(0)
    for block in range(holders_ref.shape[1]):
        holder = holders_ref[request, block]
        near = jnp.where(holder == place, block, near)
        far = jnp.where(holder == jnp.bitwise_xor(place, 1), block, far)
    for at, position in enumerate((near, far)):
        live_ref[at] = jnp.clip(lengths_ref[request] - position * block_slots, 0, block_slots)


def split3(value):
    high = value.astype(jnp.bfloat16).astype(jnp.float32)
    rest = value - high
    middle = rest.astype(jnp.bfloat16).astype(jnp.float32)
    return high, middle, rest - middle


def stat_rows(top, total):
    row = lax.broadcasted_iota(jnp.int32, (STAT, top.shape[1]), 0)
    out = jnp.zeros((STAT, top.shape[1]), jnp.float32)
    for at, piece in enumerate(split3(top) + split3(total)):
        out = jnp.where(row == at, piece, out)
    return out.astype(jnp.bfloat16)


def read_stats(rows):
    wide = rows.astype(jnp.float32)
    return wide[0:1] + wide[1:2] + wide[2:3], wide[3:4] + wide[4:5] + wide[5:6]


def scores_of(keys, rows):
    return lax.dot_general(keys, rows, (((1,), (1,)), ((), ())), preferred_element_type=jnp.float32)


def extended(values):
    return jnp.concatenate([jnp.transpose(values), jnp.ones((STAT, values.shape[0]), jnp.bfloat16)], axis=0)


def regroup_kernel(query_ref, out_ref):
    heads, half = out_ref.shape[0], query_ref.shape[1]
    for head in range(heads):
        for x in range(2):
            for h in range(2):
                rows = slice((2 * x + h) * half, (2 * x + h + 1) * half)
                out_ref[head, rows] = query_ref[x * heads + head, :, h * HEAD : (h + 1) * HEAD]


def write(out_ref, head, sums, total, top):
    width = sums.shape[1] // 2
    for x in range(2):
        lanes = slice(x * width, (x + 1) * width)
        out_ref[x, head, 0:HEAD] = sums[:, lanes].astype(jnp.bfloat16)
        out_ref[x, head, HEAD:CHUNK] = stat_rows(top[:, lanes], total[:, lanes])


def attend_kernel(
    live_ref, query_ref, near_key, near_value, far_key, far_value, out_ref, score_ref, key_ref, value_ref, key_sem, value_sem
):
    heads, slots = key_ref.shape[0], key_ref.shape[1]
    half = query_ref.shape[1] // 4
    block_slots = slots // 2
    near_live, far_live = live_ref[0], live_ref[1]
    live = near_live + far_live

    def copies(head, keys):
        sources, target, sem = ((near_key, far_key), key_ref, key_sem) if keys else ((near_value, far_value), value_ref, value_sem)
        start = head * HEAD
        lanes = pl.ds(start if isinstance(start, int) else pl.multiple_of(start, HEAD), HEAD)
        return [
            pltpu.make_async_copy(
                source.at[:, lanes], target.at[head, pl.ds(block * block_slots, block_slots)], sem.at[block * heads + head]
            )
            for block, source in enumerate(sources)
        ]

    def wait(head, keys):
        for copy in copies(head, keys):
            copy.wait()

    def attend(masked):
        def begin(start, stop):
            for head in range(start, stop):
                for keys in (True, False):
                    for copy in copies(head, keys):
                        copy.start()

        begin(0, 2)

        def score(head, at):
            scores = scores_of(key_ref[head], query_ref[head])
            if masked:
                slot = lax.broadcasted_iota(jnp.int32, (slots, 1), 0)
                allowed = (slot < near_live) | ((slot >= block_slots) & (slot < block_slots + far_live))
                scores = jnp.where(allowed, scores, DEAD)
            score_ref[at] = scores
            return jnp.max(scores, axis=0, keepdims=True)

        def finish(head, at, top):
            weights = jnp.exp2((score_ref[at] - top) * EXP2_SCALE).astype(jnp.bfloat16)
            sums = jnp.dot(extended(value_ref[head]), weights, preferred_element_type=jnp.float32)
            write(out_ref, head, sums[0:HEAD], sums[HEAD : HEAD + 1], top)

        def step(i, top):
            wait(2 * i + 1, True)
            wait(2 * i + 2, True)
            wait(2 * i, False)
            wait(2 * i + 1, False)
            later = score(2 * i + 1, 1)
            finish(2 * i, 0, top)
            top = score(2 * i + 2, 0)
            finish(2 * i + 1, 1, later)
            return top

        wait(0, True)
        top = score(0, 0)
        begin(2, heads)
        top = lax.fori_loop(0, heads // 2 - 1, step, top)
        wait(heads - 1, True)
        wait(heads - 2, False)
        wait(heads - 1, False)
        later = score(heads - 1, 1)
        finish(heads - 2, 0, top)
        finish(heads - 1, 1, later)

    @pl.when(live == slots)
    def _():
        attend(False)

    @pl.when((live > 0) & (live < slots))
    def _():
        attend(True)

    @pl.when(live == 0)
    def _():
        row = lax.broadcasted_iota(jnp.int32, (CHUNK, 2 * half), 0)
        tops = split3(jnp.full((CHUNK, 2 * half), DEAD, jnp.float32))
        dead = jnp.zeros((CHUNK, 2 * half), jnp.float32)
        for at, piece in enumerate(tops):
            dead = jnp.where(row == HEAD + at, piece, dead)
        dead = dead.astype(jnp.bfloat16)
        for x in range(2):
            for head in range(heads):
                out_ref[x, head] = dead


def add_generated_kernel(
    meta_ref, query_ref, kv_ref, far_kv_ref, gen_value_ref, mine_ref, other_ref, before_ref, out_ref, chunk_ref, sem
):
    width = query_ref.shape[1]
    half = width // 4
    head = meta_ref[2]

    @pl.when(head >= 0)
    def _():
        loads = [pltpu.make_async_copy(before_ref.at[x, head], chunk_ref.at[x, 0], sem.at[x]) for x in range(2)]
        stores = [pltpu.make_async_copy(chunk_ref.at[x, 0], out_ref.at[x, head], sem.at[2 + x]) for x in range(2)]
        for copy in loads:
            copy.start()
        values = extended(gen_value_ref[...])
        row = lax.broadcasted_iota(jnp.int32, (2 * half, width), 0)
        lane = lax.broadcasted_iota(jnp.int32, (2 * half, width), 1)
        own = (lane // (2 * half)) * half + lane % half
        beams = mine_ref.shape[1]
        swapped = meta_ref[3] != 0
        mine, other = (ref[mine_ref.shape[0] - 1 :] for ref in (mine_ref, other_ref))
        pieces = []
        for parents in (jnp.where(swapped, other, mine), jnp.where(swapped, mine, other)):
            parents = (parents // beams) * half + parents % beams
            pieces += [jnp.full_like(parents, -1), parents] * 2
        allowed = (row == own) | (row == jnp.concatenate(pieces, axis=1))
        keys = jnp.where(swapped, far_kv_ref[...], kv_ref[...])
        scores = jnp.where(allowed, scores_of(keys, query_ref[head]), DEAD)
        for copy in loads:
            copy.wait()
        before = jnp.concatenate([chunk_ref[x, 0] for x in range(2)], axis=1)
        old_top, old_total = read_stats(before[HEAD:CHUNK])
        top = jnp.maximum(old_top, jnp.max(scores, axis=0, keepdims=True))
        weights = jnp.where(allowed, jnp.exp2((scores - top) * EXP2_SCALE), 0.0)
        high = weights.astype(jnp.bfloat16)
        low = (weights - high.astype(jnp.float32)).astype(jnp.bfloat16)
        added = jnp.dot(values, high, preferred_element_type=jnp.float32)
        added = added + jnp.dot(values, low, preferred_element_type=jnp.float32)
        factor = jnp.exp2((old_top - top) * EXP2_SCALE)
        sums = before[0:HEAD].astype(jnp.float32) * factor + added[0:HEAD]
        write(chunk_ref, 0, sums, old_total * factor + added[HEAD : HEAD + 1], top)
        for copy in stores:
            copy.start()
        for copy in stores:
            copy.wait()


def combine_kernel(parts_ref, out_ref):
    count = parts_ref.shape[0]
    stats = [read_stats(parts_ref[part, HEAD:CHUNK]) for part in range(count)]
    top = functools.reduce(jnp.maximum, [each for each, _ in stats])
    total = jnp.zeros_like(top)
    sums = jnp.zeros((HEAD, parts_ref.shape[2]), jnp.float32)
    for part in range(count):
        factor = jnp.exp2((stats[part][0] - top) * EXP2_SCALE)
        total = total + stats[part][1] * factor
        sums = sums + parts_ref[part, 0:HEAD].astype(jnp.float32) * factor
    tall = jnp.transpose(sums / total)
    rows = out_ref.shape[1]
    found = jnp.concatenate([tall[0:rows], tall[rows : 2 * rows]], axis=1).astype(jnp.bfloat16)
    for target in range(out_ref.shape[0]):
        out_ref[target] = found


def project_kernel(flip, meta_ref, rows_ref, weight_ref, before_ref, out_ref):
    total = before_ref[...]
    parity = jnp.bitwise_xor(jnp.bitwise_and(meta_ref[1], 1), flip)
    for part in range(rows_ref.shape[0]):
        total = total + jnp.dot(rows_ref[part], weight_ref[part, parity], preferred_element_type=jnp.float32)
    out_ref[...] = total.astype(out_ref.dtype)


def call(kernel, out_shape, name, spaces, vmem, out_spaces="v", **rest):
    kinds = {"s": pltpu.SMEM, "v": pltpu.VMEM, "h": pltpu.HBM, "a": pl.ANY}
    specs = lambda letters: [pl.BlockSpec(memory_space=kinds[letter]) for letter in letters]
    return pl.pallas_call(
        kernel,
        out_shape=out_shape,
        in_specs=specs(spaces),
        out_specs=specs(out_spaces) if len(out_spaces) > 1 else specs(out_spaces)[0],
        compiler_params=pltpu.CompilerParams(vmem_limit_bytes=vmem * MIB),
        name=name,
        **rest,
    )


def shards(
    codes, parents, lengths, holders, history_keys, history_values, query_table, kv_table, embed_table, out_weight
):
    beams = parents.shape[0]
    levels, code_count, width = query_table.shape
    half = levels * beams
    rows = 2 * half
    slots = history_keys.shape[1]
    z_count = lax.axis_size("z")
    pair, z, core = lax.axis_index("pair"), lax.axis_index("z"), lax.axis_index("core")
    hist = 2 * z + core
    bf16, f32 = jnp.bfloat16, jnp.float32
    array = jax.ShapeDtypeStruct
    dma = pltpu.SemaphoreType.DMA
    swap = [(0, 1), (1, 0)]

    hbm = lambda x: pltpu.with_memory_space_constraint(x, pltpu.HBM)

    query_rows, mine = call(
        look_kernel,
        (array((2 * z_count, half, width), bf16), array((levels + 1, beams), jnp.int32)),
        "look",
        "hhh",
        4,
        "vv",
        scratch_shapes=[pltpu.VMEM(query_table.shape, bf16), dma((3,))],
    )(hbm(codes), hbm(parents[None]), hbm(query_table))
    queries = lax.all_to_all(query_rows, ("pair", "z"), split_axis=0, concat_axis=0, tiled=True)
    mine, near_keys, near_values = lax.optimization_barrier((mine, history_keys[0], history_values[0]))
    other = lax.ppermute(mine, "pair", swap)
    far_keys = lax.ppermute(near_keys, "core", swap)
    far_values = lax.ppermute(near_values, "core", swap)
    gen_head = jnp.where(z < z_count // 2, 2 * z + jnp.bitwise_xor(core, pair), -1)
    meta = jnp.stack([lax.axis_index("grp"), pair * 2 * z_count + hist, gen_head, pair, jnp.int32(slots)]).astype(jnp.int32)
    kv_rows, residual, live = call(
        generated_kernel,
        (array((rows, HEAD), bf16), array((half, width), f32), array((2,), jnp.int32)),
        "generated",
        "svvhhhh",
        4,
        "vvs",
        scratch_shapes=[
            pltpu.VMEM(kv_table.shape, bf16),
            pltpu.VMEM(embed_table.shape, bf16),
            pltpu.SMEM(lengths.shape, jnp.int32),
            pltpu.SMEM(holders.shape, jnp.int32),
            dma((4,)),
        ],
    )(meta, mine, other, hbm(kv_table), hbm(embed_table), hbm(lengths), hbm(holders))
    at = lambda p, k, c: (p * z_count + k) * 2 + c
    taken = [(p, k, c) for p in range(2) for k in range(z_count // 2) for c in range(2)]
    gen_values = lax.ppermute(
        kv_rows, ("pair", "z", "core"), [(at(p, k + z_count // 2, c ^ p), at(p, k, c)) for p, k, c in taken]
    )
    far_kv = lax.ppermute(kv_rows, ("pair", "z", "core"), [(at(1, k, 1 - c), at(1, k, c)) for p, k, c in taken if p])

    queries, live = lax.optimization_barrier((queries, live))
    queries = call(
        regroup_kernel,
        array((KEY_HEADS, 2 * rows, HEAD), bf16),
        "regroup",
        "v",
        4,
        cost_estimate=pl.CostEstimate(flops=10**12, bytes_accessed=0, transcendentals=0),
    )(queries)
    partial_shape = (2, z_count, CHUNK, 2 * half)
    partials = call(
        attend_kernel,
        array(partial_shape, bf16),
        "attend",
        "svhhaa",
        24,
        scratch_shapes=[
            pltpu.VMEM((2, 2 * slots, 2 * rows), f32),
            pltpu.VMEM((KEY_HEADS, 2 * slots, HEAD), bf16),
            pltpu.VMEM((KEY_HEADS, 2 * slots, HEAD), bf16),
            dma((2 * KEY_HEADS,)),
            dma((2 * KEY_HEADS,)),
        ],
        cost_estimate=pl.CostEstimate(
            flops=4 * 4 * rows * KEY_HEADS * slots * HEAD,
            bytes_accessed=4 * slots * KEY_HEADS * HEAD,
            transcendentals=4 * rows * KEY_HEADS * slots,
        ),
    )(live, queries, hbm(near_keys), hbm(near_values), far_keys, far_values)
    partials = call(
        add_generated_kernel,
        array(partial_shape, bf16),
        "add_generated",
        "svvvvvva",
        4,
        "a",
        input_output_aliases={7: 0},
        scratch_shapes=[pltpu.VMEM((2, 1, CHUNK, 2 * half), bf16), dma((4,))],
    )(meta, queries, kv_rows, far_kv, gen_values, mine, other, partials)

    shape = (2 * z_count, CHUNK, 2 * half)
    parts = lax.all_to_all(partials.reshape(shape), ("pair", "z"), split_axis=0, concat_axis=0, tiled=True)
    attention = call(combine_kernel, array((z_count, half, width), bf16), "combine", "v", 4)(parts)
    near_rows = lax.all_to_all(attention, "z", split_axis=0, concat_axis=0, tiled=True)
    far_rows = lax.ppermute(near_rows, "core", swap)
    weight = out_weight.reshape(z_count, 2, width, width)
    begun = call(functools.partial(project_kernel, 0), array((half, width), f32), "project_near", "svvv", 4)(
        meta, near_rows, weight, residual
    )
    out = call(functools.partial(project_kernel, 1), array((half, width), bf16), "project_far", "svvv", 4)(
        meta, far_rows, weight, begun
    )
    return out.reshape(levels, beams, width)


def solution(mesh):
    split = Mesh(mesh.devices.reshape(16, 2, 8, 2), ("grp", "pair", "z", "core"))
    req, hist = ("grp", "pair"), ("z", "core")
    in_specs = (
        P(None, req),
        P(req),
        P(),
        P(),
        P(req, hist, None),
        P(req, hist, None),
        P(None, None, hist),
        P(None, None, hist),
        P(None, None, hist),
        P(None, hist),
    )
    return jax.shard_map(shards, mesh=split, in_specs=in_specs, out_specs=P(None, req, hist), check_vma=False)
```

```python
import functools
import math

import jax
import jax.numpy as jnp
from jax import lax
from jax.experimental import pallas as pl
from jax.experimental.pallas import tpu as pltpu
from jax.sharding import Mesh, PartitionSpec as P

KEY_HEADS = 8
HEAD = 128
STAT = 16
CHUNK = HEAD + STAT
DEAD = -1e30
EXP2_SCALE = HEAD ** (-0.5) * math.log2(math.e)
MIB = 1024 * 1024


def one_hot_rows(index_row, count):
    rows = index_row.shape[1]
    tall = jnp.transpose(jnp.broadcast_to(index_row, (128, rows)))
    parts = []
    for start in range(0, count, 128):
        lane = lax.broadcasted_iota(jnp.int32, (rows, 128), 1) + start
        parts.append((tall == lane).astype(jnp.float32).astype(jnp.bfloat16))
    return jnp.concatenate(parts, axis=1)


def look_kernel(codes_hbm, parents_hbm, query_hbm, out_ref, mine_ref, query_ref, sem):
    levels, beams = codes_hbm.shape
    copies = [
        pltpu.make_async_copy(codes_hbm, mine_ref.at[pl.ds(0, levels)], sem.at[0]),
        pltpu.make_async_copy(parents_hbm, mine_ref.at[pl.ds(levels, 1)], sem.at[1]),
        pltpu.make_async_copy(query_hbm, query_ref, sem.at[2]),
    ]
    for copy in copies:
        copy.start()
    copies[0].wait()
    copies[1].wait()
    hots = [one_hot_rows(mine_ref[level : level + 1], query_ref.shape[1]) for level in range(levels)]
    copies[2].wait()
    for level, hot in enumerate(hots):
        found = jnp.dot(hot, query_ref[level], preferred_element_type=jnp.float32).astype(jnp.bfloat16)
        for target in range(out_ref.shape[0]):
            out_ref[target, level * beams : (level + 1) * beams] = found


def generated_kernel(
    meta_ref, mine_ref, other_ref, kv_hbm, embed_hbm, lengths_hbm, holders_hbm, out_ref, residual_ref, live_ref,
    kv_ref, embed_ref, lengths_ref, holders_ref, sem
):
    copies = [
        pltpu.make_async_copy(lengths_hbm, lengths_ref, sem.at[0]),
        pltpu.make_async_copy(holders_hbm, holders_ref, sem.at[1]),
        pltpu.make_async_copy(kv_hbm, kv_ref, sem.at[2]),
        pltpu.make_async_copy(embed_hbm, embed_ref, sem.at[3]),
    ]
    for copy in copies:
        copy.start()
    levels, beams = kv_ref.shape[0], mine_ref.shape[1]
    hots = [
        jnp.concatenate([one_hot_rows(ref[level : level + 1], kv_ref.shape[1]) for ref in (mine_ref, other_ref)])
        for level in range(levels)
    ]
    for copy in copies:
        copy.wait()
    for level, hot in enumerate(hots):
        found = jnp.dot(hot, kv_ref[level], preferred_element_type=jnp.float32).astype(jnp.bfloat16)
        residual_ref[level * beams : (level + 1) * beams] = jnp.dot(
            hot[:beams], embed_ref[level], preferred_element_type=jnp.float32
        )
        for part, x in enumerate((meta_ref[3], 1 - meta_ref[3])):
            place = pl.ds(pl.multiple_of((x * levels + level) * beams, beams), beams)
            out_ref[place] = found[part * beams : (part + 1) * beams]
    request, place, block_slots = meta_ref[0], meta_ref[1], meta_ref[4]
    near, far = jnp.int32(0), jnp.int32(0)
    for block in range(holders_ref.shape[1]):
        holder = holders_ref[request, block]
        near = jnp.where(holder == place, block, near)
        far = jnp.where(holder == jnp.bitwise_xor(place, 1), block, far)
    for at, position in enumerate((near, far)):
        live_ref[at] = jnp.clip(lengths_ref[request] - position * block_slots, 0, block_slots)


def split3(value):
    high = value.astype(jnp.bfloat16).astype(jnp.float32)
    rest = value - high
    middle = rest.astype(jnp.bfloat16).astype(jnp.float32)
    return high, middle, rest - middle


def stat_rows(top, total):
    row = lax.broadcasted_iota(jnp.int32, (STAT, top.shape[1]), 0)
    out = jnp.zeros((STAT, top.shape[1]), jnp.float32)
    for at, piece in enumerate(split3(top) + split3(total)):
        out = jnp.where(row == at, piece, out)
    return out.astype(jnp.bfloat16)


def read_stats(rows):
    wide = rows.astype(jnp.float32)
    return wide[0:1] + wide[1:2] + wide[2:3], wide[3:4] + wide[4:5] + wide[5:6]


def scores_of(keys, rows):
    return lax.dot_general(keys, rows, (((1,), (1,)), ((), ())), preferred_element_type=jnp.float32)


def extended(values):
    return jnp.concatenate([jnp.transpose(values), jnp.ones((STAT, values.shape[0]), jnp.bfloat16)], axis=0)


def regroup_kernel(query_ref, out_ref):
    heads, half = out_ref.shape[0], query_ref.shape[1]
    for head in range(heads):
        for x in range(2):
            for h in range(2):
                rows = slice((2 * x + h) * half, (2 * x + h + 1) * half)
                out_ref[head, rows] = query_ref[x * heads + head, :, h * HEAD : (h + 1) * HEAD]


def write(out_ref, head, sums, total, top):
    width = sums.shape[1] // 2
    for x in range(2):
        lanes = slice(x * width, (x + 1) * width)
        out_ref[x, head, 0:HEAD] = sums[:, lanes].astype(jnp.bfloat16)
        out_ref[x, head, HEAD:CHUNK] = stat_rows(top[:, lanes], total[:, lanes])


def attend_kernel(
    live_ref, query_ref, near_key, near_value, far_key, far_value, out_ref, score_ref, key_ref, value_ref, key_sem, value_sem
):
    heads, slots = key_ref.shape[0], key_ref.shape[1]
    half = query_ref.shape[1] // 4
    block_slots = slots // 2
    near_live, far_live = live_ref[0], live_ref[1]
    live = near_live + far_live

    def copies(head, keys):
        sources, target, sem = ((near_key, far_key), key_ref, key_sem) if keys else ((near_value, far_value), value_ref, value_sem)
        lanes = pl.ds(pl.multiple_of(head * HEAD, HEAD), HEAD)
        return [
            pltpu.make_async_copy(
                source.at[:, lanes], target.at[head, pl.ds(block * block_slots, block_slots)], sem.at[block * heads + head]
            )
            for block, source in enumerate(sources)
        ]

    def wait(head, keys):
        for copy in copies(head, keys):
            copy.wait()

    def attend(masked):
        def begin(head, _):
            for keys in (True, False):
                for copy in copies(head, keys):
                    copy.start()
            return 0

        lax.fori_loop(0, heads, begin, 0)

        def score(head, at):
            scores = scores_of(key_ref[head], query_ref[head])
            if masked:
                slot = lax.broadcasted_iota(jnp.int32, (slots, 1), 0)
                allowed = (slot < near_live) | ((slot >= block_slots) & (slot < block_slots + far_live))
                scores = jnp.where(allowed, scores, DEAD)
            score_ref[at] = scores
            return jnp.max(scores, axis=0, keepdims=True)

        def finish(head, at, top):
            weights = jnp.exp2((score_ref[at] - top) * EXP2_SCALE).astype(jnp.bfloat16)
            sums = jnp.dot(extended(value_ref[head]), weights, preferred_element_type=jnp.float32)
            write(out_ref, head, sums[0:HEAD], sums[HEAD : HEAD + 1], top)

        def step(i, top):
            wait(2 * i + 1, True)
            wait(2 * i + 2, True)
            wait(2 * i, False)
            wait(2 * i + 1, False)
            later = score(2 * i + 1, 1)
            finish(2 * i, 0, top)
            top = score(2 * i + 2, 0)
            finish(2 * i + 1, 1, later)
            return top

        wait(0, True)
        top = lax.fori_loop(0, heads // 2 - 1, step, score(0, 0))
        wait(heads - 1, True)
        wait(heads - 2, False)
        wait(heads - 1, False)
        later = score(heads - 1, 1)
        finish(heads - 2, 0, top)
        finish(heads - 1, 1, later)

    @pl.when(live == slots)
    def _():
        attend(False)

    @pl.when((live > 0) & (live < slots))
    def _():
        attend(True)

    @pl.when(live == 0)
    def _():
        row = lax.broadcasted_iota(jnp.int32, (CHUNK, 2 * half), 0)
        tops = split3(jnp.full((CHUNK, 2 * half), DEAD, jnp.float32))
        dead = jnp.zeros((CHUNK, 2 * half), jnp.float32)
        for at, piece in enumerate(tops):
            dead = jnp.where(row == HEAD + at, piece, dead)
        dead = dead.astype(jnp.bfloat16)
        for x in range(2):
            for head in range(heads):
                out_ref[x, head] = dead


def add_generated_kernel(
    meta_ref, query_ref, kv_ref, far_kv_ref, gen_value_ref, mine_ref, other_ref, before_ref, out_ref, own_query_ref, sem
):
    width = query_ref.shape[1]
    half = width // 4
    head = meta_ref[2]

    @pl.when(head >= 0)
    def _():
        copy = pltpu.make_async_copy(query_ref.at[head], own_query_ref, sem.at[0])
        copy.start()
        values = extended(gen_value_ref[...])
        row = lax.broadcasted_iota(jnp.int32, (2 * half, width), 0)
        lane = lax.broadcasted_iota(jnp.int32, (2 * half, width), 1)
        own = (lane // (2 * half)) * half + lane % half
        beams = mine_ref.shape[1]
        swapped = meta_ref[3] != 0
        mine, other = (ref[mine_ref.shape[0] - 1 :] for ref in (mine_ref, other_ref))
        pieces = []
        for parents in (jnp.where(swapped, other, mine), jnp.where(swapped, mine, other)):
            parents = (parents // beams) * half + parents % beams
            pieces += [jnp.full_like(parents, -1), parents] * 2
        allowed = (row == own) | (row == jnp.concatenate(pieces, axis=1))
        keys = jnp.where(swapped, far_kv_ref[...], kv_ref[...])
        copy.wait()
        scores = jnp.where(allowed, scores_of(keys, own_query_ref[...]), DEAD)
        before = jnp.concatenate([before_ref[x, head] for x in range(2)], axis=1)
        old_top, old_total = read_stats(before[HEAD:CHUNK])
        top = jnp.maximum(old_top, jnp.max(scores, axis=0, keepdims=True))
        weights = jnp.where(allowed, jnp.exp2((scores - top) * EXP2_SCALE), 0.0)
        high = weights.astype(jnp.bfloat16)
        low = (weights - high.astype(jnp.float32)).astype(jnp.bfloat16)
        added = jnp.dot(values, high, preferred_element_type=jnp.float32)
        added = added + jnp.dot(values, low, preferred_element_type=jnp.float32)
        factor = jnp.exp2((old_top - top) * EXP2_SCALE)
        sums = before[0:HEAD].astype(jnp.float32) * factor + added[0:HEAD]
        write(out_ref, head, sums, old_total * factor + added[HEAD : HEAD + 1], top)


def combine_kernel(parts_ref, out_ref):
    count = parts_ref.shape[0]
    stats = [read_stats(parts_ref[part, HEAD:CHUNK]) for part in range(count)]
    top = functools.reduce(jnp.maximum, [each for each, _ in stats])
    total = jnp.zeros_like(top)
    sums = jnp.zeros((HEAD, parts_ref.shape[2]), jnp.float32)
    for part in range(count):
        factor = jnp.exp2((stats[part][0] - top) * EXP2_SCALE)
        total = total + stats[part][1] * factor
        sums = sums + parts_ref[part, 0:HEAD].astype(jnp.float32) * factor
    tall = jnp.transpose(sums / total)
    rows = out_ref.shape[1]
    found = jnp.concatenate([tall[0:rows], tall[rows : 2 * rows]], axis=1).astype(jnp.bfloat16)
    for target in range(out_ref.shape[0]):
        out_ref[target] = found


def project_kernel(flip, meta_ref, rows_ref, weight_ref, before_ref, out_ref):
    total = before_ref[...]
    parity = jnp.bitwise_xor(jnp.bitwise_and(meta_ref[1], 1), flip)
    for part in range(rows_ref.shape[0]):
        total = total + jnp.dot(rows_ref[part], weight_ref[part, parity], preferred_element_type=jnp.float32)
    out_ref[...] = total.astype(out_ref.dtype)


def call(kernel, out_shape, name, spaces, vmem, out_spaces="v", **rest):
    kinds = {"s": pltpu.SMEM, "v": pltpu.VMEM, "h": pltpu.HBM, "a": pl.ANY}
    specs = lambda letters: [pl.BlockSpec(memory_space=kinds[letter]) for letter in letters]
    return pl.pallas_call(
        kernel,
        out_shape=out_shape,
        in_specs=specs(spaces),
        out_specs=specs(out_spaces) if len(out_spaces) > 1 else specs(out_spaces)[0],
        compiler_params=pltpu.CompilerParams(vmem_limit_bytes=vmem * MIB),
        name=name,
        **rest,
    )


def shards(
    codes, parents, lengths, holders, history_keys, history_values, query_table, kv_table, embed_table, out_weight
):
    beams = parents.shape[0]
    levels, code_count, width = query_table.shape
    half = levels * beams
    rows = 2 * half
    slots = history_keys.shape[1]
    z_count = lax.axis_size("z")
    pair, z, core = lax.axis_index("pair"), lax.axis_index("z"), lax.axis_index("core")
    hist = 2 * z + core
    bf16, f32 = jnp.bfloat16, jnp.float32
    array = jax.ShapeDtypeStruct
    dma = pltpu.SemaphoreType.DMA
    swap = [(0, 1), (1, 0)]

    hbm = lambda x: pltpu.with_memory_space_constraint(x, pltpu.HBM)

    query_rows, mine = call(
        look_kernel,
        (array((2 * z_count, half, width), bf16), array((levels + 1, beams), jnp.int32)),
        "look",
        "hhh",
        4,
        "vv",
        scratch_shapes=[pltpu.VMEM(query_table.shape, bf16), dma((3,))],
    )(hbm(codes), hbm(parents[None]), hbm(query_table))
    queries = lax.all_to_all(query_rows, ("pair", "z"), split_axis=0, concat_axis=0, tiled=True)
    mine, near_keys, near_values = lax.optimization_barrier((mine, history_keys[0], history_values[0]))
    other = lax.ppermute(mine, "pair", swap)
    far_keys = lax.ppermute(near_keys, "core", swap)
    far_values = lax.ppermute(near_values, "core", swap)
    gen_head = jnp.where(z < z_count // 2, 2 * z + jnp.bitwise_xor(core, pair), -1)
    meta = jnp.stack([lax.axis_index("grp"), pair * 2 * z_count + hist, gen_head, pair, jnp.int32(slots)]).astype(jnp.int32)
    kv_rows, residual, live = call(
        generated_kernel,
        (array((rows, HEAD), bf16), array((half, width), f32), array((2,), jnp.int32)),
        "generated",
        "svvhhhh",
        4,
        "vvs",
        scratch_shapes=[
            pltpu.VMEM(kv_table.shape, bf16),
            pltpu.VMEM(embed_table.shape, bf16),
            pltpu.SMEM(lengths.shape, jnp.int32),
            pltpu.SMEM(holders.shape, jnp.int32),
            dma((4,)),
        ],
    )(meta, mine, other, hbm(kv_table), hbm(embed_table), hbm(lengths), hbm(holders))
    at = lambda p, k, c: (p * z_count + k) * 2 + c
    taken = [(p, k, c) for p in range(2) for k in range(z_count // 2) for c in range(2)]
    gen_values = lax.ppermute(
        kv_rows, ("pair", "z", "core"), [(at(p, k + z_count // 2, c ^ p), at(p, k, c)) for p, k, c in taken]
    )
    far_kv = lax.ppermute(kv_rows, ("pair", "z", "core"), [(at(1, k, 1 - c), at(1, k, c)) for p, k, c in taken if p])

    queries, live = lax.optimization_barrier((queries, live))
    queries = call(
        regroup_kernel,
        array((KEY_HEADS, 2 * rows, HEAD), bf16),
        "regroup",
        "v",
        4,
        cost_estimate=pl.CostEstimate(flops=10**12, bytes_accessed=0, transcendentals=0),
    )(queries)
    partial_shape = (2, z_count, CHUNK, 2 * half)
    partials = call(
        attend_kernel,
        array(partial_shape, bf16),
        "attend",
        "svhhaa",
        24,
        scratch_shapes=[
            pltpu.VMEM((2, 2 * slots, 2 * rows), f32),
            pltpu.VMEM((KEY_HEADS, 2 * slots, HEAD), bf16),
            pltpu.VMEM((KEY_HEADS, 2 * slots, HEAD), bf16),
            dma((2 * KEY_HEADS,)),
            dma((2 * KEY_HEADS,)),
        ],
        cost_estimate=pl.CostEstimate(
            flops=4 * 4 * rows * KEY_HEADS * slots * HEAD,
            bytes_accessed=4 * slots * KEY_HEADS * HEAD,
            transcendentals=4 * rows * KEY_HEADS * slots,
        ),
    )(live, queries, hbm(near_keys), hbm(near_values), far_keys, far_values)
    partials = call(
        add_generated_kernel,
        array(partial_shape, bf16),
        "add_generated",
        "savvvvvv",
        4,
        input_output_aliases={7: 0},
        scratch_shapes=[pltpu.VMEM((2 * rows, HEAD), bf16), dma((1,))],
    )(meta, queries, kv_rows, far_kv, gen_values, mine, other, partials)

    shape = (2 * z_count, CHUNK, 2 * half)
    parts = lax.all_to_all(partials.reshape(shape), ("pair", "z"), split_axis=0, concat_axis=0, tiled=True)
    attention = call(combine_kernel, array((z_count, half, width), bf16), "combine", "v", 4)(parts)
    near_rows = lax.all_to_all(attention, "z", split_axis=0, concat_axis=0, tiled=True)
    far_rows = lax.ppermute(near_rows, "core", swap)
    weight = out_weight.reshape(z_count, 2, width, width)
    begun = call(functools.partial(project_kernel, 0), array((half, width), f32), "project_near", "svvv", 4)(
        meta, near_rows, weight, residual
    )
    out = call(functools.partial(project_kernel, 1), array((half, width), bf16), "project_far", "svvv", 4)(
        meta, far_rows, weight, begun
    )
    return out.reshape(levels, beams, width)


def solution(mesh):
    split = Mesh(mesh.devices.reshape(16, 2, 8, 2), ("grp", "pair", "z", "core"))
    req, hist = ("grp", "pair"), ("z", "core")
    in_specs = (
        P(None, req),
        P(req),
        P(),
        P(),
        P(req, hist, None),
        P(req, hist, None),
        P(None, None, hist),
        P(None, None, hist),
        P(None, None, hist),
        P(None, hist),
    )
    return jax.shard_map(shards, mesh=split, in_specs=in_specs, out_specs=P(None, req, hist), check_vma=False)
```
